32 devices in a mesh: leaf: 4 (over z), ctx: 8 (over y, x, core).
Axes of the slice: x: 2, y: 2, z: 4, core: 2. Of those that a mesh axis runs over, the one named last changes fastest.
Arguments:
- queries: bfloat16 [4096, 8192], P(('leaf', 'ctx')), may hold values from -38 to 38, as said below
- seg_keys: bfloat16 [4096, 1024], P(('leaf', 'ctx')), may hold values from -6 to 6
- seg_values: bfloat16 [4096, 1024], P(('leaf', 'ctx')), may hold values from -6 to 6
- root_keys: bfloat16 [1024, 1024], P('ctx'), may hold values from -6 to 6, as said below
- root_values: bfloat16 [1024, 1024], P('ctx'), may hold values from -6 to 6
- expansion: int32 [2, 4], replicated, may hold values from 0 to 3, as said below
- root_offsets: int32 [4], replicated, may hold values from 256 to 1024
Outputs:
- attended: bfloat16 [4096, 8192], P(('leaf', 'ctx'))
The draws below stay inside these ranges and needn't reach their ends.
Inputs may be any that keep to these rules, and one draw needn't show every extreme that they name: queries of order one, with some rows much larger. `root_keys`: keys of order one. `expansion`: group 4 - 1 is the root: it has depth 0 and is its own parent; every other group's parent has depth one less than its own.
All inputs are finite; a program needn't handle non-finite values.
Results may differ from the reference program's by a relative error of at most 0.0065.
Values may be sent and summed in bfloat16 or wider, within the bound.
No kernel may reach another device: no remote copies, remote signals or barrier semaphores. Data moves between devices by JAX's collectives and lax.ppermute only.
A program may use at most 128 MiB of HBM per device.

```python
import math
import jax
import jax.numpy as jnp
from jax import lax

HQ = 64
KVH = 8
HD = 128
GROUPS = 4
SEG = 1024
L_ROOT = 1024


def root_table(key):
    table_key = jax.random.fold_in(key, 101)
    key_table = jnp.clip(jax.random.normal(table_key, (L_ROOT, KVH * HD), jnp.float32), -6.0, 6.0)
    return key_table


def draw_root_keys(key, part):
    return root_table(key).astype(jnp.bfloat16)


def draw_queries(key, part):
    query_key = jax.random.fold_in(key, 202)
    total_rows = GROUPS * SEG
    drawn = jnp.clip(jax.random.normal(query_key, (total_rows, HQ * HD), jnp.float32), -6.0, 6.0)
    return drawn.astype(jnp.bfloat16)


def draw_expansion(key, part):
    key_order = jax.random.fold_in(key, 303)
    key_picks = jax.random.fold_in(key, 304)
    later_order = jax.random.permutation(key_order, GROUPS - 1).astype(jnp.int32)
    visit_order = jnp.concatenate([jnp.full((1,), GROUPS - 1, jnp.int32), later_order]).astype(jnp.int32)
    raw_picks = jax.random.randint(key_picks, (GROUPS,), 0, 1 << 20).astype(jnp.int32)
    parents = jnp.zeros((GROUPS,), jnp.int32).at[visit_order[0]].set(visit_order[0])
    depths = jnp.zeros((GROUPS,), jnp.int32)
    for position in range(1, GROUPS):
        parent_id = visit_order[raw_picks[position] % position]
        parents = parents.at[visit_order[position]].set(parent_id)
        depths = depths.at[visit_order[position]].set(depths[parent_id] + 1)
    return jnp.stack([parents, depths]).astype(jnp.int32)


def with_ends(values, stream_key, least, high):
    longest = values.shape.index(max(values.shape))
    spots = []
    for shift in (0, 1):
        where = [jax.random.randint(jax.random.fold_in(stream_key, axis), (), 0, length) for axis, length in enumerate(values.shape)]
        where[longest] = (where[longest] + shift) % values.shape[longest]
        spots.append(tuple(where))
    return values.at[spots[0]].set(least).at[spots[1]].set(high)


def steps_of(rng, extent, shards, low, high):
    gain, own = 1.0, jax.random.fold_in(rng, 6)
    for dim, parts in shards:
        steps = jnp.exp(jax.random.uniform(jax.random.fold_in(own, dim), (parts,), jnp.float32, low / len(shards), high / len(shards)))
        gain = gain * jnp.repeat(steps, extent[dim] // parts).reshape([-1 if axis == dim else 1 for axis in range(len(extent))])
    return gain


def centred(own_key, shape, deviation, reach, pieces=(), held_as=jnp.bfloat16):
    loudness = steps_of(own_key, shape, pieces, -0.22, 0.18) if pieces else 1.0
    array = jax.random.normal(own_key, shape, jnp.float32) * deviation * loudness
    return jnp.minimum(jnp.maximum(array, -reach), reach).astype(held_as)


def setup_inputs(seed: int = 0) -> dict:
    seeds = jax.random.split(jax.random.key(seed), 8)
    return {
        "queries": draw_queries(jax.random.fold_in(seeds[7], 71), 0),
        "seg_keys": centred(seeds[1], (GROUPS * SEG, KVH * HD), 1.0, 6.0, ((0, 32),)),
        "seg_values": centred(seeds[2], (GROUPS * SEG, KVH * HD), 1.0, 6.0, ((0, 32),)),
        "root_keys": draw_root_keys(jax.random.fold_in(seeds[7], 71), 0),
        "root_values": centred(seeds[4], (L_ROOT, KVH * HD), 1.0, 6.0, ((0, 8),)),
        "expansion": draw_expansion(jax.random.fold_in(seeds[7], 71), 0),
        "root_offsets": with_ends(jax.random.randint(seeds[6], (GROUPS,), L_ROOT // 4, L_ROOT + 1), jax.random.fold_in(seeds[6], 1), L_ROOT // 4, L_ROOT).astype(jnp.int32),
    }


def reference(queries, seg_keys, seg_values, root_keys, root_values, expansion, root_offsets):
    group_width = HQ // KVH
    score_scale = 1.0 / math.sqrt(HD)
    query_pos = jnp.arange(SEG, dtype=jnp.int32)
    key_index = jnp.arange(L_ROOT + 2 * SEG, dtype=jnp.int32)
    in_root = key_index < L_ROOT
    in_parent = (key_index >= L_ROOT) & (key_index < L_ROOT + SEG)
    own_pos = key_index - L_ROOT - SEG

    def one_pair(pair_index):
        group_idx = (pair_index // KVH).astype(jnp.int32)
        head_index = (pair_index % KVH).astype(jnp.int32)
        parent = expansion[0, group_idx].astype(jnp.int32)
        tree_depth = expansion[1, group_idx]
        visible = root_offsets[group_idx]
        head_query = lax.dynamic_slice(queries, (group_idx * SEG, head_index * group_width * HD), (SEG, group_width * HD)).reshape(SEG, group_width, HD)
        zero_row = jnp.zeros((), jnp.int32)
        all_keys = jnp.concatenate([lax.dynamic_slice(root_keys, (zero_row, head_index * HD), (L_ROOT, HD)), lax.dynamic_slice(seg_keys, (parent * SEG, head_index * HD), (SEG, HD)), lax.dynamic_slice(seg_keys, (group_idx * SEG, head_index * HD), (SEG, HD))], axis=0)
        all_values = jnp.concatenate([lax.dynamic_slice(root_values, (zero_row, head_index * HD), (L_ROOT, HD)), lax.dynamic_slice(seg_values, (parent * SEG, head_index * HD), (SEG, HD)), lax.dynamic_slice(seg_values, (group_idx * SEG, head_index * HD), (SEG, HD))], axis=0)
        scores = jnp.einsum('qgd,kd->gqk', head_query.astype(jnp.float32), all_keys.astype(jnp.float32)) * score_scale
        allowed = (in_root & (key_index < visible))[None, :] | (in_parent & (tree_depth > 0))[None, :] | (own_pos >= 0)[None, :] & (own_pos[None, :] <= query_pos[:, None])
        masked = jnp.where(allowed[None], scores, -jnp.inf)
        row_max = lax.optimization_barrier(jnp.max(masked, axis=-1, keepdims=True))
        weights = jnp.where(allowed[None], jnp.exp(masked - row_max), 0.0)
        row_total = lax.optimization_barrier(jnp.sum(weights, axis=-1))
        rounded = lax.optimization_barrier(weights.astype(jnp.bfloat16))
        blended = jnp.einsum('gqk,kd->gqd', rounded.astype(jnp.float32), all_values.astype(jnp.float32))
        return blended / row_total[..., None]
    stacked = lax.map(one_pair, jnp.arange(GROUPS * KVH, dtype=jnp.int32))
    stacked = stacked.reshape(GROUPS, KVH, group_width, SEG, HD).transpose(0, 3, 1, 2, 4).reshape(GROUPS * SEG, HQ * HD)
    return stacked.astype(jnp.bfloat16)
```

```python
import functools
import math

import jax
import jax.numpy as jnp
from jax import lax
from jax.experimental import pallas as pl
from jax.experimental.pallas import tpu as pltpu
from jax.sharding import PartitionSpec as P

HQ = 64
KVH = 8
HD = 128
GW = HQ // KVH
HALF_KV = KVH // 2
NEG = -1e30
Q_SCALE = math.log2(math.e) / math.sqrt(HD)
ROW_BLOCK = 512


def attend_kernel(ny, rows, groups, first, last, *refs):
    refs = list(refs)
    exp_ref, off_ref, q0_ref, q1_ref = refs[:4]
    refs = refs[4:]
    key_refs, value_refs = [], []
    for parts in groups:
        key_refs.append([refs.pop(0) for _ in parts])
        value_refs.append([refs.pop(0) for _ in parts])
    if not first:
        acc_in, ml_in = refs.pop(0), refs.pop(0)
    if last:
        outs = [refs.pop(0), refs.pop(0)]
    else:
        acc_out, ml_out = refs.pop(0), refs.pop(0)
    qs, accs, ms = refs
    stacked = GW * rows

    group = lax.axis_index("leaf")
    spot = lax.axis_index("ctx")
    core, chip = lax.rem(spot, 2), spot // 2
    chip_x, chip_y = lax.rem(chip, 2), chip // 2
    visible = off_ref[group]
    depth = exp_ref[1, group]

    def block_start(dx, dy, flip):
        x = lax.rem(chip_x + dx, 2)
        y = lax.rem(chip_y - dy + ny, ny)
        k = lax.rem(core + flip, 2)
        return ((y * 2 + x) * 2 + k) * rows

    for s, q_ref in enumerate((q0_ref, q1_ref)):
        for g in range(GW):
            q = q_ref[:, g * HD : (g + 1) * HD].astype(jnp.float32) * Q_SCALE
            high = q.astype(jnp.bfloat16)
            low = (q - high.astype(jnp.float32)).astype(jnp.bfloat16)
            qs[s, g * rows : (g + 1) * rows, :HD] = high
            qs[s, g * rows : (g + 1) * rows, HD:] = low
    if first:
        accs[...] = jnp.zeros_like(accs)
        ms[...] = jnp.full_like(ms, NEG)
    else:
        for s in range(2):
            accs[s, :, :HD] = acc_in[0, s]
            ml = ml_in[0, s]
            accs[s, :, HD:] = jnp.broadcast_to(ml[:, HD - 1 :], ml.shape)
            ms[s] = jnp.broadcast_to(ml[:, :1], ml.shape)

    for parts, k_refs, v_refs in zip(groups, key_refs, value_refs):
        blocks = [block for part in parts for block in part]
        width = len(blocks) * rows
        for s in range(2):
            first_row = block_start(0, 0, s)
            limits = []
            full, some = jnp.bool_(True), jnp.bool_(False)
            for kind, dx, dy, flip in blocks:
                if kind == "root":
                    limit = visible - block_start(dx, dy, flip)
                    some_here = limit > 0
                elif kind == "own":
                    limit = first_row - block_start(dx, dy, flip) + 1
                    some_here = limit + rows - 1 > 0
                else:
                    limit = jnp.where(depth > 0, rows, 0)
                    some_here = limit > 0
                limits.append(limit)
                full = full & (limit >= rows)
                some = some | some_here

            def step(masked):
                keys = jnp.concatenate([ref[...] for ref in k_refs], axis=0)
                keys = jnp.concatenate([keys, keys], axis=1)
                values = jnp.concatenate([ref[...] for ref in v_refs], axis=0)
                values = jnp.concatenate([values, jnp.ones_like(values)], axis=1)
                for base in range(0, stacked, ROW_BLOCK):
                    size = min(ROW_BLOCK, stacked)
                    here = slice(base, base + size)
                    scores = lax.dot_general(
                        qs[s, here, :], keys, (((1,), (1,)), ((), ())), preferred_element_type=jnp.float32
                    )
                    if masked:
                        column = lax.broadcasted_iota(jnp.int32, (rows, rows), 1)
                        line = lax.broadcasted_iota(jnp.int32, (rows, rows), 0)
                        allowed = []
                        for (kind, *_), limit in zip(blocks, limits):
                            ahead = column - line if kind == "own" else column
                            allowed.append(jnp.where(ahead < limit, 0.0, NEG))
                        bias = jnp.concatenate(allowed, axis=1)
                        scores = scores + jnp.concatenate([bias] * (size // rows), axis=0)
                    old = ms[s, here, :]
                    new = jnp.maximum(old, jnp.max(scores, axis=1, keepdims=True))
                    weights = jnp.exp2(scores - jnp.concatenate([new] * (width // HD), axis=1))
                    update = jnp.dot(weights.astype(jnp.bfloat16), values, preferred_element_type=jnp.float32)
                    shrink = jnp.exp2(old - new)
                    accs[s, here, :] = accs[s, here, :] * jnp.concatenate([shrink, shrink], axis=1) + update
                    ms[s, here, :] = new

            @pl.when(full)
            def _():
                step(False)

            @pl.when(jnp.logical_not(full) & some)
            def _():
                step(True)

    for s in range(2):
        if last:
            done = (accs[s, :, :HD] / accs[s, :, HD:]).astype(jnp.bfloat16)
            for g in range(GW):
                outs[s][:, g * HD : (g + 1) * HD] = done[g * rows : (g + 1) * rows]
        else:
            acc_out[0, s] = accs[s, :, :HD]
            lane = lax.broadcasted_iota(jnp.int32, (stacked, HD), 1)
            ml_out[0, s] = jnp.where(lane < HD // 2, ms[s], accs[s, :, HD:])


def attend(ny, q_pair, tables, groups, state, last):
    rows = q_pair[0].shape[0]
    stacked = GW * rows
    first = state is None
    smem = pl.BlockSpec(memory_space=pltpu.SMEM)
    q_spec = pl.BlockSpec((rows, GW * HD), lambda h: (0, h))
    state_spec = pl.BlockSpec((1, 2, stacked, HD), lambda h: (h, 0, 0, 0))
    operands = [*tables, *q_pair]
    specs = [smem, smem, q_spec, q_spec]
    total = 0
    for parts in groups:
        for shift in (0, HALF_KV):
            for array, _ in parts:
                operands.append(array)
                specs.append(pl.BlockSpec((array.shape[0], HD), functools.partial(lambda s, h: (0, s + h), shift)))
        total += sum(array.shape[0] for array, _ in parts)
    if not first:
        operands += list(state)
        specs += [state_spec, state_spec]
    if last:
        out_shape = [jax.ShapeDtypeStruct((rows, HALF_KV * GW * HD), jnp.bfloat16)] * 2
        out_specs = [q_spec, q_spec]
    else:
        out_shape = [jax.ShapeDtypeStruct((HALF_KV, 2, stacked, HD), jnp.float32)] * 2
        out_specs = [state_spec, state_spec]
    scores = HALF_KV * 2 * stacked * total
    return pl.pallas_call(
        functools.partial(
            attend_kernel, ny, rows, tuple(tuple(b for _, b in parts) for parts in groups), first, last
        ),
        grid=(HALF_KV,),
        in_specs=specs,
        out_specs=out_specs,
        out_shape=out_shape,
        scratch_shapes=[
            pltpu.VMEM((2, stacked, 2 * HD), jnp.bfloat16),
            pltpu.VMEM((2, stacked, 2 * HD), jnp.float32),
            pltpu.VMEM((2, stacked, HD), jnp.float32),
        ],
        compiler_params=pltpu.CompilerParams(vmem_limit_bytes=48 * 2**20),
        cost_estimate=pl.CostEstimate(flops=8 * scores * HD, bytes_accessed=20 * 2**20, transcendentals=scores),
    )(*operands)


def on_device(queries, seg_keys, seg_values, root_keys, root_values, expansion, root_offsets):
    leaves, spots = lax.axis_size("leaf"), lax.axis_size("ctx")
    ny = spots // 4
    rows = queries.shape[0]
    group = lax.axis_index("leaf")
    core = lax.rem(lax.axis_index("ctx"), 2)

    def halves(array):
        half = array.shape[1] // 2
        return (
            lax.dynamic_slice_in_dim(array, core * half, half, 1),
            lax.dynamic_slice_in_dim(array, (1 - core) * half, half, 1),
        )

    def index(x, y, k):
        return ((y % ny) * 2 + x % 2) * 2 + k % 2

    places = [(x, y, k) for y in range(ny) for x in range(2) for k in range(2)]

    def to_core(array):
        return lax.ppermute(array, "ctx", [(index(x, y, k), index(x, y, k + 1)) for x, y, k in places])

    def to_x(array):
        return lax.ppermute(array, "ctx", [(index(x, y, k), index(x + 1, y, k)) for x, y, k in places])

    def to_y(array, step):
        return lax.ppermute(array, "ctx", [(index(x, y, k), index(x, y + step, k)) for x, y, k in places])

    def packed(keys, values):
        (key_mine, key_other), (value_mine, value_other) = halves(keys), halves(values)
        return jnp.concatenate([key_mine, value_mine], axis=1), jnp.concatenate([key_other, value_other], axis=1)

    own_mine, own_other = packed(seg_keys, seg_values)
    root_mine, root_other = packed(root_keys, root_values)
    got = to_core(jnp.concatenate([own_other, root_other], axis=0))
    q_mine, q_other = halves(queries)
    q_pair = (q_mine, to_core(q_other))
    tables = (expansion, root_offsets)
    local = jnp.concatenate([own_mine, root_mine, got], axis=0)
    segment = jnp.concatenate([own_mine, got[:rows]], axis=0)

    def blocks(dx, dy, flips=(0, 1), kinds=("own", "root")):
        return tuple((kind, dx, dy, flip) for flip in flips for kind in kinds)

    parent = expansion[0, group]
    parent_rows = segment
    up, down = segment, segment
    for step in range(1, leaves):
        down = lax.ppermute(down, "leaf", [(i, i - 1) for i in range(1, leaves - step + 1)])
        parent_rows = jnp.where(parent == group + step, down, parent_rows)
        if step < leaves - 1:
            up = lax.ppermute(up, "leaf", [(i, i + 1) for i in range(step - 1, leaves - 2)])
            parent_rows = jnp.where(parent == group - step, up, parent_rows)

    state = attend(ny, q_pair, tables, [[(local, blocks(0, 0))]], None, False)
    from_x = to_x(local)
    from_y = [to_y(local, step) for step in range(1, ny)]
    near = [[(from_x, blocks(1, 0))]] + [[(a, blocks(0, i + 1))] for i, a in enumerate(from_y)]
    state = attend(ny, q_pair, tables, near, state, False)
    far = []
    for step in range(1, ny):
        top = to_y(from_x[: 2 * rows], step)
        low = to_x(from_y[step - 1][2 * rows :])
        far.append([(top, blocks(1, step, (0,))), (low, blocks(1, step, (1,)))])
    kin = (("kin", 0, 0, 0),)
    far.append([(parent_rows, kin * 2)])
    state = attend(ny, q_pair, tables, far, state, False)
    kin_x = to_x(parent_rows)
    kin_y = [to_y(parent_rows, step) for step in range(1, ny)]
    groups = [[(kin_x, kin * 2), (kin_y[0], kin * 2)]] + [[(a, kin * 2)] for a in kin_y[1:]]
    for step in range(1, ny):
        top = to_y(kin_x[:rows], step)
        low = to_x(kin_y[step - 1][rows:])
        groups.append([(top, kin), (low, kin)])
    out_mine, out_other = attend(ny, q_pair, tables, groups, state, True)
    out_got = to_core(out_other)
    return jnp.where(
        core == 0,
        jnp.concatenate([out_mine, out_got], axis=1),
        jnp.concatenate([out_got, out_mine], axis=1),
    )


def solution(mesh):
    return jax.shard_map(
        on_device,
        mesh=mesh,
        in_specs=(
            P(("leaf", "ctx"), None),
            P(("leaf", "ctx"), None),
            P(("leaf", "ctx"), None),
            P("ctx", None),
            P("ctx", None),
            P(),
            P(),
        ),
        out_specs=P(("leaf", "ctx"), None),
        check_vma=False,
    )
```

```python
import functools
import math

import jax
import jax.numpy as jnp
from jax import lax
from jax.experimental import pallas as pl
from jax.experimental.pallas import tpu as pltpu
from jax.sharding import PartitionSpec as P

HQ = 64
KVH = 8
HD = 128
GW = HQ // KVH
HALF_KV = KVH // 2
NEG = -1e30
Q_SCALE = math.log2(math.e) / math.sqrt(HD)
ROW_BLOCK = 256


def attend_kernel(ny, rows, arrays, groups, first, last, *refs):
    refs = list(refs)
    take = lambda count: [refs.pop(0) for _ in range(count)]
    exp_ref, off_ref = take(2)
    q_refs = take(2 if first else 1)
    key_refs = take(arrays)
    value_refs = take(arrays)
    if not first:
        acc_in, ml_in = take(2)
    if first:
        (q_out,) = take(1)
        qs = q_out
    else:
        qs = q_refs[0]
    if last:
        outs = take(2)
    else:
        acc_out, ml_out = take(2)
    accs, ms = refs
    stacked = GW * rows

    group = lax.axis_index("leaf")
    spot = lax.axis_index("ctx")
    core, chip = lax.rem(spot, 2), spot // 2
    chip_x, chip_y = lax.rem(chip, 2), chip // 2
    visible = off_ref[group]
    depth = exp_ref[1, group]

    def block_start(dx, dy, flip):
        x = lax.rem(chip_x + dx, 2)
        y = lax.rem(chip_y - dy + ny, ny)
        k = lax.rem(core + flip, 2)
        return ((y * 2 + x) * 2 + k) * rows

    if first:
        for s, q_ref in enumerate(q_refs):
            for g in range(GW):
                q = q_ref[:, g * HD : (g + 1) * HD].astype(jnp.float32) * Q_SCALE
                high = q.astype(jnp.bfloat16)
                low = (q - high.astype(jnp.float32)).astype(jnp.bfloat16)
                q_out[0, s, g * rows : (g + 1) * rows, :HD] = high
                q_out[0, s, g * rows : (g + 1) * rows, HD:] = low
    else:
        for s in range(2):
            accs[s, :, :HD] = acc_in[0, s]
            ml = ml_in[0, s]
            accs[s, :, HD:] = jnp.broadcast_to(ml[:, HD - 1 :], ml.shape)
            ms[s] = jnp.broadcast_to(ml[:, :1], ml.shape)

    def step(members, limits, masked, fresh):
        width = len(members) * rows
        cut = lambda refs: [refs[a][b * rows : (b + 1) * rows, :] for a, b, _ in members]
        keys = jnp.concatenate(cut(key_refs), axis=0)
        keys = jnp.concatenate([keys, keys], axis=1)
        values = jnp.concatenate(cut(value_refs), axis=0)
        values = jnp.concatenate([values, jnp.ones_like(values)], axis=1)
        size = min(ROW_BLOCK, stacked)
        todo = [(s, slice(base, base + size)) for s in range(2) for base in range(0, stacked, size)]

        def score(s, here):
            return lax.dot_general(
                qs[0, s, here, :], keys, (((1,), (1,)), ((), ())), preferred_element_type=jnp.float32
            )

        def bias_of(s):
            column = lax.broadcasted_iota(jnp.int32, (rows, rows), 1)
            line = lax.broadcasted_iota(jnp.int32, (rows, rows), 0)
            allowed = []
            for (_, _, block), limit in zip(members, limits[s]):
                ahead = column - line if block[0] == "own" else column
                allowed.append(jnp.where(ahead < limit, 0.0, NEG))
            return jnp.concatenate(allowed, axis=1)

        following = score(*todo[0])
        for at, (s, here) in enumerate(todo):
            scores = following
            if at + 1 < len(todo):
                following = score(*todo[at + 1])
            if masked:
                bias = bias_of(s)
                scores = scores + jnp.concatenate([bias] * (size // rows), axis=0)
            new = jnp.max(scores, axis=1, keepdims=True)
            if fresh:
                new = jnp.broadcast_to(new, (size, HD))
            else:
                old = ms[s, here, :]
                new = jnp.maximum(old, new)
            weights = jnp.exp2(scores - jnp.concatenate([new] * (width // HD), axis=1))
            update = jnp.dot(weights.astype(jnp.bfloat16), values, preferred_element_type=jnp.float32)
            if fresh:
                accs[s, here, :] = update
            else:
                shrink = jnp.exp2(old - new)
                accs[s, here, :] = accs[s, here, :] * jnp.concatenate([shrink, shrink], axis=1) + update
            ms[s, here, :] = new

    for number, members in enumerate(groups):
        limits = []
        full, some = jnp.bool_(True), jnp.bool_(False)
        for s in range(2):
            first_row = block_start(0, 0, s)
            limits.append([])
            for _, _, (kind, dx, dy, flip) in members:
                if kind == "root":
                    limit = visible - block_start(dx, dy, flip)
                    some_here = limit > 0
                elif kind == "own":
                    limit = first_row - block_start(dx, dy, flip) + 1
                    some_here = limit + rows - 1 > 0
                else:
                    limit = jnp.where(depth > 0, rows, 0)
                    some_here = limit > 0
                limits[s].append(limit)
                full = full & (limit >= rows)
                some = some | some_here
        kinds = {block[0] for _, _, block in members}
        if first and number == 0:
            step(members, limits, True, True)
            continue
        pl.when(full)(functools.partial(step, members, limits, False, False))
        if kinds != {"kin"}:
            pl.when(jnp.logical_not(full) & some)(functools.partial(step, members, limits, True, False))

    for s in range(2):
        if last:
            done = (accs[s, :, :HD] / accs[s, :, HD:]).astype(jnp.bfloat16)
            for g in range(GW):
                outs[s][:, g * HD : (g + 1) * HD] = done[g * rows : (g + 1) * rows]
        else:
            acc_out[0, s] = accs[s, :, :HD]
            lane = lax.broadcasted_iota(jnp.int32, (stacked, HD), 1)
            ml_out[0, s] = jnp.where(lane < HD // 2, ms[s], accs[s, :, HD:])


def attend(ny, rows, tables, queries, arrays, groups, state, last):
    stacked = GW * rows
    first = state is None
    smem = pl.BlockSpec(memory_space=pltpu.SMEM)
    row_spec = pl.BlockSpec((rows, GW * HD), lambda h: (0, h))
    q_spec = pl.BlockSpec((1, 2, stacked, 2 * HD), lambda h: (h, 0, 0, 0))
    state_spec = pl.BlockSpec((1, 2, stacked, HD), lambda h: (h, 0, 0, 0))
    operands = [*tables, *queries]
    specs = [smem, smem] + ([row_spec, row_spec] if first else [q_spec])
    for shift in (0, HALF_KV):
        for array in arrays:
            operands.append(array)
            specs.append(pl.BlockSpec((array.shape[0], HD), functools.partial(lambda s, h: (0, s + h), shift)))
    out_shape, out_specs = [], []
    if first:
        out_shape.append(jax.ShapeDtypeStruct((HALF_KV, 2, stacked, 2 * HD), jnp.bfloat16))
        out_specs.append(q_spec)
    else:
        operands += list(state)
        specs += [state_spec, state_spec]
    if last:
        out_shape += [jax.ShapeDtypeStruct((rows, HALF_KV * GW * HD), jnp.bfloat16)] * 2
        out_specs += [row_spec, row_spec]
    else:
        out_shape += [jax.ShapeDtypeStruct((HALF_KV, 2, stacked, HD), jnp.float32)] * 2
        out_specs += [state_spec, state_spec]
    scores = HALF_KV * 2 * stacked * rows * sum(len(members) for members in groups)
    return pl.pallas_call(
        functools.partial(attend_kernel, ny, rows, len(arrays), groups, first, last),
        grid=(HALF_KV,),
        in_specs=specs,
        out_specs=out_specs,
        out_shape=out_shape,
        scratch_shapes=[
            pltpu.VMEM((2, stacked, 2 * HD), jnp.float32),
            pltpu.VMEM((2, stacked, HD), jnp.float32),
        ],
        compiler_params=pltpu.CompilerParams(vmem_limit_bytes=40 * 2**20),
        cost_estimate=pl.CostEstimate(flops=8 * scores * HD, bytes_accessed=20 * 2**20, transcendentals=scores),
    )(*operands)


def on_device(queries, seg_keys, seg_values, root_keys, root_values, expansion, root_offsets):
    leaves, spots = lax.axis_size("leaf"), lax.axis_size("ctx")
    ny = spots // 4
    rows = queries.shape[0]
    group = lax.axis_index("leaf")
    core = lax.rem(lax.axis_index("ctx"), 2)

    def halves(array):
        half = array.shape[1] // 2
        return (
            lax.dynamic_slice_in_dim(array, core * half, half, 1),
            lax.dynamic_slice_in_dim(array, (1 - core) * half, half, 1),
        )

    def index(x, y, k):
        return ((y % ny) * 2 + x % 2) * 2 + k % 2

    places = [(x, y, k) for y in range(ny) for x in range(2) for k in range(2)]

    def to_core(array):
        return lax.ppermute(array, "ctx", [(index(x, y, k), index(x, y, k + 1)) for x, y, k in places])

    def to_x(array):
        return lax.ppermute(array, "ctx", [(index(x, y, k), index(x + 1, y, k)) for x, y, k in places])

    def to_y(array, step):
        return lax.ppermute(array, "ctx", [(index(x, y, k), index(x, y + step, k)) for x, y, k in places])

    def packed(keys, values):
        (key_mine, key_other), (value_mine, value_other) = halves(keys), halves(values)
        return jnp.concatenate([key_mine, value_mine], axis=1), jnp.concatenate([key_other, value_other], axis=1)

    own_mine, own_other = packed(seg_keys, seg_values)
    root_mine, root_other = packed(root_keys, root_values)
    got = to_core(jnp.concatenate([own_other, root_other], axis=0))
    q_mine, q_other = halves(queries)
    q_pair = (q_mine, to_core(q_other))
    tables = (expansion, root_offsets)
    local = jnp.concatenate([own_mine, root_mine, got], axis=0)
    segment = jnp.concatenate([own_mine, got[:rows]], axis=0)

    kinds = ("own", "root")

    def members(array, dx, dy, flips=(0, 1), wanted=kinds):
        return tuple(
            (array, f * 2 + kinds.index(kind), (kind, dx, dy, flip))
            for f, flip in enumerate(flips)
            for kind in wanted
        )

    def kin(*counts):
        return tuple((array, b, ("kin", 0, 0, 0)) for array, count in counts for b in range(count))

    run = functools.partial(attend, ny, rows, tables)
    steps = range(1, ny)

    parent = expansion[0, group]
    choices = []

    def hop(step, down, up):
        down = lax.ppermute(down, "leaf", [(i, i - 1) for i in range(1, leaves - step + 1)])
        choices.append((group + step, down))
        if step < leaves - 1:
            up = lax.ppermute(up, "leaf", [(i, i + 1) for i in range(step - 1, leaves - 2)])
            choices.append((group - step, up))
        return down, up

    down, up = hop(1, segment, segment)
    from_x = to_x(local)
    from_y = [to_y(local, step) for step in steps]
    q_ready, *state = run(q_pair, [local], (members(0, 0, 0),), None, False)
    if leaves > 2:
        down, up, state = lax.optimization_barrier((down, up, state))
        down, up = hop(2, down, up)

    tops = [to_y(from_x[: 2 * rows], step) for step in steps]
    lows = [to_x(array[2 * rows :]) for array in from_y]
    near = [members(0, 1, 0, wanted=(kind,)) + members(1, 0, 1, wanted=(kind,)) for kind in kinds]
    near += [members(step, 0, step) for step in steps if step > 1]
    state = run([q_ready], [from_x, *from_y], tuple(near), state, False)
    for step in range(3, leaves):
        down, up, state = lax.optimization_barrier((down, up, state))
        down, up = hop(step, down, up)
    far, arrays = [], []
    for step, top, low in zip(steps, tops, lows):
        far.append(
            members(len(arrays), 1, step, (0,)) + members(len(arrays) + 1, 1, step, (1,))
        )
        arrays += [top, low]
    state = run([q_ready], arrays, tuple(far), state, False)

    owners, helds = zip(*choices)
    helds, state = lax.optimization_barrier((helds, state))
    parent_rows = segment
    for owner, held in zip(owners, helds):
        parent_rows = jnp.where(parent == owner, held, parent_rows)
    kin_x = to_x(parent_rows)
    kin_y = [to_y(parent_rows, step) for step in steps]
    tops = [to_y(kin_x[:rows], step) for step in steps]
    lows = [to_x(array[rows:]) for array in kin_y]
    arrays = [parent_rows, kin_x, *kin_y, *tops, *lows]
    last_groups = [kin((0, 2), (1, 2), (2, 2), (1 + ny, 1), (2 * ny, 1))]
    for step in steps:
        if step > 1:
            last_groups.append(kin((1 + step, 2), (ny + step, 1), (2 * ny - 1 + step, 1)))
    out_mine, out_other = run([q_ready], arrays, tuple(last_groups), state, True)
    out_got = to_core(out_other)
    return jnp.where(
        core == 0,
        jnp.concatenate([out_mine, out_got], axis=1),
        jnp.concatenate([out_got, out_mine], axis=1),
    )


def solution(mesh):
    return jax.shard_map(
        on_device,
        mesh=mesh,
        in_specs=(
            P(("leaf", "ctx"), None),
            P(("leaf", "ctx"), None),
            P(("leaf", "ctx"), None),
            P("ctx", None),
            P("ctx", None),
            P(),
            P(),
        ),
        out_specs=P(("leaf", "ctx"), None),
        check_vma=False,
    )
```

```python
import functools
import math

import jax
import jax.numpy as jnp
from jax import lax
from jax.experimental import pallas as pl
from jax.experimental.pallas import tpu as pltpu
from jax.sharding import PartitionSpec as P

HQ = 64
KVH = 8
HD = 128
GW = HQ // KVH
HALF_KV = KVH // 2
NEG = -1e30
Q_SCALE = math.log2(math.e) / math.sqrt(HD)
ROW_BLOCK = 256


def attend_kernel(ny, rows, arrays, groups, first, last, *refs):
    refs = list(refs)
    take = lambda count: [refs.pop(0) for _ in range(count)]
    exp_ref, off_ref = take(2)
    raw = take(2) if first else None
    key_refs = take(arrays)
    value_refs = take(arrays)
    head = pl.program_id(0)
    if not first:
        take(4)
    if last:
        outs = take(2)
    else:
        take(1)[0][...] = jnp.zeros((8, HD), jnp.float32)
    qs, accs, ms = take(3)
    stacked = GW * rows

    group = lax.axis_index("leaf")
    spot = lax.axis_index("ctx")
    core, chip = lax.rem(spot, 2), spot // 2
    chip_x, chip_y = lax.rem(chip, 2), chip // 2
    visible = off_ref[group]
    depth = exp_ref[1, group]

    def block_start(dx, dy, flip):
        x = lax.rem(chip_x + dx, 2)
        y = lax.rem(chip_y - dy + ny, ny)
        k = lax.rem(core + flip, 2)
        return ((y * 2 + x) * 2 + k) * rows

    if first:
        for s, q_ref in enumerate(raw):
            for g in range(GW):
                q = q_ref[:, g * HD : (g + 1) * HD].astype(jnp.float32) * Q_SCALE
                high = q.astype(jnp.bfloat16)
                low = (q - high.astype(jnp.float32)).astype(jnp.bfloat16)
                qs[head, s, g * rows : (g + 1) * rows, :HD] = high
                qs[head, s, g * rows : (g + 1) * rows, HD:] = low

    def step(members, limits, masked, fresh):
        width = len(members) * rows
        cut = lambda refs: [refs[a][b * rows : (b + 1) * rows, :] for a, b, _ in members]
        keys = jnp.concatenate(cut(key_refs), axis=0)
        keys = jnp.concatenate([keys, keys], axis=1)
        values = jnp.concatenate(cut(value_refs), axis=0)
        values = jnp.concatenate([values, jnp.ones_like(values)], axis=1)
        size = min(ROW_BLOCK, stacked)
        todo = [(s, slice(base, base + size)) for s in range(2) for base in range(0, stacked, size)]

        def score(s, here):
            return lax.dot_general(
                qs[head, s, here, :], keys, (((1,), (1,)), ((), ())), preferred_element_type=jnp.float32
            )

        def bias_of(s):
            column = lax.broadcasted_iota(jnp.int32, (rows, rows), 1)
            line = lax.broadcasted_iota(jnp.int32, (rows, rows), 0)
            allowed = []
            for (_, _, block), limit in zip(members, limits[s]):
                ahead = column - line if block[0] == "own" else column
                allowed.append(jnp.where(ahead < limit, 0.0, NEG))
            return jnp.concatenate(allowed, axis=1)

        following = score(*todo[0])
        for at, (s, here) in enumerate(todo):
            scores = following
            if at + 1 < len(todo):
                following = score(*todo[at + 1])
            if masked:
                bias = bias_of(s)
                scores = scores + jnp.concatenate([bias] * (size // rows), axis=0)
            new = jnp.max(scores, axis=1, keepdims=True)
            if fresh:
                new = jnp.broadcast_to(new, (size, HD))
            else:
                old = ms[head, s, here, :]
                new = jnp.maximum(old, new)
            weights = jnp.exp2(scores - jnp.concatenate([new] * (width // HD), axis=1))
            update = jnp.dot(weights.astype(jnp.bfloat16), values, preferred_element_type=jnp.float32)
            if fresh:
                accs[head, s, here, :] = update
            else:
                shrink = jnp.exp2(old - new)
                accs[head, s, here, :] = accs[head, s, here, :] * jnp.concatenate([shrink, shrink], axis=1) + update
            ms[head, s, here, :] = new

    for number, members in enumerate(groups):
        limits = []
        full, some = jnp.bool_(True), jnp.bool_(False)
        for s in range(2):
            first_row = block_start(0, 0, s)
            limits.append([])
            for _, _, (kind, dx, dy, flip) in members:
                if kind == "root":
                    limit = visible - block_start(dx, dy, flip)
                    some_here = limit > 0
                elif kind == "own":
                    limit = first_row - block_start(dx, dy, flip) + 1
                    some_here = limit + rows - 1 > 0
                else:
                    limit = jnp.where(depth > 0, rows, 0)
                    some_here = limit > 0
                limits[s].append(limit)
                full = full & (limit >= rows)
                some = some | some_here
        kinds = {block[0] for _, _, block in members}
        if first and number == 0:
            step(members, limits, True, True)
            continue
        pl.when(full)(functools.partial(step, members, limits, False, False))
        if kinds != {"kin"}:
            pl.when(jnp.logical_not(full) & some)(functools.partial(step, members, limits, True, False))

    if last:
        for s in range(2):
            for g in range(GW):
                here = slice(g * rows, (g + 1) * rows)
                done = accs[head, s, here, :HD] / accs[head, s, here, HD:]
                outs[s][:, g * HD : (g + 1) * HD] = done.astype(jnp.bfloat16)


def attend(ny, rows, tables, arrays, groups, queries, state, last):
    stacked = GW * rows
    first = state is None
    smem = pl.BlockSpec(memory_space=pltpu.SMEM)
    held = pl.BlockSpec(memory_space=pltpu.VMEM)
    row_spec = pl.BlockSpec((rows, GW * HD), lambda h: (0, h))
    kept = [
        ((HALF_KV, 2, stacked, 2 * HD), jnp.bfloat16),
        ((HALF_KV, 2, stacked, 2 * HD), jnp.float32),
        ((HALF_KV, 2, stacked, HD), jnp.float32),
    ]
    operands = [*tables]
    specs = [smem, smem]
    if first:
        operands += queries
        specs += [row_spec, row_spec]
    for shift in (0, HALF_KV):
        for array in arrays:
            operands.append(array)
            specs.append(pl.BlockSpec((array.shape[0], HD), functools.partial(lambda s, h: (0, s + h), shift)))
    aliases = {}
    if last:
        out_shape = [jax.ShapeDtypeStruct((rows, HALF_KV * GW * HD), jnp.bfloat16)] * 2
        out_specs = [row_spec, row_spec]
    else:
        out_shape = [jax.ShapeDtypeStruct((8, HD), jnp.float32)]
        out_specs = [pl.BlockSpec((8, HD), lambda h: (0, 0))]
    if not first:
        mark, *state = state
        operands.append(mark)
        specs.append(pl.BlockSpec(memory_space=pl.ANY))
        for i, array in enumerate(state):
            aliases[len(operands)] = len(out_shape) + i
            operands.append(pltpu.with_memory_space_constraint(array, pltpu.VMEM))
            specs.append(held)
    out_shape += [pltpu.VMEM(shape, dtype) for shape, dtype in kept]
    out_specs += [held] * 3
    scores = HALF_KV * 2 * stacked * rows * sum(len(members) for members in groups)
    out = pl.pallas_call(
        functools.partial(attend_kernel, ny, rows, len(arrays), groups, first, last),
        grid=(HALF_KV,),
        in_specs=specs,
        out_specs=out_specs,
        out_shape=out_shape,
        input_output_aliases=aliases,
        compiler_params=pltpu.CompilerParams(vmem_limit_bytes=24 * 2**20),
        cost_estimate=pl.CostEstimate(flops=8 * scores * HD, bytes_accessed=4 * 2**20, transcendentals=scores),
    )(*operands)
    return out[:2] if last else list(out)


def on_device(queries, seg_keys, seg_values, root_keys, root_values, expansion, root_offsets):
    leaves, spots = lax.axis_size("leaf"), lax.axis_size("ctx")
    ny = spots // 4
    rows = queries.shape[0]
    group = lax.axis_index("leaf")
    core = lax.rem(lax.axis_index("ctx"), 2)

    def halves(array):
        half = array.shape[1] // 2
        return (
            lax.dynamic_slice_in_dim(array, core * half, half, 1),
            lax.dynamic_slice_in_dim(array, (1 - core) * half, half, 1),
        )

    def index(x, y, k):
        return ((y % ny) * 2 + x % 2) * 2 + k % 2

    places = [(x, y, k) for y in range(ny) for x in range(2) for k in range(2)]

    def to_core(array):
        return lax.ppermute(array, "ctx", [(index(x, y, k), index(x, y, k + 1)) for x, y, k in places])

    def to_x(array):
        return lax.ppermute(array, "ctx", [(index(x, y, k), index(x + 1, y, k)) for x, y, k in places])

    def to_y(array, step):
        return lax.ppermute(array, "ctx", [(index(x, y, k), index(x, y + step, k)) for x, y, k in places])

    def packed(keys, values):
        (key_mine, key_other), (value_mine, value_other) = halves(keys), halves(values)
        return jnp.concatenate([key_mine, value_mine], axis=1), jnp.concatenate([key_other, value_other], axis=1)

    own_mine, own_other = packed(seg_keys, seg_values)
    root_mine, root_other = packed(root_keys, root_values)
    got = to_core(jnp.concatenate([own_other, root_other], axis=0))
    q_mine, q_other = halves(queries)
    q_pair = (q_mine, to_core(q_other))
    tables = (expansion, root_offsets)
    local = jnp.concatenate([own_mine, root_mine, got], axis=0)
    segment = jnp.concatenate([own_mine, got[:rows]], axis=0)

    kinds = ("own", "root")

    def members(array, dx, dy, flips=(0, 1), wanted=kinds):
        return tuple(
            (array, f * 2 + kinds.index(kind), (kind, dx, dy, flip))
            for f, flip in enumerate(flips)
            for kind in wanted
        )

    def kin(*counts):
        return tuple((array, b, ("kin", 0, 0, 0)) for array, count in counts for b in range(count))

    run = functools.partial(attend, ny, rows, tables)
    steps = range(1, ny)

    every = lax.all_gather(segment, "leaf", axis=0, tiled=True)
    from_x = to_x(local)
    from_y = [to_y(local, step) for step in steps]
    state = run([local], (members(0, 0, 0),), q_pair, None, False)
    from_x, from_y, state[0] = lax.optimization_barrier((from_x, from_y, state[0]))
    tops = [to_y(from_x[: 2 * rows], step) for step in steps]
    lows = [to_x(array[2 * rows :]) for array in from_y]
    near = [members(0, 1, 0, wanted=(kind,)) + members(1, 0, 1, wanted=(kind,)) for kind in kinds]
    near += [members(step, 0, step) for step in steps if step > 1]
    state = run([from_x, *from_y], tuple(near), None, state, False)

    every, state[0] = lax.optimization_barrier((every, state[0]))
    parent_rows = lax.dynamic_slice_in_dim(every, expansion[0, group] * 2 * rows, 2 * rows, 0)
    parent_rows, state[0] = lax.optimization_barrier((parent_rows, state[0]))
    kin_x = to_x(parent_rows)
    kin_y = [to_y(parent_rows, step) for step in steps]
    far, arrays = [], []
    for step, top, low in zip(steps, tops, lows):
        far.append(members(len(arrays), 1, step, (0,)) + members(len(arrays) + 1, 1, step, (1,)))
        arrays += [top, low]
    state = run(arrays, tuple(far), None, state, False)
    tops = [to_y(kin_x[:rows], step) for step in steps]
    lows = [to_x(array[rows:]) for array in kin_y]
    groups = [kin((0, 2), (1, 2), (2, 2))] + [kin((1 + step, 2)) for step in steps if step > 1]
    state = run([parent_rows, kin_x, *kin_y], tuple(groups), None, state, False)
    groups = tuple(kin((step - 1, 1), (ny + step - 2, 1)) for step in steps)
    out_mine, out_other = run([*tops, *lows], groups, None, state, True)
    out_got = to_core(out_other)
    return jnp.where(
        core == 0,
        jnp.concatenate([out_mine, out_got], axis=1),
        jnp.concatenate([out_got, out_mine], axis=1),
    )


def solution(mesh):
    return jax.shard_map(
        on_device,
        mesh=mesh,
        in_specs=(
            P(("leaf", "ctx"), None),
            P(("leaf", "ctx"), None),
            P(("leaf", "ctx"), None),
            P("ctx", None),
            P("ctx", None),
            P(),
            P(),
        ),
        out_specs=P(("leaf", "ctx"), None),
        check_vma=False,
    )
```

```python
import functools
import math

import jax
import jax.numpy as jnp
from jax import lax
from jax.experimental import pallas as pl
from jax.experimental.pallas import tpu as pltpu
from jax.sharding import PartitionSpec as P

HQ = 64
KVH = 8
HD = 128
GW = HQ // KVH
HALF_KV = KVH // 2
NEG = -1e30
Q_SCALE = math.log2(math.e) / math.sqrt(HD)
ROW_BLOCK = 512


def attend_kernel(ny, rows, arrays, groups, first, last, *refs):
    refs = list(refs)
    take = lambda count: [refs.pop(0) for _ in range(count)]
    exp_ref, off_ref = take(2)
    raw = take(2) if first else None
    key_refs = take(arrays)
    value_refs = take(arrays)
    head = pl.program_id(0)
    if not first:
        take(4)
    if last:
        outs = take(2)
    else:
        take(1)[0][...] = jnp.zeros((8, HD), jnp.float32)
    qs, accs, ms = take(3)
    stacked = GW * rows

    group = lax.axis_index("leaf")
    spot = lax.axis_index("ctx")
    core, chip = lax.rem(spot, 2), spot // 2
    chip_x, chip_y = lax.rem(chip, 2), chip // 2
    visible = off_ref[group]
    depth = exp_ref[1, group]

    def block_start(dx, dy, flip):
        x = lax.rem(chip_x + dx, 2)
        y = lax.rem(chip_y - dy + ny, ny)
        k = lax.rem(core + flip, 2)
        return ((y * 2 + x) * 2 + k) * rows

    if first:
        for s, q_ref in enumerate(raw):
            for g in range(GW):
                q = q_ref[:, g * HD : (g + 1) * HD].astype(jnp.float32) * Q_SCALE
                high = q.astype(jnp.bfloat16)
                low = (q - high.astype(jnp.float32)).astype(jnp.bfloat16)
                qs[head, s, g * rows : (g + 1) * rows, :HD] = high
                qs[head, s, g * rows : (g + 1) * rows, HD:] = low

    def step(members, limits, masked, fresh):
        width = len(members) * rows
        cut = lambda refs: [refs[a][b * rows : (b + 1) * rows, :] for a, b, _ in members]
        keys = jnp.concatenate(cut(key_refs), axis=0)
        keys = jnp.concatenate([keys, keys], axis=1)
        values = jnp.concatenate(cut(value_refs), axis=0)
        values = jnp.concatenate([values, jnp.ones_like(values)], axis=1)
        size = min(ROW_BLOCK, stacked)
        todo = [(s, slice(base, base + size)) for s in range(2) for base in range(0, stacked, size)]

        def score(s, here):
            return lax.dot_general(
                qs[head, s, here, :], keys, (((1,), (1,)), ((), ())), preferred_element_type=jnp.float32
            )

        def bias_of(s):
            column = lax.broadcasted_iota(jnp.int32, (rows, rows), 1)
            line = lax.broadcasted_iota(jnp.int32, (rows, rows), 0)
            allowed = []
            for (_, _, block), limit in zip(members, limits[s]):
                ahead = column - line if block[0] == "own" else column
                allowed.append(jnp.where(ahead < limit, 0.0, NEG))
            return jnp.concatenate(allowed, axis=1)

        following = score(*todo[0])
        for at, (s, here) in enumerate(todo):
            scores = following
            if at + 1 < len(todo):
                following = score(*todo[at + 1])
            if masked:
                bias = bias_of(s)
                scores = scores + jnp.concatenate([bias] * (size // rows), axis=0)
            new = jnp.max(scores, axis=1, keepdims=True)
            if fresh:
                new = jnp.broadcast_to(new, (size, HD))
            else:
                old = ms[head, s, here, :]
                new = jnp.maximum(old, new)
            weights = jnp.exp2(scores - jnp.concatenate([new] * (width // HD), axis=1))
            update = jnp.dot(weights.astype(jnp.bfloat16), values, preferred_element_type=jnp.float32)
            if fresh:
                accs[head, s, here, :] = update
            else:
                shrink = jnp.exp2(old - new)
                accs[head, s, here, :] = accs[head, s, here, :] * jnp.concatenate([shrink, shrink], axis=1) + update
            ms[head, s, here, :] = new

    for number, members in enumerate(groups):
        limits = []
        full, some = jnp.bool_(True), jnp.bool_(False)
        for s in range(2):
            first_row = block_start(0, 0, s)
            limits.append([])
            for _, _, (kind, dx, dy, flip) in members:
                if kind == "root":
                    limit = visible - block_start(dx, dy, flip)
                    some_here = limit > 0
                elif kind == "own":
                    limit = first_row - block_start(dx, dy, flip) + 1
                    some_here = limit + rows - 1 > 0
                else:
                    limit = jnp.where(depth > 0, rows, 0)
                    some_here = limit > 0
                limits[s].append(limit)
                full = full & (limit >= rows)
                some = some | some_here
        kinds = {block[0] for _, _, block in members}
        if first and number == 0:
            step(members, limits, True, True)
            continue
        pl.when(full)(functools.partial(step, members, limits, False, False))
        if kinds != {"kin"}:
            pl.when(jnp.logical_not(full) & some)(functools.partial(step, members, limits, True, False))

    if last:
        for s in range(2):
            for g in range(GW):
                here = slice(g * rows, (g + 1) * rows)
                done = accs[head, s, here, :HD] / accs[head, s, here, HD:]
                outs[s][:, g * HD : (g + 1) * HD] = done.astype(jnp.bfloat16)


def attend(ny, rows, tables, arrays, groups, queries, state, last):
    stacked = GW * rows
    first = state is None
    smem = pl.BlockSpec(memory_space=pltpu.SMEM)
    held = pl.BlockSpec(memory_space=pltpu.VMEM)
    row_spec = pl.BlockSpec((rows, GW * HD), lambda h: (0, h))
    kept = [
        ((HALF_KV, 2, stacked, 2 * HD), jnp.bfloat16),
        ((HALF_KV, 2, stacked, 2 * HD), jnp.float32),
        ((HALF_KV, 2, stacked, HD), jnp.float32),
    ]
    operands = [*tables]
    specs = [smem, smem]
    if first:
        operands += queries
        specs += [row_spec, row_spec]
    for shift in (0, HALF_KV):
        for array in arrays:
            operands.append(array)
            specs.append(pl.BlockSpec((array.shape[0], HD), functools.partial(lambda s, h: (0, s + h), shift)))
    aliases = {}
    if last:
        out_shape = [jax.ShapeDtypeStruct((rows, HALF_KV * GW * HD), jnp.bfloat16)] * 2
        out_specs = [row_spec, row_spec]
    else:
        out_shape = [jax.ShapeDtypeStruct((8, HD), jnp.float32)]
        out_specs = [pl.BlockSpec((8, HD), lambda h: (0, 0))]
    if not first:
        mark, *state = state
        operands.append(mark)
        specs.append(pl.BlockSpec(memory_space=pl.ANY))
        for i, array in enumerate(state):
            aliases[len(operands)] = len(out_shape) + i
            operands.append(pltpu.with_memory_space_constraint(array, pltpu.VMEM))
            specs.append(held)
    out_shape += [pltpu.VMEM(shape, dtype) for shape, dtype in kept]
    out_specs += [held] * 3
    scores = HALF_KV * 2 * stacked * rows * sum(len(members) for members in groups)
    out = pl.pallas_call(
        functools.partial(attend_kernel, ny, rows, len(arrays), groups, first, last),
        grid=(HALF_KV,),
        in_specs=specs,
        out_specs=out_specs,
        out_shape=out_shape,
        input_output_aliases=aliases,
        compiler_params=pltpu.CompilerParams(vmem_limit_bytes=24 * 2**20),
        cost_estimate=pl.CostEstimate(flops=8 * scores * HD, bytes_accessed=4 * 2**20, transcendentals=scores),
    )(*operands)
    return out[:2] if last else list(out)


def on_device(queries, seg_keys, seg_values, root_keys, root_values, expansion, root_offsets):
    leaves, spots = lax.axis_size("leaf"), lax.axis_size("ctx")
    ny = spots // 4
    rows = queries.shape[0]
    group = lax.axis_index("leaf")
    core = lax.rem(lax.axis_index("ctx"), 2)

    def halves(array):
        half = array.shape[1] // 2
        return (
            lax.dynamic_slice_in_dim(array, core * half, half, 1),
            lax.dynamic_slice_in_dim(array, (1 - core) * half, half, 1),
        )

    def index(x, y, k):
        return ((y % ny) * 2 + x % 2) * 2 + k % 2

    places = [(x, y, k) for y in range(ny) for x in range(2) for k in range(2)]

    def to_core(array):
        return lax.ppermute(array, "ctx", [(index(x, y, k), index(x, y, k + 1)) for x, y, k in places])

    def to_x(array):
        return lax.ppermute(array, "ctx", [(index(x, y, k), index(x + 1, y, k)) for x, y, k in places])

    def to_y(array, step):
        return lax.ppermute(array, "ctx", [(index(x, y, k), index(x, y + step, k)) for x, y, k in places])

    def packed(keys, values):
        (key_mine, key_other), (value_mine, value_other) = halves(keys), halves(values)
        return jnp.concatenate([key_mine, value_mine], axis=1), jnp.concatenate([key_other, value_other], axis=1)

    own_mine, own_other = packed(seg_keys, seg_values)
    root_mine, root_other = packed(root_keys, root_values)
    got = to_core(jnp.concatenate([own_other, root_other], axis=0))
    q_mine, q_other = halves(queries)
    q_pair = (q_mine, to_core(q_other))
    own = jnp.concatenate([own_mine, got[:rows]], axis=0)
    root = jnp.concatenate([root_mine, got[rows:]], axis=0)
    run = functools.partial(attend, ny, rows, (expansion, root_offsets))
    steps = range(1, ny)

    def members(array, kind, dx=0, dy=0, flips=(0, 1), first=0):
        return tuple((array, first + i, (kind, dx, dy, flip)) for i, flip in enumerate(flips))

    def after(state, *values):
        *values, state[0] = lax.optimization_barrier((*values, state[0]))
        return values

    choices = []

    def hop(step, down, up):
        down = lax.ppermute(down, "leaf", [(i, i - 1) for i in range(1, leaves - step + 1)])
        choices.append((group + step, down))
        if step < leaves - 1:
            up = lax.ppermute(up, "leaf", [(i, i + 1) for i in range(step - 1, leaves - 2)])
            choices.append((group - step, up))
        return down, up

    down, up = hop(1, own, own)
    own_x, own_y = to_x(own), [to_y(own, step) for step in steps]
    root_x, root_y = to_x(root), [to_y(root, step) for step in steps]
    state = run([own, root], (members(0, "own") + members(1, "root"),), q_pair, None, False)

    if leaves > 2:
        down, up = hop(2, *after(state, down, up))

    def near(kind, arrays):
        groups = [members(0, kind, 1) + members(1, kind, 0, 1)]
        groups += [members(step, kind, 0, step) for step in steps if step > 1]
        return run(arrays, tuple(groups), None, state, False)

    state = near("own", [own_x, *own_y])
    for step in range(3, leaves):
        down, up = hop(step, *after(state, down, up))
    own_x, root_x, *pairs = after(state, own_x, root_x, *own_y, *root_y)
    own_y, root_y = pairs[: ny - 1], pairs[ny - 1 :]
    tops = [to_y(jnp.concatenate([own_x[:rows], root_x[:rows]], axis=0), step) for step in steps]
    lows = [to_x(jnp.concatenate([a[rows:], b[rows:]], axis=0)) for a, b in zip(own_y, root_y)]
    state = near("root", [root_x, *root_y])

    parent = expansion[0, group]
    owners, helds = zip(*choices)
    helds = after(state, *helds)
    parent_rows = own
    for owner, held in zip(owners, helds):
        parent_rows = jnp.where(parent == owner, held, parent_rows)
    (parent_rows,) = after(state, parent_rows)
    kin_x, kin_y = to_x(parent_rows), [to_y(parent_rows, step) for step in steps]
    groups, arrays = [], []
    for step, top, low in zip(steps, tops, lows):
        at = len(arrays)
        groups.append(
            members(at, "own", 1, step, (0,))
            + members(at, "root", 1, step, (0,), 1)
            + members(at + 1, "own", 1, step, (1,))
            + members(at + 1, "root", 1, step, (1,), 1)
        )
        arrays += [top, low]
    state = run([*arrays, parent_rows], (*groups, members(len(arrays), "kin")), None, state, False)

    (kin_x,) = after(state, kin_x)
    tops = [to_y(kin_x[:rows], step) for step in steps]
    lows = [to_x(array[rows:]) for array in kin_y]
    groups = [members(0, "kin") + members(1, "kin")] + [members(step, "kin") for step in steps if step > 1]
    state = run([kin_x, *kin_y], tuple(groups), None, state, False)
    groups = [members(i, "kin", flips=(0,)) + members(len(tops) + i, "kin", flips=(1,)) for i in range(len(tops))]
    out_mine, out_other = run([*tops, *lows], tuple(groups), None, state, True)
    out_got = to_core(out_other)
    return jnp.where(
        core == 0,
        jnp.concatenate([out_mine, out_got], axis=1),
        jnp.concatenate([out_got, out_mine], axis=1),
    )


def solution(mesh):
    return jax.shard_map(
        on_device,
        mesh=mesh,
        in_specs=(
            P(("leaf", "ctx"), None),
            P(("leaf", "ctx"), None),
            P(("leaf", "ctx"), None),
            P("ctx", None),
            P("ctx", None),
            P(),
            P(),
        ),
        out_specs=P(("leaf", "ctx"), None),
        check_vma=False,
    )
```

```python
import functools
import math

import jax
import jax.numpy as jnp
from jax import lax
from jax.experimental import pallas as pl
from jax.experimental.pallas import tpu as pltpu
from jax.sharding import PartitionSpec as P

HQ = 64
KVH = 8
HD = 128
GW = HQ // KVH
HALF_KV = KVH // 2
NEG = -1e30
Q_SCALE = math.log2(math.e) / math.sqrt(HD)
ROW_BLOCK = 256


def attend_kernel(ny, rows, arrays, groups, first, last, *refs):
    refs = list(refs)
    take = lambda count: [refs.pop(0) for _ in range(count)]
    exp_ref, off_ref = take(2)
    raw = take(2) if first else take(1)
    key_refs = take(arrays)
    value_refs = take(arrays)
    if not first:
        take(1)
        acc_in, stat_in = take(2)
    if last:
        outs = take(2)
        acc_out, stat_out = take(2)
    else:
        take(1)[0][...] = jnp.zeros((8, HD), jnp.float32)
        acc_out, stat_out = take(2)
    qs = take(1)[0] if first else raw[0]
    stacked = GW * rows
    lane = lax.broadcasted_iota(jnp.int32, (min(ROW_BLOCK, stacked), HD), 1)

    group = lax.axis_index("leaf")
    spot = lax.axis_index("ctx")
    core, chip = lax.rem(spot, 2), spot // 2
    chip_x, chip_y = lax.rem(chip, 2), chip // 2
    visible = off_ref[group]
    depth = exp_ref[1, group]

    def block_start(dx, dy, flip):
        x = lax.rem(chip_x + dx, 2)
        y = lax.rem(chip_y - dy + ny, ny)
        k = lax.rem(core + flip, 2)
        return ((y * 2 + x) * 2 + k) * rows

    if first:
        for s, q_ref in enumerate(raw):
            for g in range(GW):
                q = q_ref[:, g * HD : (g + 1) * HD].astype(jnp.float32) * Q_SCALE
                high = q.astype(jnp.bfloat16)
                low = (q - high.astype(jnp.float32)).astype(jnp.bfloat16)
                qs[0, s, g * rows : (g + 1) * rows, :HD] = high
                qs[0, s, g * rows : (g + 1) * rows, HD:] = low

    def step(members, limits, masked, start):
        width = len(members) * rows
        cut = lambda refs: [refs[a][b * rows : (b + 1) * rows, :] for a, b, _ in members]
        keys = jnp.concatenate(cut(key_refs), axis=0)
        keys = jnp.concatenate([keys, keys], axis=1)
        values = jnp.concatenate(cut(value_refs), axis=0)
        values = jnp.concatenate([values, jnp.ones_like(values)], axis=1)
        size = min(ROW_BLOCK, stacked)
        todo = [(s, slice(base, base + size)) for s in range(2) for base in range(0, stacked, size)]

        def score(s, here):
            return lax.dot_general(
                qs[0, s, here, :], keys, (((1,), (1,)), ((), ())), preferred_element_type=jnp.float32
            )

        def bias_of(s):
            column = lax.broadcasted_iota(jnp.int32, (rows, rows), 1)
            line = lax.broadcasted_iota(jnp.int32, (rows, rows), 0)
            allowed = []
            for (_, _, block), limit in zip(members, limits[s]):
                ahead = column - line if block[0] == "own" else column
                allowed.append(jnp.where(ahead < limit, 0.0, NEG))
            return jnp.concatenate(allowed, axis=1)

        following = score(*todo[0])
        for at, (s, here) in enumerate(todo):
            scores = following
            if at + 1 < len(todo):
                following = score(*todo[at + 1])
            if masked:
                bias = bias_of(s)
                scores = scores + jnp.concatenate([bias] * (size // rows), axis=0)
            new = jnp.max(scores, axis=1, keepdims=True)
            if start == "new":
                new = jnp.broadcast_to(new, (size, HD))
            else:
                acc, stat = (acc_in, stat_in) if start == "in" else (acc_out, stat_out)
                stats = stat[0, s, here, :]
                old = jnp.broadcast_to(stats[:, :1], (size, HD))
                total = jnp.broadcast_to(stats[:, HD - 1 :], (size, HD))
                new = jnp.maximum(old, new)
            weights = jnp.exp2(scores - jnp.concatenate([new] * (width // HD), axis=1))
            update = jnp.dot(weights.astype(jnp.bfloat16), values, preferred_element_type=jnp.float32)
            update, share = update[:, :HD], update[:, HD:]
            if start != "new":
                shrink = jnp.exp2(old - new)
                update = acc[0, s, here, :] * shrink + update
                share = total * shrink + share
            acc_out[0, s, here, :] = update
            stat_out[0, s, here, :] = jnp.where(lane < HD // 2, new, share)

    for number, members in enumerate(groups):
        limits = []
        full, some = jnp.bool_(True), jnp.bool_(False)
        for s in range(2):
            first_row = block_start(0, 0, s)
            limits.append([])
            for _, _, (kind, dx, dy, flip) in members:
                if kind == "root":
                    limit = visible - block_start(dx, dy, flip)
                    some_here = limit > 0
                elif kind == "own":
                    limit = first_row - block_start(dx, dy, flip) + 1
                    some_here = limit + rows - 1 > 0
                else:
                    limit = jnp.where(depth > 0, rows, 0)
                    some_here = limit > 0
                limits[s].append(limit)
                full = full & (limit >= rows)
                some = some | some_here
        kinds = {block[0] for _, _, block in members}
        if first and number == 0:
            step(members, limits, True, "new")
            continue
        start = "in" if number == 0 else "out"
        pl.when(full)(functools.partial(step, members, limits, False, start))
        if kinds == {"kin"}:
            some = full
        else:
            pl.when(jnp.logical_not(full) & some)(functools.partial(step, members, limits, True, start))
        if number == 0:

            @pl.when(jnp.logical_not(some))
            def _():
                acc_out[...] = acc_in[...]
                stat_out[...] = stat_in[...]

    if last:
        for s in range(2):
            for g in range(GW):
                here = slice(g * rows, (g + 1) * rows)
                done = acc_out[0, s, here, :] / stat_out[0, s, here, HD - 1 :]
                outs[s][:, g * HD : (g + 1) * HD] = done.astype(jnp.bfloat16)


def attend(ny, rows, tables, arrays, groups, queries, state, last):
    stacked = GW * rows
    first = state is None
    smem = pl.BlockSpec(memory_space=pltpu.SMEM)
    row_spec = pl.BlockSpec((rows, GW * HD), lambda h: (0, h))
    q_spec = pl.BlockSpec((1, 2, stacked, 2 * HD), lambda h: (h, 0, 0, 0))
    state_spec = pl.BlockSpec((1, 2, stacked, HD), lambda h: (h, 0, 0, 0))
    scratch = []
    operands = [*tables]
    specs = [smem, smem]
    if first:
        operands += queries
        specs += [row_spec, row_spec]
    else:
        mark, *state, prepared = state
        operands.append(pltpu.with_memory_space_constraint(prepared, pltpu.HBM))
        specs.append(q_spec)
    for shift in (0, HALF_KV):
        for array in arrays:
            operands.append(array)
            specs.append(pl.BlockSpec((array.shape[0], HD), functools.partial(lambda s, h: (0, s + h), shift)))
    if not first:
        operands.append(mark)
        specs.append(pl.BlockSpec(memory_space=pl.ANY))
        for array in state:
            operands.append(pltpu.with_memory_space_constraint(array, pltpu.HBM))
            specs.append(state_spec)
    if last:
        out_shape = [jax.ShapeDtypeStruct((rows, HALF_KV * GW * HD), jnp.bfloat16)] * 2
        out_specs = [row_spec, row_spec]
        scratch = [pltpu.VMEM((1, 2, stacked, HD), jnp.float32)] * 2
    else:
        out_shape = [jax.ShapeDtypeStruct((8, HD), jnp.float32)]
        out_shape += [pltpu.HBM((HALF_KV, 2, stacked, HD), jnp.float32)] * 2
        out_specs = [pl.BlockSpec((8, HD), lambda h: (0, 0)), state_spec, state_spec]
    if first:
        out_shape.append(pltpu.HBM((HALF_KV, 2, stacked, 2 * HD), jnp.bfloat16))
        out_specs.append(q_spec)
    scores = HALF_KV * 2 * stacked * rows * sum(len(members) for members in groups)
    out = pl.pallas_call(
        functools.partial(attend_kernel, ny, rows, len(arrays), groups, first, last),
        grid=(HALF_KV,),
        in_specs=specs,
        out_specs=out_specs,
        out_shape=out_shape,
        scratch_shapes=scratch,
        compiler_params=pltpu.CompilerParams(vmem_limit_bytes=24 * 2**20),
        cost_estimate=pl.CostEstimate(flops=8 * scores * HD, bytes_accessed=4 * 2**20, transcendentals=scores),
    )(*operands)
    return list(out) if first or last else [*out, prepared]


def on_device(queries, seg_keys, seg_values, root_keys, root_values, expansion, root_offsets):
    leaves, spots = lax.axis_size("leaf"), lax.axis_size("ctx")
    ny = spots // 4
    rows = queries.shape[0]
    group = lax.axis_index("leaf")
    core = lax.rem(lax.axis_index("ctx"), 2)

    def halves(array):
        half = array.shape[1] // 2
        return (
            lax.dynamic_slice_in_dim(array, core * half, half, 1),
            lax.dynamic_slice_in_dim(array, (1 - core) * half, half, 1),
        )

    def index(x, y, k):
        return ((y % ny) * 2 + x % 2) * 2 + k % 2

    places = [(x, y, k) for y in range(ny) for x in range(2) for k in range(2)]

    def to_core(array):
        return lax.ppermute(array, "ctx", [(index(x, y, k), index(x, y, k + 1)) for x, y, k in places])

    def to_x(array):
        return lax.ppermute(array, "ctx", [(index(x, y, k), index(x + 1, y, k)) for x, y, k in places])

    def to_y(array, step):
        return lax.ppermute(array, "ctx", [(index(x, y, k), index(x, y + step, k)) for x, y, k in places])

    def packed(keys, values):
        (key_mine, key_other), (value_mine, value_other) = halves(keys), halves(values)
        return jnp.concatenate([key_mine, value_mine], axis=1), jnp.concatenate([key_other, value_other], axis=1)

    own_mine, own_other = packed(seg_keys, seg_values)
    root_mine, root_other = packed(root_keys, root_values)
    got = to_core(jnp.concatenate([own_other, root_other], axis=0))
    q_mine, q_other = halves(queries)
    q_pair = (q_mine, to_core(q_other))
    own = jnp.concatenate([own_mine, got[:rows]], axis=0)
    root = jnp.concatenate([root_mine, got[rows:]], axis=0)
    run = functools.partial(attend, ny, rows, (expansion, root_offsets))
    steps = range(1, ny)

    def members(array, kind, dx=0, dy=0, flips=(0, 1), first=0):
        return tuple((array, first + i, (kind, dx, dy, flip)) for i, flip in enumerate(flips))

    def after(state, *values):
        *values, state[0] = lax.optimization_barrier((*values, state[0]))
        return values

    choices = []

    def hop(step, down, up):
        down = lax.ppermute(down, "leaf", [(i, i - 1) for i in range(1, leaves - step + 1)])
        choices.append((group + step, down))
        if step < leaves - 1:
            up = lax.ppermute(up, "leaf", [(i, i + 1) for i in range(step - 1, leaves - 2)])
            choices.append((group - step, up))
        return down, up

    down, up = hop(1, own, own)
    own_x, own_y = to_x(own), [to_y(own, step) for step in steps]
    root_x, root_y = to_x(root), [to_y(root, step) for step in steps]
    state = run([own, root], (members(0, "own") + members(1, "root"),), q_pair, None, False)

    if leaves > 2:
        down, up = hop(2, *after(state, down, up))

    def near(kind, arrays):
        groups = [members(0, kind, 1) + members(1, kind, 0, 1)]
        groups += [members(step, kind, 0, step) for step in steps if step > 1]
        return run(arrays, tuple(groups), None, state, False)

    state = near("own", [own_x, *own_y])
    for step in range(3, leaves):
        down, up = hop(step, *after(state, down, up))
    own_x, root_x, *pairs = after(state, own_x, root_x, *own_y, *root_y)
    own_y, root_y = pairs[: ny - 1], pairs[ny - 1 :]
    tops = [to_y(jnp.concatenate([own_x[:rows], root_x[:rows]], axis=0), step) for step in steps]
    lows = [to_x(jnp.concatenate([a[rows:], b[rows:]], axis=0)) for a, b in zip(own_y, root_y)]
    state = near("root", [root_x, *root_y])

    parent = expansion[0, group]
    owners, helds = zip(*choices)
    helds = after(state, *helds)
    parent_rows = own
    for owner, held in zip(owners, helds):
        parent_rows = jnp.where(parent == owner, held, parent_rows)
    (parent_rows,) = after(state, parent_rows)
    kin_x, kin_y = to_x(parent_rows), [to_y(parent_rows, step) for step in steps]
    groups, arrays = [], []
    for step, top, low in zip(steps, tops, lows):
        at = len(arrays)
        groups.append(
            members(at, "own", 1, step, (0,))
            + members(at, "root", 1, step, (0,), 1)
            + members(at + 1, "own", 1, step, (1,))
            + members(at + 1, "root", 1, step, (1,), 1)
        )
        arrays += [top, low]
    state = run([*arrays, parent_rows], (*groups, members(len(arrays), "kin")), None, state, False)

    (kin_x,) = after(state, kin_x)
    tops = [to_y(kin_x[:rows], step) for step in steps]
    lows = [to_x(array[rows:]) for array in kin_y]
    groups = [members(0, "kin") + members(1, "kin")] + [members(step, "kin") for step in steps if step > 1]
    state = run([kin_x, *kin_y], tuple(groups), None, state, False)
    groups = [members(i, "kin", flips=(0,)) + members(len(tops) + i, "kin", flips=(1,)) for i in range(len(tops))]
    out_mine, out_other = run([*tops, *lows], tuple(groups), None, state, True)
    out_got = to_core(out_other)
    return jnp.where(
        core == 0,
        jnp.concatenate([out_mine, out_got], axis=1),
        jnp.concatenate([out_got, out_mine], axis=1),
    )


def solution(mesh):
    return jax.shard_map(
        on_device,
        mesh=mesh,
        in_specs=(
            P(("leaf", "ctx"), None),
            P(("leaf", "ctx"), None),
            P(("leaf", "ctx"), None),
            P("ctx", None),
            P("ctx", None),
            P(),
            P(),
        ),
        out_specs=P(("leaf", "ctx"), None),
        check_vma=False,
    )
```

```python
import functools
import math

import jax
import jax.numpy as jnp
from jax import lax
from jax.experimental import pallas as pl
from jax.experimental.pallas import tpu as pltpu
from jax.sharding import PartitionSpec as P

HQ = 64
KVH = 8
HD = 128
GW = HQ // KVH
HALF_KV = KVH // 2
NEG = -1e30
Q_SCALE = math.log2(math.e) / math.sqrt(HD)
ROW_BLOCK = 256


def attend_kernel(ny, rows, arrays, groups, first, last, *refs):
    refs = list(refs)
    take = lambda count: [refs.pop(0) for _ in range(count)]
    exp_ref, off_ref = take(2)
    raw = take(2 if first else 1)
    key_refs = take(arrays)
    value_refs = take(arrays)
    head = pl.program_id(0)
    if not first:
        take(2)
    if last:
        outs = take(2)
    else:
        take(1)[0][...] = jnp.zeros((8, HD), jnp.float32)
    (held,) = take(1)
    qs = take(1)[0] if first else raw[0]
    stacked = GW * rows

    group = lax.axis_index("leaf")
    spot = lax.axis_index("ctx")
    core, chip = lax.rem(spot, 2), spot // 2
    chip_x, chip_y = lax.rem(chip, 2), chip // 2
    visible = off_ref[group]
    depth = exp_ref[1, group]

    def block_start(dx, dy, flip):
        x = lax.rem(chip_x + dx, 2)
        y = lax.rem(chip_y - dy + ny, ny)
        k = lax.rem(core + flip, 2)
        return ((y * 2 + x) * 2 + k) * rows

    if first:
        for s, q_ref in enumerate(raw):
            for g in range(GW):
                q = q_ref[:, g * HD : (g + 1) * HD].astype(jnp.float32) * Q_SCALE
                high = q.astype(jnp.bfloat16)
                low = (q - high.astype(jnp.float32)).astype(jnp.bfloat16)
                qs[0, s, g * rows : (g + 1) * rows, :HD] = high
                qs[0, s, g * rows : (g + 1) * rows, HD:] = low

    def step(members, limits, masked, fresh):
        width = len(members) * rows
        cut = lambda refs: [refs[a][b * rows : (b + 1) * rows, :] for a, b, _ in members]
        keys = jnp.concatenate(cut(key_refs), axis=0)
        keys = jnp.concatenate([keys, keys], axis=1)
        values = jnp.concatenate(cut(value_refs), axis=0)
        values = jnp.concatenate([values, jnp.ones_like(values)], axis=1)
        size = min(ROW_BLOCK, stacked)
        todo = [(s, slice(base, base + size)) for s in range(2) for base in range(0, stacked, size)]

        def score(s, here):
            return lax.dot_general(
                qs[0, s, here, :], keys, (((1,), (1,)), ((), ())), preferred_element_type=jnp.float32
            )

        def bias_of(s):
            column = lax.broadcasted_iota(jnp.int32, (rows, rows), 1)
            line = lax.broadcasted_iota(jnp.int32, (rows, rows), 0)
            allowed = []
            for (_, _, block), limit in zip(members, limits[s]):
                ahead = column - line if block[0] == "own" else column
                allowed.append(jnp.where(ahead < limit, 0.0, NEG))
            return jnp.concatenate(allowed, axis=1)

        following = score(*todo[0])
        for at, (s, here) in enumerate(todo):
            scores = following
            if at + 1 < len(todo):
                following = score(*todo[at + 1])
            if masked:
                bias = bias_of(s)
                scores = scores + jnp.concatenate([bias] * (size // rows), axis=0)
            new = jnp.max(scores, axis=1, keepdims=True)
            if fresh:
                new = jnp.broadcast_to(new, (size, HD))
            else:
                old = held[head, s, here, 2 * HD :]
                new = jnp.maximum(old, new)
            weights = jnp.exp2(scores - jnp.concatenate([new] * (width // HD), axis=1))
            update = jnp.dot(weights.astype(jnp.bfloat16), values, preferred_element_type=jnp.float32)
            if fresh:
                held[head, s, here, : 2 * HD] = update
            else:
                shrink = jnp.exp2(old - new)
                before = held[head, s, here, : 2 * HD] * jnp.concatenate([shrink, shrink], axis=1)
                held[head, s, here, : 2 * HD] = before + update
            held[head, s, here, 2 * HD :] = new

    for number, members in enumerate(groups):
        limits = []
        full, some = jnp.bool_(True), jnp.bool_(False)
        for s in range(2):
            first_row = block_start(0, 0, s)
            limits.append([])
            for _, _, (kind, dx, dy, flip) in members:
                if kind == "root":
                    limit = visible - block_start(dx, dy, flip)
                    some_here = limit > 0
                elif kind == "own":
                    limit = first_row - block_start(dx, dy, flip) + 1
                    some_here = limit + rows - 1 > 0
                else:
                    limit = jnp.where(depth > 0, rows, 0)
                    some_here = limit > 0
                limits[s].append(limit)
                full = full & (limit >= rows)
                some = some | some_here
        kinds = {block[0] for _, _, block in members}
        if first and number == 0:
            step(members, limits, True, True)
            continue
        pl.when(full)(functools.partial(step, members, limits, False, False))
        if kinds != {"kin"}:
            pl.when(jnp.logical_not(full) & some)(functools.partial(step, members, limits, True, False))

    if last:
        for s in range(2):
            for g in range(GW):
                here = slice(g * rows, (g + 1) * rows)
                done = held[head, s, here, :HD] / held[head, s, here, HD : 2 * HD]
                outs[s][:, g * HD : (g + 1) * HD] = done.astype(jnp.bfloat16)


WHOLE = pl.BlockSpec(memory_space=pltpu.VMEM)


def fence(state, *values):
    mark, held, prepared = state
    *values, mark = lax.optimization_barrier((*values, mark))

    def kernel(mark_ref, held_ref, out_ref, held_out_ref):
        out_ref[...] = mark_ref[...]

    mark, held = pl.pallas_call(
        kernel,
        in_specs=[WHOLE, WHOLE],
        out_specs=[WHOLE, WHOLE],
        out_shape=[jax.ShapeDtypeStruct(mark.shape, mark.dtype), pltpu.VMEM(held.shape, held.dtype)],
        input_output_aliases={1: 1},
        compiler_params=pltpu.CompilerParams(vmem_limit_bytes=4 * 2**20),
    )(mark, pltpu.with_memory_space_constraint(held, pltpu.VMEM))
    state[:] = [mark, held, prepared]
    return values


def pick(state, table, owners, arrays):
    mark, held, prepared = state
    count = len(arrays)

    def kernel(table_ref, mark_ref, *refs):
        out_ref, mark_out_ref, _, sem = refs[count + 1 :]
        group = lax.axis_index("leaf")
        parent = table_ref[0, group]
        mark_out_ref[...] = mark_ref[...]
        for owner, ref in zip(owners, refs):

            @pl.when(parent == group + owner)
            def _():
                copy = pltpu.make_async_copy(ref, out_ref, sem)
                copy.start()
                copy.wait()

    anywhere = pl.BlockSpec(memory_space=pl.ANY)
    picked, mark, held = pl.pallas_call(
        kernel,
        in_specs=[pl.BlockSpec(memory_space=pltpu.SMEM), WHOLE] + [anywhere] * count + [WHOLE],
        out_specs=[anywhere, WHOLE, WHOLE],
        out_shape=[
            jax.ShapeDtypeStruct(arrays[0].shape, arrays[0].dtype),
            jax.ShapeDtypeStruct(mark.shape, mark.dtype),
            pltpu.VMEM(held.shape, held.dtype),
        ],
        scratch_shapes=[pltpu.SemaphoreType.DMA(())],
        input_output_aliases={count + 2: 2},
        compiler_params=pltpu.CompilerParams(vmem_limit_bytes=4 * 2**20),
    )(table, mark, *arrays, pltpu.with_memory_space_constraint(held, pltpu.VMEM))
    state[:] = [mark, held, prepared]
    return picked


def attend(ny, rows, tables, arrays, groups, queries, state, last):
    stacked = GW * rows
    first = state is None
    smem = pl.BlockSpec(memory_space=pltpu.SMEM)
    row_spec = pl.BlockSpec((rows, GW * HD), lambda h: (0, h))
    q_spec = pl.BlockSpec((1, 2, stacked, 2 * HD), lambda h: (h, 0, 0, 0))
    operands = [*tables]
    specs = [smem, smem]
    if first:
        operands += queries
        specs += [row_spec, row_spec]
    else:
        mark, state, prepared = state
        operands.append(pltpu.with_memory_space_constraint(prepared, pltpu.HBM))
        specs.append(q_spec)
    for shift in (0, HALF_KV):
        for array in arrays:
            operands.append(array)
            specs.append(pl.BlockSpec((array.shape[0], HD), functools.partial(lambda s, h: (0, s + h), shift)))
    aliases = {}
    if last:
        out_shape = [jax.ShapeDtypeStruct((rows, HALF_KV * GW * HD), jnp.bfloat16)] * 2
        out_specs = [row_spec, row_spec]
    else:
        out_shape = [jax.ShapeDtypeStruct((8, HD), jnp.float32)]
        out_specs = [pl.BlockSpec((8, HD), lambda h: (0, 0))]
    if not first:
        aliases = {len(operands) + 1: len(out_shape)}
        operands += [mark, pltpu.with_memory_space_constraint(state, pltpu.VMEM)]
        specs += [pl.BlockSpec(memory_space=pl.ANY), WHOLE]
    out_shape.append(pltpu.VMEM((HALF_KV, 2, stacked, 3 * HD), jnp.float32))
    out_specs.append(WHOLE)
    if first:
        out_shape.append(pltpu.HBM((HALF_KV, 2, stacked, 2 * HD), jnp.bfloat16))
        out_specs.append(q_spec)
    scores = HALF_KV * 2 * stacked * rows * sum(len(members) for members in groups)
    out = pl.pallas_call(
        functools.partial(attend_kernel, ny, rows, len(arrays), groups, first, last),
        grid=(HALF_KV,),
        in_specs=specs,
        out_specs=out_specs,
        out_shape=out_shape,
        input_output_aliases=aliases,
        compiler_params=pltpu.CompilerParams(vmem_limit_bytes=24 * 2**20),
        cost_estimate=pl.CostEstimate(flops=8 * scores * HD, bytes_accessed=4 * 2**20, transcendentals=scores),
    )(*operands)
    return out[:2] if last else list(out) if first else [*out, prepared]


def on_device(queries, seg_keys, seg_values, root_keys, root_values, expansion, root_offsets):
    leaves, spots = lax.axis_size("leaf"), lax.axis_size("ctx")
    ny = spots // 4
    rows = queries.shape[0]
    group = lax.axis_index("leaf")
    core = lax.rem(lax.axis_index("ctx"), 2)

    def halves(array):
        half = array.shape[1] // 2
        return (
            lax.dynamic_slice_in_dim(array, core * half, half, 1),
            lax.dynamic_slice_in_dim(array, (1 - core) * half, half, 1),
        )

    def index(x, y, k):
        return ((y % ny) * 2 + x % 2) * 2 + k % 2

    places = [(x, y, k) for y in range(ny) for x in range(2) for k in range(2)]

    def to_core(array):
        return lax.ppermute(array, "ctx", [(index(x, y, k), index(x, y, k + 1)) for x, y, k in places])

    def to_x(array):
        return lax.ppermute(array, "ctx", [(index(x, y, k), index(x + 1, y, k)) for x, y, k in places])

    def to_y(array, step):
        return lax.ppermute(array, "ctx", [(index(x, y, k), index(x, y + step, k)) for x, y, k in places])

    def packed(keys, values):
        (key_mine, key_other), (value_mine, value_other) = halves(keys), halves(values)
        return jnp.concatenate([key_mine, value_mine], axis=1), jnp.concatenate([key_other, value_other], axis=1)

    own_mine, own_other = packed(seg_keys, seg_values)
    root_mine, root_other = packed(root_keys, root_values)
    got = to_core(jnp.concatenate([own_other, root_other], axis=0))
    q_mine, q_other = halves(queries)
    q_pair = (q_mine, to_core(q_other))
    own = jnp.concatenate([own_mine, got[:rows]], axis=0)
    root = jnp.concatenate([root_mine, got[rows:]], axis=0)
    run = functools.partial(attend, ny, rows, (expansion, root_offsets))
    steps = range(1, ny)

    def members(array, kind, dx=0, dy=0, flips=(0, 1), first=0):
        return tuple((array, first + i, (kind, dx, dy, flip)) for i, flip in enumerate(flips))

    def after(state, *values):
        *values, state[0] = lax.optimization_barrier((*values, state[0]))
        return values

    choices = []

    def hop(step, down, up):
        down = lax.ppermute(down, "leaf", [(i, i - 1) for i in range(1, leaves - step + 1)])
        choices.append((step, down))
        if step < leaves - 1:
            up = lax.ppermute(up, "leaf", [(i, i + 1) for i in range(step - 1, leaves - 2)])
            choices.append((-step, up))
        return down, up

    down, up = hop(1, own, own)
    own_x, own_y = to_x(own), [to_y(own, step) for step in steps]
    root_x, root_y = to_x(root), [to_y(root, step) for step in steps]
    state = run([own, root], (members(0, "own") + members(1, "root"),), q_pair, None, False)

    if leaves > 2:
        down, up = hop(2, *fence(state, down, up))
    own_x, *own_y = after(state, own_x, *own_y)

    def near(kind, arrays):
        groups = [members(0, kind, 1) + members(1, kind, 0, 1)]
        groups += [members(step, kind, 0, step) for step in steps if step > 1]
        return run(arrays, tuple(groups), None, state, False)

    state = near("own", [own_x, *own_y])
    for step in range(3, leaves):
        down, up = hop(step, *fence(state, down, up))
    own_x, root_x, *pairs = after(state, own_x, root_x, *own_y, *root_y)
    own_y, root_y = pairs[: ny - 1], pairs[ny - 1 :]
    tops = [to_y(jnp.concatenate([own_x[:rows], root_x[:rows]], axis=0), step) for step in steps]
    lows = [to_x(jnp.concatenate([a[rows:], b[rows:]], axis=0)) for a, b in zip(own_y, root_y)]
    state = near("root", [root_x, *root_y])

    owners, helds = zip(*choices)
    parent_rows = pick(state, expansion, (0, *owners), (own, *after(state, *helds)))
    (parent_rows,) = after(state, parent_rows)
    kin_x, kin_y = to_x(parent_rows), [to_y(parent_rows, step) for step in steps]
    groups, arrays = [], []
    for step, top, low in zip(steps, tops, lows):
        at = len(arrays)
        groups.append(
            members(at, "own", 1, step, (0,))
            + members(at, "root", 1, step, (0,), 1)
            + members(at + 1, "own", 1, step, (1,))
            + members(at + 1, "root", 1, step, (1,), 1)
        )
        arrays += [top, low]
    state = run([*arrays, parent_rows], (*groups, members(len(arrays), "kin")), None, state, False)

    (kin_x,) = after(state, kin_x)
    tops = [to_y(kin_x[:rows], step) for step in steps]
    lows = [to_x(array[rows:]) for array in kin_y]
    groups = [members(0, "kin") + members(1, "kin")] + [members(step, "kin") for step in steps if step > 1]
    state = run([kin_x, *kin_y], tuple(groups), None, state, False)
    groups = [members(i, "kin", flips=(0,)) + members(len(tops) + i, "kin", flips=(1,)) for i in range(len(tops))]
    out_mine, out_other = run([*tops, *lows], tuple(groups), None, state, True)
    out_got = to_core(out_other)
    return jnp.where(
        core == 0,
        jnp.concatenate([out_mine, out_got], axis=1),
        jnp.concatenate([out_got, out_mine], axis=1),
    )


def solution(mesh):
    return jax.shard_map(
        on_device,
        mesh=mesh,
        in_specs=(
            P(("leaf", "ctx"), None),
            P(("leaf", "ctx"), None),
            P(("leaf", "ctx"), None),
            P("ctx", None),
            P("ctx", None),
            P(),
            P(),
        ),
        out_specs=P(("leaf", "ctx"), None),
        check_vma=False,
    )
```

```python
import functools
import math

import jax
import jax.numpy as jnp
from jax import lax
from jax.experimental import pallas as pl
from jax.experimental.pallas import tpu as pltpu
from jax.sharding import PartitionSpec as P

HQ = 64
KVH = 8
HD = 128
GW = HQ // KVH
HALF_KV = KVH // 2
NEG = -1e30
Q_SCALE = math.log2(math.e) / math.sqrt(HD)
ROW_BLOCK = 256


def attend_kernel(ny, rows, arrays, groups, first, last, *refs):
    refs = list(refs)
    take = lambda count: [refs.pop(0) for _ in range(count)]
    exp_ref, off_ref = take(2)
    raw = take(2) if first else None
    key_refs = take(arrays)
    value_refs = take(arrays)
    head = pl.program_id(0)
    if not first:
        take(3)
    if last:
        outs = take(2)
    else:
        take(1)[0][...] = jnp.zeros((8, HD), jnp.float32)
    held, qs = take(2)
    stacked = GW * rows

    group = lax.axis_index("leaf")
    spot = lax.axis_index("ctx")
    core, chip = lax.rem(spot, 2), spot // 2
    chip_x, chip_y = lax.rem(chip, 2), chip // 2
    visible = off_ref[group]
    depth = exp_ref[1, group]

    def block_start(dx, dy, flip):
        x = lax.rem(chip_x + dx, 2)
        y = lax.rem(chip_y - dy + ny, ny)
        k = lax.rem(core + flip, 2)
        return ((y * 2 + x) * 2 + k) * rows

    if first:
        for s, q_ref in enumerate(raw):
            for g in range(GW):
                q = q_ref[:, g * HD : (g + 1) * HD].astype(jnp.float32) * Q_SCALE
                high = q.astype(jnp.bfloat16)
                low = (q - high.astype(jnp.float32)).astype(jnp.bfloat16)
                qs[head, s, g * rows : (g + 1) * rows, :HD] = high
                qs[head, s, g * rows : (g + 1) * rows, HD:] = low

    def step(members, limits, masked, fresh):
        width = len(members) * rows
        cut = lambda refs: [refs[a][b * rows : (b + 1) * rows, :] for a, b, _ in members]
        keys = jnp.concatenate(cut(key_refs), axis=0)
        keys = jnp.concatenate([keys, keys], axis=1)
        values = jnp.concatenate(cut(value_refs), axis=0)
        values = jnp.concatenate([values, jnp.ones_like(values)], axis=1)
        size = min(ROW_BLOCK, stacked)
        todo = [(s, slice(base, base + size)) for s in range(2) for base in range(0, stacked, size)]

        def score(s, here):
            return lax.dot_general(
                qs[head, s, here, :], keys, (((1,), (1,)), ((), ())), preferred_element_type=jnp.float32
            )

        def bias_of(s):
            column = lax.broadcasted_iota(jnp.int32, (rows, rows), 1)
            line = lax.broadcasted_iota(jnp.int32, (rows, rows), 0)
            allowed = []
            for (_, _, block), limit in zip(members, limits[s]):
                ahead = column - line if block[0] == "own" else column
                allowed.append(jnp.where(ahead < limit, 0.0, NEG))
            return jnp.concatenate(allowed, axis=1)

        following = score(*todo[0])
        for at, (s, here) in enumerate(todo):
            scores = following
            if at + 1 < len(todo):
                following = score(*todo[at + 1])
            if masked:
                bias = bias_of(s)
                scores = scores + jnp.concatenate([bias] * (size // rows), axis=0)
            new = jnp.max(scores, axis=1, keepdims=True)
            if fresh:
                new = jnp.broadcast_to(new, (size, HD))
            else:
                old = held[head, s, here, 2 * HD :]
                new = jnp.maximum(old, new)
            weights = jnp.exp2(scores - jnp.concatenate([new] * (width // HD), axis=1))
            update = jnp.dot(weights.astype(jnp.bfloat16), values, preferred_element_type=jnp.float32)
            if fresh:
                held[head, s, here, : 2 * HD] = update
            else:
                shrink = jnp.exp2(old - new)
                before = held[head, s, here, : 2 * HD] * jnp.concatenate([shrink, shrink], axis=1)
                held[head, s, here, : 2 * HD] = before + update
            held[head, s, here, 2 * HD :] = new

    for number, members in enumerate(groups):
        limits = []
        full, some = jnp.bool_(True), jnp.bool_(False)
        for s in range(2):
            first_row = block_start(0, 0, s)
            limits.append([])
            for _, _, (kind, dx, dy, flip) in members:
                if kind == "root":
                    limit = visible - block_start(dx, dy, flip)
                    some_here = limit > 0
                elif kind == "own":
                    limit = first_row - block_start(dx, dy, flip) + 1
                    some_here = limit + rows - 1 > 0
                else:
                    limit = jnp.where(depth > 0, rows, 0)
                    some_here = limit > 0
                limits[s].append(limit)
                full = full & (limit >= rows)
                some = some | some_here
        kinds = {block[0] for _, _, block in members}
        if first and number == 0:
            step(members, limits, True, True)
            continue
        pl.when(full)(functools.partial(step, members, limits, False, False))
        if kinds != {"kin"}:
            pl.when(jnp.logical_not(full) & some)(functools.partial(step, members, limits, True, False))

    if last:
        for s in range(2):
            for g in range(GW):
                here = slice(g * rows, (g + 1) * rows)
                done = held[head, s, here, :HD] / held[head, s, here, HD : 2 * HD]
                outs[s][:, g * HD : (g + 1) * HD] = done.astype(jnp.bfloat16)


WHOLE = pl.BlockSpec(memory_space=pltpu.VMEM)


def in_vmem(array):
    return pltpu.with_memory_space_constraint(array, pltpu.VMEM)


def fence(state, *values):
    mark, held, prepared = state
    *values, mark = lax.optimization_barrier((*values, mark))

    def kernel(mark_ref, *refs):
        refs[2][...] = mark_ref[...]

    state[:] = pl.pallas_call(
        kernel,
        in_specs=[WHOLE] * 3,
        out_specs=[WHOLE] * 3,
        out_shape=[
            jax.ShapeDtypeStruct(mark.shape, mark.dtype),
            pltpu.VMEM(held.shape, held.dtype),
            pltpu.VMEM(prepared.shape, prepared.dtype),
        ],
        input_output_aliases={1: 1, 2: 2},
        compiler_params=pltpu.CompilerParams(vmem_limit_bytes=4 * 2**20),
    )(mark, in_vmem(held), in_vmem(prepared))
    return values


def pick(state, table, leaves, arrays):
    mark, held, prepared = state
    count = len(arrays)

    def kernel(table_ref, mark_ref, *refs):
        out_ref, mark_out_ref, _, _, sem = refs[count + 2 :]
        group = lax.axis_index("leaf")
        parent = table_ref[0, group]
        mark_out_ref[...] = mark_ref[...]
        for ahead, ref in enumerate(refs[:count]):

            @pl.when(parent == lax.rem(group + ahead, leaves))
            def _():
                copy = pltpu.make_async_copy(ref, out_ref, sem)
                copy.start()
                copy.wait()

    anywhere = pl.BlockSpec(memory_space=pl.ANY)
    picked, *state[:] = pl.pallas_call(
        kernel,
        in_specs=[pl.BlockSpec(memory_space=pltpu.SMEM), WHOLE] + [anywhere] * count + [WHOLE] * 2,
        out_specs=[anywhere, WHOLE, WHOLE, WHOLE],
        out_shape=[
            jax.ShapeDtypeStruct(arrays[0].shape, arrays[0].dtype),
            jax.ShapeDtypeStruct(mark.shape, mark.dtype),
            pltpu.VMEM(held.shape, held.dtype),
            pltpu.VMEM(prepared.shape, prepared.dtype),
        ],
        scratch_shapes=[pltpu.SemaphoreType.DMA(())],
        input_output_aliases={count + 2: 2, count + 3: 3},
        compiler_params=pltpu.CompilerParams(vmem_limit_bytes=4 * 2**20),
    )(table, mark, *arrays, in_vmem(held), in_vmem(prepared))
    return picked


def assemble(mine, got):
    rows, half = mine.shape

    def kernel(mine_ref, got_ref, out_ref, sems):
        core = lax.rem(lax.axis_index("ctx"), 2)
        copies = []
        for i, (ref, place) in enumerate(((mine_ref, core), (got_ref, 1 - core))):
            columns = pl.ds(pl.multiple_of(place * half, half), half)
            copies.append(pltpu.make_async_copy(ref, out_ref.at[:, columns], sems.at[i]))
            copies[i].start()
        for copy in copies:
            copy.wait()

    anywhere = pl.BlockSpec(memory_space=pl.ANY)
    return pl.pallas_call(
        kernel,
        in_specs=[anywhere] * 2,
        out_specs=anywhere,
        out_shape=jax.ShapeDtypeStruct((rows, 2 * half), mine.dtype),
        scratch_shapes=[pltpu.SemaphoreType.DMA((2,))],
        compiler_params=pltpu.CompilerParams(vmem_limit_bytes=4 * 2**20),
    )(mine, got)


def attend(ny, rows, tables, arrays, groups, queries, state, last):
    stacked = GW * rows
    first = state is None
    smem = pl.BlockSpec(memory_space=pltpu.SMEM)
    row_spec = pl.BlockSpec((rows, GW * HD), lambda h: (0, h))
    operands = [*tables]
    specs = [smem, smem]
    if first:
        operands += queries
        specs += [row_spec, row_spec]
    else:
        mark, state, prepared = state
    for shift in (0, HALF_KV):
        for array in arrays:
            operands.append(array)
            specs.append(pl.BlockSpec((array.shape[0], HD), functools.partial(lambda s, h: (0, s + h), shift)))
    aliases = {}
    if last:
        out_shape = [jax.ShapeDtypeStruct((rows, HALF_KV * GW * HD), jnp.bfloat16)] * 2
        out_specs = [row_spec, row_spec]
    else:
        out_shape = [jax.ShapeDtypeStruct((8, HD), jnp.float32)]
        out_specs = [pl.BlockSpec((8, HD), lambda h: (0, 0))]
    if not first:
        aliases = {len(operands) + 1 + i: len(out_shape) + i for i in range(2)}
        operands += [mark, in_vmem(state), in_vmem(prepared)]
        specs += [pl.BlockSpec(memory_space=pl.ANY), WHOLE, WHOLE]
    out_shape.append(pltpu.VMEM((HALF_KV, 2, stacked, 3 * HD), jnp.float32))
    out_shape.append(pltpu.VMEM((HALF_KV, 2, stacked, 2 * HD), jnp.bfloat16))
    out_specs += [WHOLE, WHOLE]
    scores = HALF_KV * 2 * stacked * rows * sum(len(members) for members in groups)
    out = pl.pallas_call(
        functools.partial(attend_kernel, ny, rows, len(arrays), groups, first, last),
        grid=(HALF_KV,),
        in_specs=specs,
        out_specs=out_specs,
        out_shape=out_shape,
        input_output_aliases=aliases,
        compiler_params=pltpu.CompilerParams(vmem_limit_bytes=24 * 2**20),
        cost_estimate=pl.CostEstimate(flops=8 * scores * HD, bytes_accessed=4 * 2**20, transcendentals=scores),
    )(*operands)
    return out[:2] if last else list(out)


def on_device(queries, seg_keys, seg_values, root_keys, root_values, expansion, root_offsets):
    leaves, spots = lax.axis_size("leaf"), lax.axis_size("ctx")
    ny = spots // 4
    rows = queries.shape[0]
    group = lax.axis_index("leaf")
    core = lax.rem(lax.axis_index("ctx"), 2)

    def halves(array):
        half = array.shape[1] // 2
        return (
            lax.dynamic_slice_in_dim(array, core * half, half, 1),
            lax.dynamic_slice_in_dim(array, (1 - core) * half, half, 1),
        )

    def index(x, y, k):
        return ((y % ny) * 2 + x % 2) * 2 + k % 2

    places = [(x, y, k) for y in range(ny) for x in range(2) for k in range(2)]

    def to_core(array):
        return lax.ppermute(array, "ctx", [(index(x, y, k), index(x, y, k + 1)) for x, y, k in places])

    def to_x(array):
        return lax.ppermute(array, "ctx", [(index(x, y, k), index(x + 1, y, k)) for x, y, k in places])

    def to_y(array, step):
        return lax.ppermute(array, "ctx", [(index(x, y, k), index(x, y + step, k)) for x, y, k in places])

    def packed(keys, values):
        (key_mine, key_other), (value_mine, value_other) = halves(keys), halves(values)
        return jnp.concatenate([key_mine, value_mine], axis=1), jnp.concatenate([key_other, value_other], axis=1)

    own_mine, own_other = packed(seg_keys, seg_values)
    root_mine, root_other = packed(root_keys, root_values)
    sent = jnp.concatenate([own_other, root_other], axis=0)
    got = to_core(sent)
    queries, _ = lax.optimization_barrier((queries, sent))
    q_mine, q_other = halves(queries)
    q_pair = (q_mine, to_core(q_other))
    own = jnp.concatenate([own_mine, got[:rows]], axis=0)
    root = jnp.concatenate([root_mine, got[rows:]], axis=0)
    run = functools.partial(attend, ny, rows, (expansion, root_offsets))
    steps = range(1, ny)

    def members(array, kind, dx=0, dy=0, flips=(0, 1), first=0):
        return tuple((array, first + i, (kind, dx, dy, flip)) for i, flip in enumerate(flips))

    def after(state, *values):
        *values, state[0] = lax.optimization_barrier((*values, state[0]))
        return values

    def hop(step, rows_held):
        pairs = [(i, (i - 1) % leaves) for i in range(leaves)]
        return lax.ppermute(rows_held, "leaf", pairs if step < leaves - 1 else pairs[1:])

    ahead = [own]
    if leaves > 1:
        ahead.append(hop(1, own))
    own_x, own_y = to_x(own), [to_y(own, step) for step in steps]
    root_x, root_y = to_x(root), [to_y(root, step) for step in steps]
    state = run([own, root], (members(0, "own") + members(1, "root"),), q_pair, None, False)

    def near(kind, arrays):
        groups = [members(0, kind, 1) + members(1, kind, 0, 1)]
        groups += [members(step, kind, 0, step) for step in steps if step > 1]
        return run(arrays, tuple(groups), None, state, False)

    if leaves > 2:
        (held,) = fence(state, ahead[-1])
        ahead[-1] = held
        ahead.append(hop(2, held))
    own_x, *own_y = after(state, own_x, *own_y)
    own_far = [to_y(own_x, step) for step in steps]
    state = near("own", [own_x, *own_y])
    for step in range(3, leaves):
        (held,) = fence(state, ahead[-1])
        ahead[-1] = held
        ahead.append(hop(step, held))
    root_x, *root_y = after(state, root_x, *root_y)
    root_far = [to_y(root_x, step) for step in steps]
    state = near("root", [root_x, *root_y])

    parent_rows = pick(state, expansion, leaves, after(state, *ahead))
    (parent_rows,) = after(state, parent_rows)
    kin_x, kin_y = to_x(parent_rows), [to_y(parent_rows, step) for step in steps]
    far = [members(i, "own", 1, i + 1) + members(ny - 1 + i, "root", 1, i + 1) for i in range(ny - 1)]
    far.append(members(2 * ny - 2, "kin"))
    if ny == 2:
        far = [far[0] + far[1]]
    state = run([*own_far, *root_far, parent_rows], tuple(far), None, state, False)

    (kin_x,) = after(state, kin_x)
    tops = [to_y(kin_x[:rows], step) for step in steps]
    lows = [to_x(array[rows:]) for array in kin_y]
    groups = [members(0, "kin") + members(1, "kin")] + [members(step, "kin") for step in steps if step > 1]
    state = run([kin_x, *kin_y], tuple(groups), None, state, False)
    groups = [members(i, "kin", flips=(0,)) + members(len(tops) + i, "kin", flips=(1,)) for i in range(len(tops))]
    out_mine, out_other = run([*tops, *lows], tuple(groups), None, state, True)
    return assemble(out_mine, to_core(out_other))


def solution(mesh):
    return jax.shard_map(
        on_device,
        mesh=mesh,
        in_specs=(
            P(("leaf", "ctx"), None),
            P(("leaf", "ctx"), None),
            P(("leaf", "ctx"), None),
            P("ctx", None),
            P("ctx", None),
            P(),
            P(),
        ),
        out_specs=P(("leaf", "ctx"), None),
        check_vma=False,
    )
```

```python
import functools
import math

import jax
import jax.numpy as jnp
from jax import lax
from jax.experimental import pallas as pl
from jax.experimental.pallas import tpu as pltpu
from jax.sharding import PartitionSpec as P

HQ = 64
KVH = 8
HD = 128
GW = HQ // KVH
HALF_KV = KVH // 2
NEG = -1e30
Q_SCALE = math.log2(math.e) / math.sqrt(HD)
ROW_BLOCK = 256


def attend_kernel(ny, rows, arrays, groups, first, last, *refs):
    refs = list(refs)
    take = lambda count: [refs.pop(0) for _ in range(count)]
    exp_ref, off_ref = take(2)
    raw = take(2) if first else None
    key_refs = take(arrays)
    value_refs = take(arrays)
    head = pl.program_id(0)
    if not first:
        take(3)
    if last:
        outs = take(2)
    else:
        take(1)[0][...] = jnp.zeros((8, HD), jnp.float32)
    held, qs = take(2)
    stacked = GW * rows

    group = lax.axis_index("leaf")
    spot = lax.axis_index("ctx")
    core, chip = lax.rem(spot, 2), spot // 2
    chip_x, chip_y = lax.rem(chip, 2), chip // 2
    visible = off_ref[group]
    depth = exp_ref[1, group]

    def block_start(dx, dy, flip):
        x = lax.rem(chip_x + dx, 2)
        y = lax.rem(chip_y - dy + ny, ny)
        k = lax.rem(core + flip, 2)
        return ((y * 2 + x) * 2 + k) * rows

    if first:
        for s, q_ref in enumerate(raw):
            for g in range(GW):
                q = q_ref[:, g * HD : (g + 1) * HD].astype(jnp.float32) * Q_SCALE
                high = q.astype(jnp.bfloat16)
                low = (q - high.astype(jnp.float32)).astype(jnp.bfloat16)
                qs[head, s, g * rows : (g + 1) * rows, :HD] = high
                qs[head, s, g * rows : (g + 1) * rows, HD:] = low

    def step(members, limits, masked, fresh):
        width = len(members) * rows
        cut = lambda refs: [refs[a][b * rows : (b + 1) * rows, :] for a, b, _ in members]
        keys = jnp.concatenate(cut(key_refs), axis=0)
        keys = jnp.concatenate([keys, keys], axis=1)
        values = jnp.concatenate(cut(value_refs), axis=0)
        values = jnp.concatenate([values, jnp.ones_like(values)], axis=1)
        size = min(ROW_BLOCK, stacked)
        todo = [(s, slice(base, base + size)) for s in range(2) for base in range(0, stacked, size)]

        def score(s, here):
            return lax.dot_general(
                qs[head, s, here, :], keys, (((1,), (1,)), ((), ())), preferred_element_type=jnp.float32
            )

        def bias_of(s):
            column = lax.broadcasted_iota(jnp.int32, (rows, rows), 1)
            line = lax.broadcasted_iota(jnp.int32, (rows, rows), 0)
            allowed = []
            for (_, _, block), limit in zip(members, limits[s]):
                ahead = column - line if block[0] == "own" else column
                allowed.append(jnp.where(ahead < limit, 0.0, NEG))
            return jnp.concatenate(allowed, axis=1)

        following = score(*todo[0])
        for at, (s, here) in enumerate(todo):
            scores = following
            if at + 1 < len(todo):
                following = score(*todo[at + 1])
            if masked:
                bias = bias_of(s)
                scores = scores + jnp.concatenate([bias] * (size // rows), axis=0)
            new = jnp.max(scores, axis=1, keepdims=True)
            if fresh:
                new = jnp.broadcast_to(new, (size, HD))
            else:
                old = held[head, s, here, 2 * HD :]
                new = jnp.maximum(old, new)
            weights = jnp.exp2(scores - jnp.concatenate([new] * (width // HD), axis=1))
            update = jnp.dot(weights.astype(jnp.bfloat16), values, preferred_element_type=jnp.float32)
            if fresh:
                held[head, s, here, : 2 * HD] = update
            else:
                shrink = jnp.exp2(old - new)
                before = held[head, s, here, : 2 * HD] * jnp.concatenate([shrink, shrink], axis=1)
                held[head, s, here, : 2 * HD] = before + update
            held[head, s, here, 2 * HD :] = new

    for number, members in enumerate(groups):
        limits = []
        full, some = jnp.bool_(True), jnp.bool_(False)
        for s in range(2):
            first_row = block_start(0, 0, s)
            limits.append([])
            for _, _, (kind, dx, dy, flip) in members:
                if kind == "root":
                    limit = visible - block_start(dx, dy, flip)
                    some_here = limit > 0
                elif kind == "own":
                    limit = first_row - block_start(dx, dy, flip) + 1
                    some_here = limit + rows - 1 > 0
                else:
                    limit = jnp.where(depth > 0, rows, 0)
                    some_here = limit > 0
                limits[s].append(limit)
                full = full & (limit >= rows)
                some = some | some_here
        kinds = {block[0] for _, _, block in members}
        if first and number == 0:
            step(members, limits, True, True)
            continue
        pl.when(full)(functools.partial(step, members, limits, False, False))
        if kinds != {"kin"}:
            pl.when(jnp.logical_not(full) & some)(functools.partial(step, members, limits, True, False))

    if last:
        for s in range(2):
            for g in range(GW):
                here = slice(g * rows, (g + 1) * rows)
                done = held[head, s, here, :HD] / held[head, s, here, HD : 2 * HD]
                outs[s][:, g * HD : (g + 1) * HD] = done.astype(jnp.bfloat16)


WHOLE = pl.BlockSpec(memory_space=pltpu.VMEM)


def in_vmem(array):
    return pltpu.with_memory_space_constraint(array, pltpu.VMEM)


def fence(state, *values):
    mark, held, prepared = state
    *values, mark = lax.optimization_barrier((*values, mark))

    def kernel(mark_ref, *refs):
        refs[2][...] = mark_ref[...]

    state[:] = pl.pallas_call(
        kernel,
        in_specs=[WHOLE] * 3,
        out_specs=[WHOLE] * 3,
        out_shape=[
            jax.ShapeDtypeStruct(mark.shape, mark.dtype),
            pltpu.VMEM(held.shape, held.dtype),
            pltpu.VMEM(prepared.shape, prepared.dtype),
        ],
        input_output_aliases={1: 1, 2: 2},
        compiler_params=pltpu.CompilerParams(vmem_limit_bytes=4 * 2**20),
    )(mark, in_vmem(held), in_vmem(prepared))
    return values


def pick(state, table, leaves, arrays):
    mark, held, prepared = state
    count = len(arrays)

    def kernel(table_ref, mark_ref, *refs):
        out_ref, mark_out_ref, _, _, sem = refs[count + 2 :]
        group = lax.axis_index("leaf")
        parent = table_ref[0, group]
        mark_out_ref[...] = mark_ref[...]
        for ahead, ref in enumerate(refs[:count]):

            @pl.when(parent == lax.rem(group + ahead, leaves))
            def _():
                copy = pltpu.make_async_copy(ref, out_ref, sem)
                copy.start()
                copy.wait()

    anywhere = pl.BlockSpec(memory_space=pl.ANY)
    picked, *state[:] = pl.pallas_call(
        kernel,
        in_specs=[pl.BlockSpec(memory_space=pltpu.SMEM), WHOLE] + [anywhere] * count + [WHOLE] * 2,
        out_specs=[anywhere, WHOLE, WHOLE, WHOLE],
        out_shape=[
            jax.ShapeDtypeStruct(arrays[0].shape, arrays[0].dtype),
            jax.ShapeDtypeStruct(mark.shape, mark.dtype),
            pltpu.VMEM(held.shape, held.dtype),
            pltpu.VMEM(prepared.shape, prepared.dtype),
        ],
        scratch_shapes=[pltpu.SemaphoreType.DMA(())],
        input_output_aliases={count + 2: 2, count + 3: 3},
        compiler_params=pltpu.CompilerParams(vmem_limit_bytes=4 * 2**20),
    )(table, mark, *arrays, in_vmem(held), in_vmem(prepared))
    return picked


def assemble(mine, got):
    rows, half = mine.shape

    def kernel(mine_ref, got_ref, out_ref, sems):
        core = lax.rem(lax.axis_index("ctx"), 2)
        copies = []
        for i, (ref, place) in enumerate(((mine_ref, core), (got_ref, 1 - core))):
            columns = pl.ds(pl.multiple_of(place * half, half), half)
            copies.append(pltpu.make_async_copy(ref, out_ref.at[:, columns], sems.at[i]))
            copies[i].start()
        for copy in copies:
            copy.wait()

    anywhere = pl.BlockSpec(memory_space=pl.ANY)
    return pl.pallas_call(
        kernel,
        in_specs=[anywhere] * 2,
        out_specs=anywhere,
        out_shape=jax.ShapeDtypeStruct((rows, 2 * half), mine.dtype),
        scratch_shapes=[pltpu.SemaphoreType.DMA((2,))],
        compiler_params=pltpu.CompilerParams(vmem_limit_bytes=4 * 2**20),
    )(mine, got)


def attend(ny, rows, tables, arrays, groups, queries, state, last):
    stacked = GW * rows
    first = state is None
    smem = pl.BlockSpec(memory_space=pltpu.SMEM)
    row_spec = pl.BlockSpec((rows, GW * HD), lambda h: (0, h))
    operands = [*tables]
    specs = [smem, smem]
    if first:
        operands += queries
        specs += [row_spec, row_spec]
    else:
        mark, state, prepared = state
    for shift in (0, HALF_KV):
        for array in arrays:
            operands.append(array)
            specs.append(pl.BlockSpec((array.shape[0], HD), functools.partial(lambda s, h: (0, s + h), shift)))
    aliases = {}
    if last:
        out_shape = [jax.ShapeDtypeStruct((rows, HALF_KV * GW * HD), jnp.bfloat16)] * 2
        out_specs = [row_spec, row_spec]
    else:
        out_shape = [jax.ShapeDtypeStruct((8, HD), jnp.float32)]
        out_specs = [pl.BlockSpec((8, HD), lambda h: (0, 0))]
    if not first:
        aliases = {len(operands) + 1 + i: len(out_shape) + i for i in range(2)}
        operands += [mark, in_vmem(state), in_vmem(prepared)]
        specs += [pl.BlockSpec(memory_space=pl.ANY), WHOLE, WHOLE]
    out_shape.append(pltpu.VMEM((HALF_KV, 2, stacked, 3 * HD), jnp.float32))
    out_shape.append(pltpu.VMEM((HALF_KV, 2, stacked, 2 * HD), jnp.bfloat16))
    out_specs += [WHOLE, WHOLE]
    scores = HALF_KV * 2 * stacked * rows * sum(len(members) for members in groups)
    out = pl.pallas_call(
        functools.partial(attend_kernel, ny, rows, len(arrays), groups, first, last),
        grid=(HALF_KV,),
        in_specs=specs,
        out_specs=out_specs,
        out_shape=out_shape,
        input_output_aliases=aliases,
        compiler_params=pltpu.CompilerParams(vmem_limit_bytes=24 * 2**20),
        cost_estimate=pl.CostEstimate(flops=8 * scores * HD, bytes_accessed=4 * 2**20, transcendentals=scores),
    )(*operands)
    return out[:2] if last else list(out)


def on_device(queries, seg_keys, seg_values, root_keys, root_values, expansion, root_offsets):
    leaves, spots = lax.axis_size("leaf"), lax.axis_size("ctx")
    ny = spots // 4
    rows = queries.shape[0]
    group = lax.axis_index("leaf")
    core = lax.rem(lax.axis_index("ctx"), 2)

    def halves(array):
        half = array.shape[1] // 2
        return (
            lax.dynamic_slice_in_dim(array, core * half, half, 1),
            lax.dynamic_slice_in_dim(array, (1 - core) * half, half, 1),
        )

    def index(x, y, k):
        return ((y % ny) * 2 + x % 2) * 2 + k % 2

    places = [(x, y, k) for y in range(ny) for x in range(2) for k in range(2)]

    def to_core(array):
        return lax.ppermute(array, "ctx", [(index(x, y, k), index(x, y, k + 1)) for x, y, k in places])

    def to_x(array):
        return lax.ppermute(array, "ctx", [(index(x, y, k), index(x + 1, y, k)) for x, y, k in places])

    def to_y(array, step):
        return lax.ppermute(array, "ctx", [(index(x, y, k), index(x, y + step, k)) for x, y, k in places])

    def packed(keys, values):
        (key_mine, key_other), (value_mine, value_other) = halves(keys), halves(values)
        return jnp.concatenate([key_mine, value_mine], axis=1), jnp.concatenate([key_other, value_other], axis=1)

    own_mine, own_other = packed(seg_keys, seg_values)
    root_mine, root_other = packed(root_keys, root_values)
    sent = jnp.concatenate([own_other, root_other], axis=0)
    queries, got = lax.optimization_barrier((queries, to_core(sent)))
    q_mine, q_other = halves(queries)
    own = jnp.concatenate([own_mine, got[:rows]], axis=0)
    root = jnp.concatenate([root_mine, got[rows:]], axis=0)
    run = functools.partial(attend, ny, rows, (expansion, root_offsets))
    steps = range(1, ny)

    def members(array, kind, dx=0, dy=0, flips=(0, 1), first=0):
        return tuple((array, first + i, (kind, dx, dy, flip)) for i, flip in enumerate(flips))

    def after(state, *values):
        *values, state[0] = lax.optimization_barrier((*values, state[0]))
        return values

    def hop(step, rows_held):
        pairs = [(i, (i - 1) % leaves) for i in range(leaves)]
        return lax.ppermute(rows_held, "leaf", pairs if step < leaves - 1 else pairs[1:])

    ahead = [own]
    if leaves > 1:
        ahead.append(hop(1, own))
    own, root, q_other = lax.optimization_barrier((own, root, q_other))
    q_pair = (q_mine, to_core(q_other))
    own_x, own_y = to_x(own), [to_y(own, step) for step in steps]
    root_x, root_y = to_x(root), [to_y(root, step) for step in steps]
    state = run([own, root], (members(0, "own") + members(1, "root"),), q_pair, None, False)

    def near(kind):
        groups = [members(0, kind, 1) + members(1, kind, 0, 1)]
        return groups + [members(step, kind, 0, step) for step in steps if step > 1]

    if leaves > 2:
        (held,) = fence(state, ahead[-1])
        ahead[-1] = held
        ahead.append(hop(2, held))
    own_x, *own_y = after(state, own_x, *own_y)
    own_far = [to_y(own_x, step) for step in steps]
    state = run([own_x, *own_y], tuple(near("own")), None, state, False)
    for step in range(3, leaves):
        (held,) = fence(state, ahead[-1])
        ahead[-1] = held
        ahead.append(hop(step, held))
    root_x, *root_y = after(state, root_x, *root_y)
    root_far = [to_y(root_x, step) for step in steps]
    groups = near("root")
    groups[0] += members(ny, "own", 1, 1)
    groups += [members(ny - 1 + step, "own", 1, step) for step in steps if step > 1]
    state = run([root_x, *root_y, *own_far], tuple(groups), None, state, False)

    parent_rows = pick(state, expansion, leaves, after(state, *ahead))
    (parent_rows,) = after(state, parent_rows)
    kin_x, kin_y = to_x(parent_rows), [to_y(parent_rows, step) for step in steps]
    groups = [members(0, "kin") + members(1, "root", 1, 1)]
    groups += [members(step, "root", 1, step) for step in steps if step > 1]
    state = run([parent_rows, *root_far], tuple(groups), None, state, False)

    (kin_x,) = after(state, kin_x)
    tops = [to_y(kin_x[:rows], step) for step in steps]
    lows = [to_x(array[rows:]) for array in kin_y]
    groups = [members(0, "kin") + members(1, "kin")] + [members(step, "kin") for step in steps if step > 1]
    state = run([kin_x, *kin_y], tuple(groups), None, state, False)
    groups = [members(i, "kin", flips=(0,)) + members(len(tops) + i, "kin", flips=(1,)) for i in range(len(tops))]
    out_mine, out_other = run([*tops, *lows], tuple(groups), None, state, True)
    return assemble(out_mine, to_core(out_other))


def solution(mesh):
    return jax.shard_map(
        on_device,
        mesh=mesh,
        in_specs=(
            P(("leaf", "ctx"), None),
            P(("leaf", "ctx"), None),
            P(("leaf", "ctx"), None),
            P("ctx", None),
            P("ctx", None),
            P(),
            P(),
        ),
        out_specs=P(("leaf", "ctx"), None),
        check_vma=False,
    )
```

```python
import functools
import math

import jax
import jax.numpy as jnp
from jax import lax
from jax.experimental import pallas as pl
from jax.experimental.pallas import tpu as pltpu
from jax.sharding import PartitionSpec as P

HQ = 64
KVH = 8
HD = 128
GW = HQ // KVH
HALF_KV = KVH // 2
NEG = -1e30
EXP_SCALE = math.log2(math.e) / math.sqrt(HD)
ROW_BLOCK = 256


def attend_kernel(ny, rows, arrays, groups, first, last, *refs):
    refs = list(refs)
    take = lambda count: [refs.pop(0) for _ in range(count)]
    exp_ref, off_ref = take(2)
    raw = take(2) if first else None
    key_refs = take(arrays)
    value_refs = take(arrays)
    head = pl.program_id(0)
    if not first:
        take(3)
    if last:
        outs = take(2)
    else:
        take(1)[0][...] = jnp.zeros((8, HD), jnp.float32)
    held, qs = take(2)
    stacked = GW * rows

    group = lax.axis_index("leaf")
    spot = lax.axis_index("ctx")
    core, chip = lax.rem(spot, 2), spot // 2
    chip_x, chip_y = lax.rem(chip, 2), chip // 2
    visible = off_ref[group]
    depth = exp_ref[1, group]

    def block_start(dx, dy, flip):
        x = lax.rem(chip_x + dx, 2)
        y = lax.rem(chip_y - dy + ny, ny)
        k = lax.rem(core + flip, 2)
        return ((y * 2 + x) * 2 + k) * rows

    if first:
        for s, q_ref in enumerate(raw):
            for g in range(GW):
                qs[head, s, g * rows : (g + 1) * rows, :] = q_ref[:, g * HD : (g + 1) * HD]

    def step(members, limits, masked, fresh):
        width = len(members) * rows
        cut = lambda refs: [refs[a][b * rows : (b + 1) * rows, :] for a, b, _ in members]
        keys = jnp.concatenate(cut(key_refs), axis=0)
        values = jnp.concatenate(cut(value_refs), axis=0)
        values = jnp.concatenate([values, jnp.ones_like(values)], axis=1)
        size = min(ROW_BLOCK, stacked)
        todo = [(s, slice(base, base + size)) for s in range(2) for base in range(0, stacked, size)]

        def score(s, here):
            return lax.dot_general(
                qs[head, s, here, :], keys, (((1,), (1,)), ((), ())), preferred_element_type=jnp.float32
            )

        def bias_of(s):
            column = lax.broadcasted_iota(jnp.int32, (rows, rows), 1)
            line = lax.broadcasted_iota(jnp.int32, (rows, rows), 0)
            allowed = []
            for (_, _, block), limit in zip(members, limits[s]):
                ahead = column - line if block[0] == "own" else column
                allowed.append(jnp.where(ahead < limit, 0.0, NEG))
            return jnp.concatenate(allowed, axis=1)

        following = score(*todo[0])
        for at, (s, here) in enumerate(todo):
            scores = following
            if at + 1 < len(todo):
                following = score(*todo[at + 1])
            if masked:
                bias = bias_of(s)
                scores = scores + jnp.concatenate([bias] * (size // rows), axis=0)
            new = jnp.max(scores, axis=1, keepdims=True)
            if fresh:
                new = jnp.broadcast_to(new, (size, HD))
            else:
                old = held[head, s, here, 2 * HD :]
                new = jnp.maximum(old, new)
            weights = jnp.exp2((scores - jnp.concatenate([new] * (width // HD), axis=1)) * EXP_SCALE)
            update = jnp.dot(weights.astype(jnp.bfloat16), values, preferred_element_type=jnp.float32)
            if fresh:
                held[head, s, here, : 2 * HD] = update
            else:
                shrink = jnp.exp2((old - new) * EXP_SCALE)
                before = held[head, s, here, : 2 * HD] * jnp.concatenate([shrink, shrink], axis=1)
                held[head, s, here, : 2 * HD] = before + update
            held[head, s, here, 2 * HD :] = new

    for number, members in enumerate(groups):
        limits = []
        full, some = jnp.bool_(True), jnp.bool_(False)
        for s in range(2):
            first_row = block_start(0, 0, s)
            limits.append([])
            for _, _, (kind, dx, dy, flip) in members:
                if kind == "root":
                    limit = visible - block_start(dx, dy, flip)
                    some_here = limit > 0
                elif kind == "own":
                    limit = first_row - block_start(dx, dy, flip) + 1
                    some_here = limit + rows - 1 > 0
                else:
                    limit = jnp.where(depth > 0, rows, 0)
                    some_here = limit > 0
                limits[s].append(limit)
                full = full & (limit >= rows)
                some = some | some_here
        kinds = {block[0] for _, _, block in members}
        if first and number == 0:
            step(members, limits, True, True)
            continue
        pl.when(full)(functools.partial(step, members, limits, False, False))
        if kinds != {"kin"}:
            pl.when(jnp.logical_not(full) & some)(functools.partial(step, members, limits, True, False))

    if last:
        for s in range(2):
            for g in range(GW):
                here = slice(g * rows, (g + 1) * rows)
                done = held[head, s, here, :HD] / held[head, s, here, HD : 2 * HD]
                outs[s][:, g * HD : (g + 1) * HD] = done.astype(jnp.bfloat16)


WHOLE = pl.BlockSpec(memory_space=pltpu.VMEM)


def in_vmem(array):
    return pltpu.with_memory_space_constraint(array, pltpu.VMEM)


def fence(state, *values):
    mark, held, prepared = state
    *values, mark = lax.optimization_barrier((*values, mark))

    def kernel(mark_ref, *refs):
        refs[2][...] = mark_ref[...]

    state[:] = pl.pallas_call(
        kernel,
        in_specs=[WHOLE] * 3,
        out_specs=[WHOLE] * 3,
        out_shape=[
            jax.ShapeDtypeStruct(mark.shape, mark.dtype),
            pltpu.VMEM(held.shape, held.dtype),
            pltpu.VMEM(prepared.shape, prepared.dtype),
        ],
        input_output_aliases={1: 1, 2: 2},
        compiler_params=pltpu.CompilerParams(vmem_limit_bytes=4 * 2**20),
    )(mark, in_vmem(held), in_vmem(prepared))
    return values


def pick(state, table, leaves, arrays):
    mark, held, prepared = state
    count = len(arrays)

    def kernel(table_ref, mark_ref, *refs):
        out_ref, mark_out_ref, _, _, sem = refs[count + 2 :]
        group = lax.axis_index("leaf")
        parent = table_ref[0, group]
        mark_out_ref[...] = mark_ref[...]
        for ahead, ref in enumerate(refs[:count]):

            @pl.when(parent == lax.rem(group + ahead, leaves))
            def _():
                copy = pltpu.make_async_copy(ref, out_ref, sem)
                copy.start()
                copy.wait()

    anywhere = pl.BlockSpec(memory_space=pl.ANY)
    picked, *state[:] = pl.pallas_call(
        kernel,
        in_specs=[pl.BlockSpec(memory_space=pltpu.SMEM), WHOLE] + [anywhere] * count + [WHOLE] * 2,
        out_specs=[anywhere, WHOLE, WHOLE, WHOLE],
        out_shape=[
            jax.ShapeDtypeStruct(arrays[0].shape, arrays[0].dtype),
            jax.ShapeDtypeStruct(mark.shape, mark.dtype),
            pltpu.VMEM(held.shape, held.dtype),
            pltpu.VMEM(prepared.shape, prepared.dtype),
        ],
        scratch_shapes=[pltpu.SemaphoreType.DMA(())],
        input_output_aliases={count + 2: 2, count + 3: 3},
        compiler_params=pltpu.CompilerParams(vmem_limit_bytes=4 * 2**20),
    )(table, mark, *arrays, in_vmem(held), in_vmem(prepared))
    return picked


def assemble(mine, got):
    rows, half = mine.shape

    def kernel(mine_ref, got_ref, out_ref, sems):
        core = lax.rem(lax.axis_index("ctx"), 2)
        copies = []
        for i, (ref, place) in enumerate(((mine_ref, core), (got_ref, 1 - core))):
            columns = pl.ds(pl.multiple_of(place * half, half), half)
            copies.append(pltpu.make_async_copy(ref, out_ref.at[:, columns], sems.at[i]))
            copies[i].start()
        for copy in copies:
            copy.wait()

    anywhere = pl.BlockSpec(memory_space=pl.ANY)
    return pl.pallas_call(
        kernel,
        in_specs=[anywhere] * 2,
        out_specs=anywhere,
        out_shape=jax.ShapeDtypeStruct((rows, 2 * half), mine.dtype),
        scratch_shapes=[pltpu.SemaphoreType.DMA((2,))],
        compiler_params=pltpu.CompilerParams(vmem_limit_bytes=4 * 2**20),
    )(mine, got)


def attend(ny, rows, tables, arrays, groups, queries, state, last):
    stacked = GW * rows
    first = state is None
    smem = pl.BlockSpec(memory_space=pltpu.SMEM)
    row_spec = pl.BlockSpec((rows, GW * HD), lambda h: (0, h))
    operands = [*tables]
    specs = [smem, smem]
    if first:
        operands += queries
        specs += [row_spec, row_spec]
    else:
        mark, state, prepared = state
    for shift in (0, HALF_KV):
        for array in arrays:
            operands.append(array)
            specs.append(pl.BlockSpec((array.shape[0], HD), functools.partial(lambda s, h: (0, s + h), shift)))
    aliases = {}
    if last:
        out_shape = [jax.ShapeDtypeStruct((rows, HALF_KV * GW * HD), jnp.bfloat16)] * 2
        out_specs = [row_spec, row_spec]
    else:
        out_shape = [jax.ShapeDtypeStruct((8, HD), jnp.float32)]
        out_specs = [pl.BlockSpec((8, HD), lambda h: (0, 0))]
    if not first:
        aliases = {len(operands) + 1 + i: len(out_shape) + i for i in range(2)}
        operands += [mark, in_vmem(state), in_vmem(prepared)]
        specs += [pl.BlockSpec(memory_space=pl.ANY), WHOLE, WHOLE]
    out_shape.append(pltpu.VMEM((HALF_KV, 2, stacked, 3 * HD), jnp.float32))
    out_shape.append(pltpu.VMEM((HALF_KV, 2, stacked, HD), jnp.bfloat16))
    out_specs += [WHOLE, WHOLE]
    scores = HALF_KV * 2 * stacked * rows * sum(len(members) for members in groups)
    out = pl.pallas_call(
        functools.partial(attend_kernel, ny, rows, len(arrays), groups, first, last),
        grid=(HALF_KV,),
        in_specs=specs,
        out_specs=out_specs,
        out_shape=out_shape,
        input_output_aliases=aliases,
        compiler_params=pltpu.CompilerParams(vmem_limit_bytes=24 * 2**20),
        cost_estimate=pl.CostEstimate(flops=8 * scores * HD, bytes_accessed=4 * 2**20, transcendentals=scores),
    )(*operands)
    return out[:2] if last else list(out)


def on_device(queries, seg_keys, seg_values, root_keys, root_values, expansion, root_offsets):
    leaves, spots = lax.axis_size("leaf"), lax.axis_size("ctx")
    ny = spots // 4
    rows = queries.shape[0]
    group = lax.axis_index("leaf")
    core = lax.rem(lax.axis_index("ctx"), 2)

    def halves(array):
        half = array.shape[1] // 2
        return (
            lax.dynamic_slice_in_dim(array, core * half, half, 1),
            lax.dynamic_slice_in_dim(array, (1 - core) * half, half, 1),
        )

    def index(x, y, k):
        return ((y % ny) * 2 + x % 2) * 2 + k % 2

    places = [(x, y, k) for y in range(ny) for x in range(2) for k in range(2)]

    def to_core(array):
        return lax.ppermute(array, "ctx", [(index(x, y, k), index(x, y, k + 1)) for x, y, k in places])

    def to_x(array):
        return lax.ppermute(array, "ctx", [(index(x, y, k), index(x + 1, y, k)) for x, y, k in places])

    def to_y(array, step):
        return lax.ppermute(array, "ctx", [(index(x, y, k), index(x, y + step, k)) for x, y, k in places])

    def packed(keys, values):
        (key_mine, key_other), (value_mine, value_other) = halves(keys), halves(values)
        return jnp.concatenate([key_mine, value_mine], axis=1), jnp.concatenate([key_other, value_other], axis=1)

    own_mine, own_other = packed(seg_keys, seg_values)
    root_mine, root_other = packed(root_keys, root_values)
    sent = jnp.concatenate([own_other, root_other], axis=0)
    queries, got = lax.optimization_barrier((queries, to_core(sent)))
    q_mine, q_other = halves(queries)
    own = jnp.concatenate([own_mine, got[:rows]], axis=0)
    root = jnp.concatenate([root_mine, got[rows:]], axis=0)
    run = functools.partial(attend, ny, rows, (expansion, root_offsets))
    steps = range(1, ny)

    def members(array, kind, dx=0, dy=0, flips=(0, 1), first=0):
        return tuple((array, first + i, (kind, dx, dy, flip)) for i, flip in enumerate(flips))

    def after(state, *values):
        *values, state[0] = lax.optimization_barrier((*values, state[0]))
        return values

    def hop(step, rows_held):
        pairs = [(i, (i - 1) % leaves) for i in range(leaves)]
        return lax.ppermute(rows_held, "leaf", pairs if step < leaves - 1 else pairs[1:])

    ahead = [own]
    if leaves > 1:
        ahead.append(hop(1, own))
    own, root, q_other = lax.optimization_barrier((own, root, q_other))
    q_pair = (q_mine, to_core(q_other))
    own_x, own_y = to_x(own), [to_y(own, step) for step in steps]
    root_x, root_y = to_x(root), [to_y(root, step) for step in steps]
    state = run([own, root], (members(0, "own") + members(1, "root"),), q_pair, None, False)

    def near(kind):
        groups = [members(0, kind, 1) + members(1, kind, 0, 1)]
        return groups + [members(step, kind, 0, step) for step in steps if step > 1]

    if leaves > 2:
        (held,) = fence(state, ahead[-1])
        ahead[-1] = held
        ahead.append(hop(2, held))
    own_x, *own_y = after(state, own_x, *own_y)
    state = run([own_x, *own_y], tuple(near("own")), None, state, False)
    for step in range(3, leaves):
        (held,) = fence(state, ahead[-1])
        ahead[-1] = held
        ahead.append(hop(step, held))
    own_x, root_x, *root_y = after(state, own_x, root_x, *root_y)
    own_far = [to_y(own_x, step) for step in steps]
    root_far = [to_x(array) for array in root_y]
    state = run([root_x, *root_y], tuple(near("root")), None, state, False)

    parent_rows = pick(state, expansion, leaves, after(state, *ahead))
    (parent_rows,) = after(state, parent_rows)
    kin_x, kin_y = to_x(parent_rows), [to_y(parent_rows, step) for step in steps]
    groups = [members(i, "own", 1, i + 1) + members(ny - 1 + i, "root", 1, i + 1) for i in range(ny - 1)]
    groups[0] += members(2 * ny - 2, "kin")
    state = run([*own_far, *root_far, parent_rows], tuple(groups), None, state, False)

    (kin_x,) = after(state, kin_x)
    tops = [to_y(kin_x[:rows], step) for step in steps]
    lows = [to_x(array[rows:]) for array in kin_y]
    groups = [members(0, "kin") + members(1, "kin")] + [members(step, "kin") for step in steps if step > 1]
    state = run([kin_x, *kin_y], tuple(groups), None, state, False)
    groups = [members(i, "kin", flips=(0,)) + members(len(tops) + i, "kin", flips=(1,)) for i in range(len(tops))]
    out_mine, out_other = run([*tops, *lows], tuple(groups), None, state, True)
    return assemble(out_mine, to_core(out_other))


def solution(mesh):
    return jax.shard_map(
        on_device,
        mesh=mesh,
        in_specs=(
            P(("leaf", "ctx"), None),
            P(("leaf", "ctx"), None),
            P(("leaf", "ctx"), None),
            P("ctx", None),
            P("ctx", None),
            P(),
            P(),
        ),
        out_specs=P(("leaf", "ctx"), None),
        check_vma=False,
    )
```

```python
import functools
import math

import jax
import jax.numpy as jnp
from jax import lax
from jax.experimental import pallas as pl
from jax.experimental.pallas import tpu as pltpu
from jax.sharding import PartitionSpec as P

HQ = 64
KVH = 8
HD = 128
GW = HQ // KVH
HALF_KV = KVH // 2
NEG = -1e30
EXP_SCALE = math.log2(math.e) / math.sqrt(HD)
ROW_BLOCK = 128


def attend_kernel(ny, rows, arrays, groups, first, last, *refs):
    refs = list(refs)
    take = lambda count: [refs.pop(0) for _ in range(count)]
    exp_ref, off_ref = take(2)
    raw = take(2) if first else None
    key_refs = take(arrays)
    value_refs = take(arrays)
    head = pl.program_id(0)
    if not first:
        take(3)
    if last:
        outs = take(2)
    else:
        take(1)[0][...] = jnp.zeros((8, HD), jnp.float32)
    held, qs = take(2)
    stacked = GW * rows

    group = lax.axis_index("leaf")
    spot = lax.axis_index("ctx")
    core, chip = lax.rem(spot, 2), spot // 2
    chip_x, chip_y = lax.rem(chip, 2), chip // 2
    visible = off_ref[group]
    depth = exp_ref[1, group]

    def block_start(dx, dy, flip):
        x = lax.rem(chip_x + dx, 2)
        y = lax.rem(chip_y - dy + ny, ny)
        k = lax.rem(core + flip, 2)
        return ((y * 2 + x) * 2 + k) * rows

    if first:
        for s, q_ref in enumerate(raw):
            for g in range(GW):
                qs[head, s, g * rows : (g + 1) * rows, :] = q_ref[:, g * HD : (g + 1) * HD]

    def step(members, limits, masked, fresh):
        width = len(members) * rows
        cut = lambda refs: [refs[a][b * rows : (b + 1) * rows, :] for a, b, _ in members]
        keys = jnp.concatenate(cut(key_refs), axis=0)
        values = jnp.concatenate(cut(value_refs), axis=0)
        values = jnp.concatenate([values, jnp.ones_like(values)], axis=1)
        size = min(ROW_BLOCK, stacked)
        todo = [(s, slice(base, base + size)) for s in range(2) for base in range(0, stacked, size)]

        def score(s, here):
            return lax.dot_general(
                qs[head, s, here, :], keys, (((1,), (1,)), ((), ())), preferred_element_type=jnp.float32
            )

        def bias_of(s):
            column = lax.broadcasted_iota(jnp.int32, (rows, rows), 1)
            line = lax.broadcasted_iota(jnp.int32, (rows, rows), 0)
            allowed = []
            for (_, _, block), limit in zip(members, limits[s]):
                ahead = column - line if block[0] == "own" else column
                allowed.append(jnp.where(ahead < limit, 0.0, NEG))
            return jnp.concatenate(allowed, axis=1)

        following = score(*todo[0])
        for at, (s, here) in enumerate(todo):
            scores = following
            if at + 1 < len(todo):
                following = score(*todo[at + 1])
            if masked:
                bias = bias_of(s)
                scores = scores + jnp.concatenate([bias] * (size // rows), axis=0)
            new = jnp.max(scores, axis=1, keepdims=True)
            if fresh:
                new = jnp.broadcast_to(new, (size, HD))
            else:
                old = held[head, s, here, 2 * HD :]
                new = jnp.maximum(old, new)
            weights = jnp.exp2((scores - jnp.concatenate([new] * (width // HD), axis=1)) * EXP_SCALE)
            update = jnp.dot(weights.astype(jnp.bfloat16), values, preferred_element_type=jnp.float32)
            if fresh:
                held[head, s, here, : 2 * HD] = update
            else:
                shrink = jnp.exp2((old - new) * EXP_SCALE)
                before = held[head, s, here, : 2 * HD] * jnp.concatenate([shrink, shrink], axis=1)
                held[head, s, here, : 2 * HD] = before + update
            held[head, s, here, 2 * HD :] = new

    for number, members in enumerate(groups):
        limits = []
        full, some = jnp.bool_(True), jnp.bool_(False)
        for s in range(2):
            first_row = block_start(0, 0, s)
            limits.append([])
            for _, _, (kind, dx, dy, flip) in members:
                if kind == "root":
                    limit = visible - block_start(dx, dy, flip)
                    some_here = limit > 0
                elif kind == "own":
                    limit = first_row - block_start(dx, dy, flip) + 1
                    some_here = limit + rows - 1 > 0
                else:
                    limit = jnp.where(depth > 0, rows, 0)
                    some_here = limit > 0
                limits[s].append(limit)
                full = full & (limit >= rows)
                some = some | some_here
        kinds = {block[0] for _, _, block in members}
        if first and number == 0:
            step(members, limits, True, True)
            continue
        pl.when(full)(functools.partial(step, members, limits, False, False))
        if kinds != {"kin"}:
            pl.when(jnp.logical_not(full) & some)(functools.partial(step, members, limits, True, False))

    if last:
        for s in range(2):
            for g in range(GW):
                here = slice(g * rows, (g + 1) * rows)
                done = held[head, s, here, :HD] / held[head, s, here, HD : 2 * HD]
                outs[s][:, g * HD : (g + 1) * HD] = done.astype(jnp.bfloat16)


WHOLE = pl.BlockSpec(memory_space=pltpu.VMEM)


def in_vmem(array):
    return pltpu.with_memory_space_constraint(array, pltpu.VMEM)


def fence(state, *values):
    mark, held, prepared = state
    *values, mark = lax.optimization_barrier((*values, mark))

    def kernel(mark_ref, *refs):
        refs[2][...] = mark_ref[...]

    state[:] = pl.pallas_call(
        kernel,
        in_specs=[WHOLE] * 3,
        out_specs=[WHOLE] * 3,
        out_shape=[
            jax.ShapeDtypeStruct(mark.shape, mark.dtype),
            pltpu.VMEM(held.shape, held.dtype),
            pltpu.VMEM(prepared.shape, prepared.dtype),
        ],
        input_output_aliases={1: 1, 2: 2},
        compiler_params=pltpu.CompilerParams(vmem_limit_bytes=4 * 2**20),
    )(mark, in_vmem(held), in_vmem(prepared))
    return values


def pick(state, table, choose, arrays):
    mark, held, prepared = state
    count = len(arrays)

    def kernel(table_ref, mark_ref, *refs):
        out_ref, mark_out_ref, _, _, sem = refs[count + 2 :]
        mark_out_ref[...] = mark_ref[...]
        chosen = choose(table_ref, lax.axis_index("leaf"))
        for i, ref in enumerate(refs[:count]):

            @pl.when(chosen == i)
            def _():
                copy = pltpu.make_async_copy(ref, out_ref, sem)
                copy.start()
                copy.wait()

    anywhere = pl.BlockSpec(memory_space=pl.ANY)
    picked, *state[:] = pl.pallas_call(
        kernel,
        in_specs=[pl.BlockSpec(memory_space=pltpu.SMEM), WHOLE] + [anywhere] * count + [WHOLE] * 2,
        out_specs=[anywhere, WHOLE, WHOLE, WHOLE],
        out_shape=[
            jax.ShapeDtypeStruct(arrays[0].shape, arrays[0].dtype),
            jax.ShapeDtypeStruct(mark.shape, mark.dtype),
            pltpu.VMEM(held.shape, held.dtype),
            pltpu.VMEM(prepared.shape, prepared.dtype),
        ],
        scratch_shapes=[pltpu.SemaphoreType.DMA(())],
        input_output_aliases={count + 2: 2, count + 3: 3},
        compiler_params=pltpu.CompilerParams(vmem_limit_bytes=4 * 2**20),
    )(table, mark, *arrays, in_vmem(held), in_vmem(prepared))
    return picked


def pack(*arrays):
    rows, width = arrays[0].shape
    half = width // 2

    def kernel(*refs):
        *in_refs, mine_ref, other_ref, sems = refs
        core = lax.rem(lax.axis_index("ctx"), 2)
        copies = []
        for out_ref, place in ((other_ref, 1 - core), (mine_ref, core)):
            columns = pl.ds(pl.multiple_of(place * half, half), half)
            for i, ref in enumerate(in_refs):
                target = out_ref.at[pl.ds(i // 2 * rows, rows), pl.ds(i % 2 * half, half)]
                copies.append(pltpu.make_async_copy(ref.at[:, columns], target, sems.at[len(copies)]))
        for copy in copies:
            copy.start()
        for copy in copies:
            copy.wait()

    anywhere = pl.BlockSpec(memory_space=pl.ANY)
    packed = jax.ShapeDtypeStruct((len(arrays) // 2 * rows, width), arrays[0].dtype)
    return pl.pallas_call(
        kernel,
        in_specs=[anywhere] * len(arrays),
        out_specs=[anywhere] * 2,
        out_shape=[packed] * 2,
        scratch_shapes=[pltpu.SemaphoreType.DMA((2 * len(arrays),))],
        compiler_params=pltpu.CompilerParams(vmem_limit_bytes=4 * 2**20),
    )(*(pltpu.with_memory_space_constraint(array, pltpu.HBM) for array in arrays))


def assemble(mine, got):
    rows, half = mine.shape

    def kernel(mine_ref, got_ref, out_ref, sems):
        core = lax.rem(lax.axis_index("ctx"), 2)
        copies = []
        for i, (ref, place) in enumerate(((mine_ref, core), (got_ref, 1 - core))):
            columns = pl.ds(pl.multiple_of(place * half, half), half)
            copies.append(pltpu.make_async_copy(ref, out_ref.at[:, columns], sems.at[i]))
            copies[i].start()
        for copy in copies:
            copy.wait()

    anywhere = pl.BlockSpec(memory_space=pl.ANY)
    return pl.pallas_call(
        kernel,
        in_specs=[anywhere] * 2,
        out_specs=anywhere,
        out_shape=jax.ShapeDtypeStruct((rows, 2 * half), mine.dtype),
        scratch_shapes=[pltpu.SemaphoreType.DMA((2,))],
        compiler_params=pltpu.CompilerParams(vmem_limit_bytes=4 * 2**20),
    )(mine, got)


def attend(ny, rows, tables, arrays, groups, queries, state, last):
    stacked = GW * rows
    first = state is None
    smem = pl.BlockSpec(memory_space=pltpu.SMEM)
    row_spec = pl.BlockSpec((rows, GW * HD), lambda h: (0, h))
    operands = [*tables]
    specs = [smem, smem]
    if first:
        operands += queries
        specs += [row_spec, row_spec]
    else:
        mark, state, prepared = state
    for shift in (0, HALF_KV):
        for array in arrays:
            operands.append(array)
            specs.append(pl.BlockSpec((array.shape[0], HD), functools.partial(lambda s, h: (0, s + h), shift)))
    aliases = {}
    if last:
        out_shape = [jax.ShapeDtypeStruct((rows, HALF_KV * GW * HD), jnp.bfloat16)] * 2
        out_specs = [row_spec, row_spec]
    else:
        out_shape = [jax.ShapeDtypeStruct((8, HD), jnp.float32)]
        out_specs = [pl.BlockSpec((8, HD), lambda h: (0, 0))]
    if not first:
        aliases = {len(operands) + 1 + i: len(out_shape) + i for i in range(2)}
        operands += [mark, in_vmem(state), in_vmem(prepared)]
        specs += [pl.BlockSpec(memory_space=pl.ANY), WHOLE, WHOLE]
    out_shape.append(pltpu.VMEM((HALF_KV, 2, stacked, 3 * HD), jnp.float32))
    out_shape.append(pltpu.VMEM((HALF_KV, 2, stacked, HD), jnp.bfloat16))
    out_specs += [WHOLE, WHOLE]
    scores = HALF_KV * 2 * stacked * rows * sum(len(members) for members in groups)
    out = pl.pallas_call(
        functools.partial(attend_kernel, ny, rows, len(arrays), groups, first, last),
        grid=(HALF_KV,),
        in_specs=specs,
        out_specs=out_specs,
        out_shape=out_shape,
        input_output_aliases=aliases,
        compiler_params=pltpu.CompilerParams(vmem_limit_bytes=24 * 2**20),
        cost_estimate=pl.CostEstimate(flops=8 * scores * HD, bytes_accessed=4 * 2**20, transcendentals=scores),
    )(*operands)
    return out[:2] if last else list(out)


def on_device(queries, seg_keys, seg_values, root_keys, root_values, expansion, root_offsets):
    leaves, spots = lax.axis_size("leaf"), lax.axis_size("ctx")
    ny = spots // 4
    rows = queries.shape[0]
    group = lax.axis_index("leaf")
    core = lax.rem(lax.axis_index("ctx"), 2)

    def halves(array):
        half = array.shape[1] // 2
        return (
            lax.dynamic_slice_in_dim(array, core * half, half, 1),
            lax.dynamic_slice_in_dim(array, (1 - core) * half, half, 1),
        )

    def index(x, y, k):
        return ((y % ny) * 2 + x % 2) * 2 + k % 2

    places = [(x, y, k) for y in range(ny) for x in range(2) for k in range(2)]

    def to_core(array):
        return lax.ppermute(array, "ctx", [(index(x, y, k), index(x, y, k + 1)) for x, y, k in places])

    def to_x(array):
        return lax.ppermute(array, "ctx", [(index(x, y, k), index(x + 1, y, k)) for x, y, k in places])

    def to_y(array, step):
        return lax.ppermute(array, "ctx", [(index(x, y, k), index(x, y + step, k)) for x, y, k in places])

    mine, sent = pack(seg_keys, seg_values, root_keys, root_values)
    queries, got = lax.optimization_barrier((queries, to_core(sent)))
    q_mine, q_other = halves(queries)
    own = jnp.concatenate([mine[:rows], got[:rows]], axis=0)
    root = jnp.concatenate([mine[rows:], got[rows:]], axis=0)
    run = functools.partial(attend, ny, rows, (expansion, root_offsets))
    steps = range(1, ny)

    def members(array, kind, dx=0, dy=0, flips=(0, 1), first=0):
        return tuple((array, first + i, (kind, dx, dy, flip)) for i, flip in enumerate(flips))

    def after(state, *values):
        *values, state[0] = lax.optimization_barrier((*values, state[0]))
        return values

    def hop(step, rows_held):
        pairs = [(i, (i - 1) % leaves) for i in range(leaves)]
        return lax.ppermute(rows_held, "leaf", pairs if step < leaves - 1 else pairs[1:])

    direct = leaves == 4
    ahead = [own]
    if direct:
        for pairs in (((1, 0), (2, 1), (3, 2)), ((0, 2), (3, 1)), ((0, 1), (1, 2))):
            ahead.append(lax.ppermute(own, "leaf", pairs))
    elif leaves > 1:
        ahead.append(hop(1, own))
    own, q_got = lax.optimization_barrier((own, to_core(q_other)))
    q_pair = (q_mine, q_got)
    own_x, own_y = to_x(own), [to_y(own, step) for step in steps]
    state = run([own, root], (members(0, "own") + members(1, "root"),), q_pair, None, False)

    (root,) = after(state, root)
    root_x, root_y = to_x(root), [to_y(root, step) for step in steps]

    def near(kind):
        groups = [members(0, kind, 1) + members(1, kind, 0, 1)]
        return groups + [members(step, kind, 0, step) for step in steps if step > 1]

    if leaves > 2 and not direct:
        (held,) = fence(state, ahead[-1])
        ahead[-1] = held
        ahead.append(hop(2, held))
    own_x, *own_y = after(state, own_x, *own_y)
    state = run([own_x, *own_y], tuple(near("own")), None, state, False)
    if direct:
        ahead = after(state, *ahead)
        relay = pick(state, expansion, lambda table, g: jnp.where(table[0, 0] == 3, 1, 0), ahead[1:3])
        ahead.append(lax.ppermute(relay, "leaf", [(1, 0)]))
    else:
        for step in range(3, leaves):
            (held,) = fence(state, ahead[-1])
            ahead[-1] = held
            ahead.append(hop(step, held))
    own_x, root_x, *root_y = after(state, own_x, root_x, *root_y)
    own_far = [to_y(own_x, step) for step in steps]
    root_far = [to_x(array) for array in root_y]
    state = run([root_x, *root_y], tuple(near("root")), None, state, False)

    def choose(table, g):
        offset = table[0, g] - g
        if not direct:
            return lax.rem(offset + leaves, leaves)
        far_one = jnp.where(g == 0, 4, 2)
        return jnp.where(offset == 0, 0, jnp.where(offset == 1, 1, jnp.where(offset == -1, 3, far_one)))

    parent_rows = pick(state, expansion, choose, after(state, *ahead))
    (parent_rows,) = after(state, parent_rows)
    kin_x, kin_y = to_x(parent_rows), [to_y(parent_rows, step) for step in steps]
    groups = [members(i, "own", 1, i + 1) + members(ny - 1 + i, "root", 1, i + 1) for i in range(ny - 1)]
    groups[0] += members(2 * ny - 2, "kin")
    state = run([*own_far, *root_far, parent_rows], tuple(groups), None, state, False)

    (kin_x,) = after(state, kin_x)
    tops = [to_y(kin_x[:rows], step) for step in steps]
    lows = [to_x(array[rows:]) for array in kin_y]
    groups = [members(0, "kin") + members(1, "kin")] + [members(step, "kin") for step in steps if step > 1]
    state = run([kin_x, *kin_y], tuple(groups), None, state, False)
    groups = [members(i, "kin", flips=(0,)) + members(len(tops) + i, "kin", flips=(1,)) for i in range(len(tops))]
    out_mine, out_other = run([*tops, *lows], tuple(groups), None, state, True)
    return assemble(out_mine, to_core(out_other))


def solution(mesh):
    return jax.shard_map(
        on_device,
        mesh=mesh,
        in_specs=(
            P(("leaf", "ctx"), None),
            P(("leaf", "ctx"), None),
            P(("leaf", "ctx"), None),
            P("ctx", None),
            P("ctx", None),
            P(),
            P(),
        ),
        out_specs=P(("leaf", "ctx"), None),
        check_vma=False,
    )
```

```python
import functools
import math

import jax
import jax.numpy as jnp
from jax import lax
from jax.experimental import pallas as pl
from jax.experimental.pallas import tpu as pltpu
from jax.sharding import PartitionSpec as P

HQ = 64
KVH = 8
HD = 128
GW = HQ // KVH
HALF_KV = KVH // 2
NEG = -1e30
EXP_SCALE = math.log2(math.e) / math.sqrt(HD)
ROW_BLOCK = 256
KEY_CHUNK = 256


def attend_kernel(ny, rows, arrays, groups, first, last, *refs):
    refs = list(refs)
    take = lambda count: [refs.pop(0) for _ in range(count)]
    exp_ref, off_ref = take(2)
    raw = take(2) if first else None
    key_refs = take(arrays)
    value_refs = take(arrays)
    head = pl.program_id(0)
    if not first:
        take(3)
    if last:
        outs = take(2)
    else:
        take(1)[0][...] = jnp.zeros((8, HD), jnp.float32)
    held, qs = take(2)
    stacked = GW * rows

    group = lax.axis_index("leaf")
    spot = lax.axis_index("ctx")
    core, chip = lax.rem(spot, 2), spot // 2
    chip_x, chip_y = lax.rem(chip, 2), chip // 2
    visible = off_ref[group]
    depth = exp_ref[1, group]

    def block_start(dx, dy, flip):
        x = lax.rem(chip_x + dx, 2)
        y = lax.rem(chip_y - dy + ny, ny)
        k = lax.rem(core + flip, 2)
        return ((y * 2 + x) * 2 + k) * rows

    if first:
        for s, q_ref in enumerate(raw):
            for g in range(GW):
                qs[head, s, g * rows : (g + 1) * rows, :] = q_ref[:, g * HD : (g + 1) * HD]

    def step(members, limits, masked, fresh):
        width = len(members) * rows
        cut = lambda refs: [refs[a][b * rows : (b + 1) * rows, :] for a, b, _ in members]
        keys = jnp.concatenate(cut(key_refs), axis=0)
        values = jnp.concatenate(cut(value_refs), axis=0)
        values = jnp.concatenate([values, jnp.ones_like(values)], axis=1)
        size = min(ROW_BLOCK, stacked)
        todo = [(s, slice(base, base + size)) for s in range(2) for base in range(0, stacked, size)]

        chunks = [slice(c, min(c + KEY_CHUNK, width)) for c in range(0, width, KEY_CHUNK)]
        biases = {}

        def bias_of(s):
            if s not in biases:
                column = lax.broadcasted_iota(jnp.int32, (rows, rows), 1)
                line = lax.broadcasted_iota(jnp.int32, (rows, rows), 0)
                allowed = []
                for (_, _, block), limit in zip(members, limits[s]):
                    ahead = column - line if block[0] == "own" else column
                    allowed.append(jnp.where(ahead < limit, 0.0, NEG))
                biases[s] = jnp.concatenate(allowed, axis=1)
            return biases[s]

        def score(item, chunk):
            s, here = item
            found = lax.dot_general(
                qs[head, s, here, :], keys[chunk], (((1,), (1,)), ((), ())), preferred_element_type=jnp.float32
            )
            if masked:
                found = found + jnp.concatenate([bias_of(s)[:, chunk]] * (size // rows), axis=0)
            return found

        def peak_of(scores):
            parts = [part[:, c : c + HD] for part in scores for c in range(0, part.shape[1], HD)]
            return jnp.max(functools.reduce(jnp.maximum, parts), axis=1, keepdims=True)

        scores = [score(todo[0], chunk) for chunk in chunks]
        peak = peak_of(scores)
        for at, (s, here) in enumerate(todo):
            if fresh:
                new = jnp.broadcast_to(peak, (size, HD))
            else:
                old = held[head, s, here, 2 * HD :]
                new = jnp.maximum(old, peak)
            following, weights = [], []
            for i, chunk in enumerate(chunks):
                if at + 1 < len(todo):
                    following.append(score(todo[at + 1], chunk))
                shifted = scores[i] - jnp.concatenate([new] * (scores[i].shape[1] // HD), axis=1)
                weights.append(jnp.exp2(shifted * EXP_SCALE).astype(jnp.bfloat16))
            update = jnp.dot(jnp.concatenate(weights, axis=1), values, preferred_element_type=jnp.float32)
            if following:
                scores, peak = following, peak_of(following)
            if fresh:
                held[head, s, here, : 2 * HD] = update
            else:
                shrink = jnp.exp2((old - new) * EXP_SCALE)
                before = held[head, s, here, : 2 * HD] * jnp.concatenate([shrink, shrink], axis=1)
                held[head, s, here, : 2 * HD] = before + update
            held[head, s, here, 2 * HD :] = new

    for number, members in enumerate(groups):
        limits = []
        full, some = jnp.bool_(True), jnp.bool_(False)
        for s in range(2):
            first_row = block_start(0, 0, s)
            limits.append([])
            for _, _, (kind, dx, dy, flip) in members:
                if kind == "root":
                    limit = visible - block_start(dx, dy, flip)
                    some_here = limit > 0
                elif kind == "own":
                    limit = first_row - block_start(dx, dy, flip) + 1
                    some_here = limit + rows - 1 > 0
                else:
                    limit = jnp.where(depth > 0, rows, 0)
                    some_here = limit > 0
                limits[s].append(limit)
                full = full & (limit >= rows)
                some = some | some_here
        kinds = {block[0] for _, _, block in members}
        if first and number == 0:
            step(members, limits, True, True)
            continue
        pl.when(full)(functools.partial(step, members, limits, False, False))
        if kinds != {"kin"}:
            pl.when(jnp.logical_not(full) & some)(functools.partial(step, members, limits, True, False))

    if last:
        for s in range(2):
            for g in range(GW):
                here = slice(g * rows, (g + 1) * rows)
                done = held[head, s, here, :HD] / held[head, s, here, HD : 2 * HD]
                outs[s][:, g * HD : (g + 1) * HD] = done.astype(jnp.bfloat16)


WHOLE = pl.BlockSpec(memory_space=pltpu.VMEM)


def in_vmem(array):
    return pltpu.with_memory_space_constraint(array, pltpu.VMEM)


def fence(state, *values):
    mark, held, prepared = state
    *values, mark = lax.optimization_barrier((*values, mark))

    def kernel(mark_ref, *refs):
        refs[2][...] = mark_ref[...]

    state[:] = pl.pallas_call(
        kernel,
        in_specs=[WHOLE] * 3,
        out_specs=[WHOLE] * 3,
        out_shape=[
            jax.ShapeDtypeStruct(mark.shape, mark.dtype),
            pltpu.VMEM(held.shape, held.dtype),
            pltpu.VMEM(prepared.shape, prepared.dtype),
        ],
        input_output_aliases={1: 1, 2: 2},
        compiler_params=pltpu.CompilerParams(vmem_limit_bytes=4 * 2**20),
    )(mark, in_vmem(held), in_vmem(prepared))
    return values


def pick(state, table, choose, arrays):
    mark, held, prepared = state
    count = len(arrays)

    def kernel(table_ref, mark_ref, *refs):
        out_ref, mark_out_ref, _, _, sem = refs[count + 2 :]
        mark_out_ref[...] = mark_ref[...]
        chosen = choose(table_ref, lax.axis_index("leaf"))
        for i, ref in enumerate(refs[:count]):

            @pl.when(chosen == i)
            def _():
                copy = pltpu.make_async_copy(ref, out_ref, sem)
                copy.start()
                copy.wait()

    anywhere = pl.BlockSpec(memory_space=pl.ANY)
    picked, *state[:] = pl.pallas_call(
        kernel,
        in_specs=[pl.BlockSpec(memory_space=pltpu.SMEM), WHOLE] + [anywhere] * count + [WHOLE] * 2,
        out_specs=[anywhere, WHOLE, WHOLE, WHOLE],
        out_shape=[
            jax.ShapeDtypeStruct(arrays[0].shape, arrays[0].dtype),
            jax.ShapeDtypeStruct(mark.shape, mark.dtype),
            pltpu.VMEM(held.shape, held.dtype),
            pltpu.VMEM(prepared.shape, prepared.dtype),
        ],
        scratch_shapes=[pltpu.SemaphoreType.DMA(())],
        input_output_aliases={count + 2: 2, count + 3: 3},
        compiler_params=pltpu.CompilerParams(vmem_limit_bytes=4 * 2**20),
    )(table, mark, *arrays, in_vmem(held), in_vmem(prepared))
    return picked


def pack(beside, *arrays):
    rows, width = arrays[0].shape
    half = width // 2

    def kernel(*refs):
        *in_refs, mine_ref, other_ref, sems = refs
        core = lax.rem(lax.axis_index("ctx"), 2)
        copies = []
        for out_ref, place in ((other_ref, 1 - core), (mine_ref, core)):
            columns = pl.ds(pl.multiple_of(place * half, half), half)
            for i, ref in enumerate(in_refs):
                target = out_ref.at[pl.ds(i // beside * rows, rows), pl.ds(i % beside * half, half)]
                copies.append(pltpu.make_async_copy(ref.at[:, columns], target, sems.at[len(copies)]))
        for copy in copies:
            copy.start()
        for copy in copies:
            copy.wait()

    anywhere = pl.BlockSpec(memory_space=pl.ANY)
    packed = jax.ShapeDtypeStruct((len(arrays) // beside * rows, beside * half), arrays[0].dtype)
    return pl.pallas_call(
        kernel,
        in_specs=[anywhere] * len(arrays),
        out_specs=[anywhere] * 2,
        out_shape=[packed] * 2,
        scratch_shapes=[pltpu.SemaphoreType.DMA((2 * len(arrays),))],
        compiler_params=pltpu.CompilerParams(vmem_limit_bytes=4 * 2**20),
    )(*(pltpu.with_memory_space_constraint(array, pltpu.HBM) for array in arrays))


def assemble(mine, got):
    rows, half = mine.shape

    def kernel(mine_ref, got_ref, out_ref, sems):
        core = lax.rem(lax.axis_index("ctx"), 2)
        copies = []
        for i, (ref, place) in enumerate(((mine_ref, core), (got_ref, 1 - core))):
            columns = pl.ds(pl.multiple_of(place * half, half), half)
            copies.append(pltpu.make_async_copy(ref, out_ref.at[:, columns], sems.at[i]))
            copies[i].start()
        for copy in copies:
            copy.wait()

    anywhere = pl.BlockSpec(memory_space=pl.ANY)
    return pl.pallas_call(
        kernel,
        in_specs=[anywhere] * 2,
        out_specs=anywhere,
        out_shape=jax.ShapeDtypeStruct((rows, 2 * half), mine.dtype),
        scratch_shapes=[pltpu.SemaphoreType.DMA((2,))],
        compiler_params=pltpu.CompilerParams(vmem_limit_bytes=4 * 2**20),
    )(mine, got)


def attend(ny, rows, tables, arrays, groups, queries, state, last):
    stacked = GW * rows
    first = state is None
    smem = pl.BlockSpec(memory_space=pltpu.SMEM)
    row_spec = pl.BlockSpec((rows, GW * HD), lambda h: (0, h))
    operands = [*tables]
    specs = [smem, smem]
    if first:
        operands += queries
        specs += [row_spec, row_spec]
    else:
        mark, state, prepared = state
    for shift in (0, HALF_KV):
        for array in arrays:
            operands.append(array)
            specs.append(pl.BlockSpec((array.shape[0], HD), functools.partial(lambda s, h: (0, s + h), shift)))
    aliases = {}
    if last:
        out_shape = [jax.ShapeDtypeStruct((rows, HALF_KV * GW * HD), jnp.bfloat16)] * 2
        out_specs = [row_spec, row_spec]
    else:
        out_shape = [jax.ShapeDtypeStruct((8, HD), jnp.float32)]
        out_specs = [pl.BlockSpec((8, HD), lambda h: (0, 0))]
    if not first:
        aliases = {len(operands) + 1 + i: len(out_shape) + i for i in range(2)}
        operands += [mark, in_vmem(state), in_vmem(prepared)]
        specs += [pl.BlockSpec(memory_space=pl.ANY), WHOLE, WHOLE]
    out_shape.append(pltpu.VMEM((HALF_KV, 2, stacked, 3 * HD), jnp.float32))
    out_shape.append(pltpu.VMEM((HALF_KV, 2, stacked, HD), jnp.bfloat16))
    out_specs += [WHOLE, WHOLE]
    scores = HALF_KV * 2 * stacked * rows * sum(len(members) for members in groups)
    out = pl.pallas_call(
        functools.partial(attend_kernel, ny, rows, len(arrays), groups, first, last),
        grid=(HALF_KV,),
        in_specs=specs,
        out_specs=out_specs,
        out_shape=out_shape,
        input_output_aliases=aliases,
        compiler_params=pltpu.CompilerParams(vmem_limit_bytes=24 * 2**20),
        cost_estimate=pl.CostEstimate(flops=8 * scores * HD, bytes_accessed=4 * 2**20, transcendentals=scores),
    )(*operands)
    return out[:2] if last else list(out)


def on_device(queries, seg_keys, seg_values, root_keys, root_values, expansion, root_offsets):
    leaves, spots = lax.axis_size("leaf"), lax.axis_size("ctx")
    ny = spots // 4
    rows = queries.shape[0]
    group = lax.axis_index("leaf")
    def index(x, y, k):
        return ((y % ny) * 2 + x % 2) * 2 + k % 2

    places = [(x, y, k) for y in range(ny) for x in range(2) for k in range(2)]

    def to_core(array):
        return lax.ppermute(array, "ctx", [(index(x, y, k), index(x, y, k + 1)) for x, y, k in places])

    def to_x(array):
        return lax.ppermute(array, "ctx", [(index(x, y, k), index(x + 1, y, k)) for x, y, k in places])

    def to_y(array, step):
        return lax.ppermute(array, "ctx", [(index(x, y, k), index(x, y + step, k)) for x, y, k in places])

    mine, sent = pack(2, seg_keys, seg_values, root_keys, root_values)
    queries, sent = lax.optimization_barrier((queries, sent))
    q_mine, q_other = pack(1, queries)
    q_other, got = lax.optimization_barrier((q_other, to_core(sent)))
    own = jnp.concatenate([mine[:rows], got[:rows]], axis=0)
    root = jnp.concatenate([mine[rows:], got[rows:]], axis=0)
    run = functools.partial(attend, ny, rows, (expansion, root_offsets))
    steps = range(1, ny)

    def members(array, kind, dx=0, dy=0, flips=(0, 1), first=0):
        return tuple((array, first + i, (kind, dx, dy, flip)) for i, flip in enumerate(flips))

    def after(state, *values):
        *values, state[0] = lax.optimization_barrier((*values, state[0]))
        return values

    def hop(step, rows_held):
        pairs = [(i, (i - 1) % leaves) for i in range(leaves)]
        return lax.ppermute(rows_held, "leaf", pairs if step < leaves - 1 else pairs[1:])

    own_x, own_y = to_x(own), [to_y(own, step) for step in steps]
    own, q_got = lax.optimization_barrier((own, to_core(q_other)))
    q_pair = (q_mine, q_got)
    direct = leaves == 4
    ahead = [own]
    if direct:
        for pairs in (((1, 0), (2, 1), (3, 2)), ((0, 2), (3, 1)), ((0, 1), (1, 2))):
            ahead.append(lax.ppermute(own, "leaf", pairs))
    elif leaves > 1:
        ahead.append(hop(1, own))
    state = run([own, root], (members(0, "own") + members(1, "root"),), q_pair, None, False)

    (root,) = after(state, root)
    root_x, root_y = to_x(root), [to_y(root, step) for step in steps]

    def near(kind):
        groups = [members(0, kind, 1) + members(1, kind, 0, 1)]
        return groups + [members(step, kind, 0, step) for step in steps if step > 1]

    if leaves > 2 and not direct:
        (held,) = fence(state, ahead[-1])
        ahead[-1] = held
        ahead.append(hop(2, held))
    own_x, *own_y = after(state, own_x, *own_y)
    state = run([own_x, *own_y], tuple(near("own")), None, state, False)
    if direct:
        ahead = after(state, *ahead)
        relay = pick(state, expansion, lambda table, g: jnp.where(table[0, 0] == 3, 1, 0), ahead[1:3])
        ahead.append(lax.ppermute(relay, "leaf", [(1, 0)]))
    else:
        for step in range(3, leaves):
            (held,) = fence(state, ahead[-1])
            ahead[-1] = held
            ahead.append(hop(step, held))
    own_x, root_x, *root_y = after(state, own_x, root_x, *root_y)
    own_far = [to_y(own_x, step) for step in steps]
    root_far = [to_x(array) for array in root_y]
    state = run([root_x, *root_y], tuple(near("root")), None, state, False)

    def choose(table, g):
        offset = table[0, g] - g
        if not direct:
            return lax.rem(offset + leaves, leaves)
        far_one = jnp.where(g == 0, 4, 2)
        return jnp.where(offset == 0, 0, jnp.where(offset == 1, 1, jnp.where(offset == -1, 3, far_one)))

    parent_rows = pick(state, expansion, choose, after(state, *ahead))
    (parent_rows,) = after(state, parent_rows)
    kin_x, kin_y = to_x(parent_rows), [to_y(parent_rows, step) for step in steps]
    groups = [members(i, "own", 1, i + 1) + members(ny - 1 + i, "root", 1, i + 1) for i in range(ny - 1)]
    groups[0] += members(2 * ny - 2, "kin")
    state = run([*own_far, *root_far, parent_rows], tuple(groups), None, state, False)

    (kin_x,) = after(state, kin_x)
    tops = [to_y(kin_x[:rows], step) for step in steps]
    lows = [to_x(array[rows:]) for array in kin_y]
    groups = [members(0, "kin") + members(1, "kin")] + [members(step, "kin") for step in steps if step > 1]
    state = run([kin_x, *kin_y], tuple(groups), None, state, False)
    groups = [members(i, "kin", flips=(0,)) + members(len(tops) + i, "kin", flips=(1,)) for i in range(len(tops))]
    out_mine, out_other = run([*tops, *lows], tuple(groups), None, state, True)
    return assemble(out_mine, to_core(out_other))


def solution(mesh):
    return jax.shard_map(
        on_device,
        mesh=mesh,
        in_specs=(
            P(("leaf", "ctx"), None),
            P(("leaf", "ctx"), None),
            P(("leaf", "ctx"), None),
            P("ctx", None),
            P("ctx", None),
            P(),
            P(),
        ),
        out_specs=P(("leaf", "ctx"), None),
        check_vma=False,
    )
```

```python
import functools
import math

import jax
import jax.numpy as jnp
from jax import lax
from jax.experimental import pallas as pl
from jax.experimental.pallas import tpu as pltpu
from jax.sharding import PartitionSpec as P

HQ = 64
KVH = 8
HD = 128
GW = HQ // KVH
HALF_KV = KVH // 2
NEG = -1e30
EXP_SCALE = math.log2(math.e) / math.sqrt(HD)
ROW_BLOCK = 256
KEY_CHUNK = 256


def attend_kernel(ny, rows, arrays, groups, first, last, *refs):
    refs = list(refs)
    take = lambda count: [refs.pop(0) for _ in range(count)]
    exp_ref, off_ref = take(2)
    raw = take(2) if first else None
    key_refs = take(arrays)
    value_refs = take(arrays)
    head = pl.program_id(0)
    if not first:
        take(3)
    if last:
        outs = take(2)
    else:
        take(1)[0][...] = jnp.zeros((8, HD), jnp.float32)
    held, qs = take(2)
    stacked = GW * rows

    group = lax.axis_index("leaf")
    spot = lax.axis_index("ctx")
    core, chip = lax.rem(spot, 2), spot // 2
    chip_x, chip_y = lax.rem(chip, 2), chip // 2
    visible = off_ref[group]
    depth = exp_ref[1, group]

    def block_start(dx, dy, flip):
        x = lax.rem(chip_x + dx, 2)
        y = lax.rem(chip_y - dy + ny, ny)
        k = lax.rem(core + flip, 2)
        return ((y * 2 + x) * 2 + k) * rows

    if first:
        for s, q_ref in enumerate(raw):
            for g in range(GW):
                qs[head, s, g * rows : (g + 1) * rows, :] = q_ref[:, g * HD : (g + 1) * HD]

    def step(members, limits, masked, fresh):
        width = len(members) * rows
        cut = lambda refs: [refs[a][b * rows : (b + 1) * rows, :] for a, b, _ in members]
        keys = jnp.concatenate(cut(key_refs), axis=0)
        values = jnp.concatenate(cut(value_refs), axis=0)
        values = jnp.concatenate([values, jnp.ones_like(values)], axis=1)
        size = min(ROW_BLOCK, stacked)
        todo = [(s, slice(base, base + size)) for s in range(2) for base in range(0, stacked, size)]

        chunks = [slice(c, min(c + KEY_CHUNK, width)) for c in range(0, width, KEY_CHUNK)]
        biases = {}

        def bias_of(s):
            if s not in biases:
                column = lax.broadcasted_iota(jnp.int32, (rows, rows), 1)
                line = lax.broadcasted_iota(jnp.int32, (rows, rows), 0)
                allowed = []
                for (_, _, block), limit in zip(members, limits[s]):
                    ahead = column - line if block[0] == "own" else column
                    allowed.append(jnp.where(ahead < limit, 0.0, NEG))
                biases[s] = jnp.concatenate(allowed, axis=1)
            return biases[s]

        def score(item, chunk):
            s, here = item
            found = lax.dot_general(
                qs[head, s, here, :], keys[chunk], (((1,), (1,)), ((), ())), preferred_element_type=jnp.float32
            )
            if masked:
                found = found + jnp.concatenate([bias_of(s)[:, chunk]] * (size // rows), axis=0)
            return found

        def peak_of(scores):
            parts = [part[:, c : c + HD] for part in scores for c in range(0, part.shape[1], HD)]
            return jnp.max(functools.reduce(jnp.maximum, parts), axis=1, keepdims=True)

        scores = [score(todo[0], chunk) for chunk in chunks]
        peak = peak_of(scores)
        for at, (s, here) in enumerate(todo):
            if fresh:
                new = jnp.broadcast_to(peak, (size, HD))
            else:
                old = held[head, s, here, 2 * HD :]
                new = jnp.maximum(old, peak)
            following, weights = [], []
            for i, chunk in enumerate(chunks):
                if at + 1 < len(todo):
                    following.append(score(todo[at + 1], chunk))
                shifted = scores[i] - jnp.concatenate([new] * (scores[i].shape[1] // HD), axis=1)
                weights.append(jnp.exp2(shifted * EXP_SCALE).astype(jnp.bfloat16))
            update = jnp.dot(jnp.concatenate(weights, axis=1), values, preferred_element_type=jnp.float32)
            if following:
                scores, peak = following, peak_of(following)
            if fresh:
                held[head, s, here, : 2 * HD] = update
            else:
                shrink = jnp.exp2((old - new) * EXP_SCALE)
                before = held[head, s, here, : 2 * HD] * jnp.concatenate([shrink, shrink], axis=1)
                held[head, s, here, : 2 * HD] = before + update
            held[head, s, here, 2 * HD :] = new

    for number, members in enumerate(groups):
        limits = []
        full, some = jnp.bool_(True), jnp.bool_(False)
        for s in range(2):
            first_row = block_start(0, 0, s)
            limits.append([])
            for _, _, (kind, dx, dy, flip) in members:
                if kind == "root":
                    limit = visible - block_start(dx, dy, flip)
                    some_here = limit > 0
                elif kind == "own":
                    limit = first_row - block_start(dx, dy, flip) + 1
                    some_here = limit + rows - 1 > 0
                else:
                    limit = jnp.where(depth > 0, rows, 0)
                    some_here = limit > 0
                limits[s].append(limit)
                full = full & (limit >= rows)
                some = some | some_here
        kinds = {block[0] for _, _, block in members}
        if first and number == 0:
            step(members, limits, True, True)
            continue
        pl.when(full)(functools.partial(step, members, limits, False, False))
        if kinds != {"kin"}:
            pl.when(jnp.logical_not(full) & some)(functools.partial(step, members, limits, True, False))

    if last:
        for s in range(2):
            for g in range(GW):
                here = slice(g * rows, (g + 1) * rows)
                done = held[head, s, here, :HD] / held[head, s, here, HD : 2 * HD]
                outs[s][:, g * HD : (g + 1) * HD] = done.astype(jnp.bfloat16)


WHOLE = pl.BlockSpec(memory_space=pltpu.VMEM)


def in_vmem(array):
    return pltpu.with_memory_space_constraint(array, pltpu.VMEM)


def fence(state, *values):
    mark, held, prepared = state
    *values, mark = lax.optimization_barrier((*values, mark))

    def kernel(mark_ref, *refs):
        refs[2][...] = mark_ref[...]

    state[:] = pl.pallas_call(
        kernel,
        in_specs=[WHOLE] * 3,
        out_specs=[WHOLE] * 3,
        out_shape=[
            jax.ShapeDtypeStruct(mark.shape, mark.dtype),
            pltpu.VMEM(held.shape, held.dtype),
            pltpu.VMEM(prepared.shape, prepared.dtype),
        ],
        input_output_aliases={1: 1, 2: 2},
        compiler_params=pltpu.CompilerParams(vmem_limit_bytes=4 * 2**20),
    )(mark, in_vmem(held), in_vmem(prepared))
    return values


def pick(state, table, choose, arrays):
    mark, held, prepared = state
    count = len(arrays)

    def kernel(table_ref, mark_ref, *refs):
        out_ref, mark_out_ref, _, _, sem = refs[count + 2 :]
        mark_out_ref[...] = mark_ref[...]
        chosen = choose(table_ref, lax.axis_index("leaf"))
        for i, ref in enumerate(refs[:count]):

            @pl.when(chosen == i)
            def _():
                copy = pltpu.make_async_copy(ref, out_ref, sem)
                copy.start()
                copy.wait()

    anywhere = pl.BlockSpec(memory_space=pl.ANY)
    picked, *state[:] = pl.pallas_call(
        kernel,
        in_specs=[pl.BlockSpec(memory_space=pltpu.SMEM), WHOLE] + [anywhere] * count + [WHOLE] * 2,
        out_specs=[anywhere, WHOLE, WHOLE, WHOLE],
        out_shape=[
            jax.ShapeDtypeStruct(arrays[0].shape, arrays[0].dtype),
            jax.ShapeDtypeStruct(mark.shape, mark.dtype),
            pltpu.VMEM(held.shape, held.dtype),
            pltpu.VMEM(prepared.shape, prepared.dtype),
        ],
        scratch_shapes=[pltpu.SemaphoreType.DMA(())],
        input_output_aliases={count + 2: 2, count + 3: 3},
        compiler_params=pltpu.CompilerParams(vmem_limit_bytes=4 * 2**20),
    )(table, mark, *arrays, in_vmem(held), in_vmem(prepared))
    return picked


def pack(beside, *arrays):
    rows, width = arrays[0].shape
    half = width // 2

    def kernel(*refs):
        *in_refs, mine_ref, other_ref, sems = refs
        core = lax.rem(lax.axis_index("ctx"), 2)
        copies = []
        for out_ref, place in ((other_ref, 1 - core), (mine_ref, core)):
            columns = pl.ds(pl.multiple_of(place * half, half), half)
            for i, ref in enumerate(in_refs):
                target = out_ref.at[pl.ds(i // beside * rows, rows), pl.ds(i % beside * half, half)]
                copies.append(pltpu.make_async_copy(ref.at[:, columns], target, sems.at[len(copies)]))
        for copy in copies:
            copy.start()
        for copy in copies:
            copy.wait()

    anywhere = pl.BlockSpec(memory_space=pl.ANY)
    packed = jax.ShapeDtypeStruct((len(arrays) // beside * rows, beside * half), arrays[0].dtype)
    return pl.pallas_call(
        kernel,
        in_specs=[anywhere] * len(arrays),
        out_specs=[anywhere] * 2,
        out_shape=[packed] * 2,
        scratch_shapes=[pltpu.SemaphoreType.DMA((2 * len(arrays),))],
        compiler_params=pltpu.CompilerParams(vmem_limit_bytes=4 * 2**20),
    )(*(pltpu.with_memory_space_constraint(array, pltpu.HBM) for array in arrays))


def assemble(mine, got):
    rows, half = mine.shape

    def kernel(mine_ref, got_ref, out_ref, sems):
        core = lax.rem(lax.axis_index("ctx"), 2)
        copies = []
        for i, (ref, place) in enumerate(((mine_ref, core), (got_ref, 1 - core))):
            columns = pl.ds(pl.multiple_of(place * half, half), half)
            copies.append(pltpu.make_async_copy(ref, out_ref.at[:, columns], sems.at[i]))
            copies[i].start()
        for copy in copies:
            copy.wait()

    anywhere = pl.BlockSpec(memory_space=pl.ANY)
    return pl.pallas_call(
        kernel,
        in_specs=[anywhere] * 2,
        out_specs=anywhere,
        out_shape=jax.ShapeDtypeStruct((rows, 2 * half), mine.dtype),
        scratch_shapes=[pltpu.SemaphoreType.DMA((2,))],
        compiler_params=pltpu.CompilerParams(vmem_limit_bytes=4 * 2**20),
    )(mine, got)


def attend(ny, rows, tables, arrays, groups, queries, state, last):
    stacked = GW * rows
    first = state is None
    smem = pl.BlockSpec(memory_space=pltpu.SMEM)
    row_spec = pl.BlockSpec((rows, GW * HD), lambda h: (0, h))
    operands = [*tables]
    specs = [smem, smem]
    if first:
        operands += queries
        specs += [row_spec, row_spec]
    else:
        mark, state, prepared = state
    for shift in (0, HALF_KV):
        for array in arrays:
            operands.append(array)
            specs.append(pl.BlockSpec((array.shape[0], HD), functools.partial(lambda s, h: (0, s + h), shift)))
    aliases = {}
    if last:
        out_shape = [jax.ShapeDtypeStruct((rows, HALF_KV * GW * HD), jnp.bfloat16)] * 2
        out_specs = [row_spec, row_spec]
    else:
        out_shape = [jax.ShapeDtypeStruct((8, HD), jnp.float32)]
        out_specs = [pl.BlockSpec((8, HD), lambda h: (0, 0))]
    if not first:
        aliases = {len(operands) + 1 + i: len(out_shape) + i for i in range(2)}
        operands += [mark, in_vmem(state), in_vmem(prepared)]
        specs += [pl.BlockSpec(memory_space=pl.ANY), WHOLE, WHOLE]
    out_shape.append(pltpu.VMEM((HALF_KV, 2, stacked, 3 * HD), jnp.float32))
    out_shape.append(pltpu.VMEM((HALF_KV, 2, stacked, HD), jnp.bfloat16))
    out_specs += [WHOLE, WHOLE]
    scores = HALF_KV * 2 * stacked * rows * sum(len(members) for members in groups)
    out = pl.pallas_call(
        functools.partial(attend_kernel, ny, rows, len(arrays), groups, first, last),
        grid=(HALF_KV,),
        in_specs=specs,
        out_specs=out_specs,
        out_shape=out_shape,
        input_output_aliases=aliases,
        compiler_params=pltpu.CompilerParams(vmem_limit_bytes=24 * 2**20),
        cost_estimate=pl.CostEstimate(flops=8 * scores * HD, bytes_accessed=4 * 2**20, transcendentals=scores),
    )(*operands)
    return out[:2] if last else list(out)


def on_device(queries, seg_keys, seg_values, root_keys, root_values, expansion, root_offsets):
    leaves, spots = lax.axis_size("leaf"), lax.axis_size("ctx")
    ny = spots // 4
    rows = queries.shape[0]
    group = lax.axis_index("leaf")
    def index(x, y, k):
        return ((y % ny) * 2 + x % 2) * 2 + k % 2

    places = [(x, y, k) for y in range(ny) for x in range(2) for k in range(2)]

    def to_core(array):
        return lax.ppermute(array, "ctx", [(index(x, y, k), index(x, y, k + 1)) for x, y, k in places])

    def to_x(array):
        return lax.ppermute(array, "ctx", [(index(x, y, k), index(x + 1, y, k)) for x, y, k in places])

    def to_y(array, step):
        return lax.ppermute(array, "ctx", [(index(x, y, k), index(x, y + step, k)) for x, y, k in places])

    mine, sent = pack(2, seg_keys, seg_values, root_keys, root_values)
    queries, sent = lax.optimization_barrier((queries, sent))
    q_mine, q_other = pack(1, queries)
    q_other, got = lax.optimization_barrier((q_other, to_core(sent)))
    own = jnp.concatenate([mine[:rows], got[:rows]], axis=0)
    root = jnp.concatenate([mine[rows:], got[rows:]], axis=0)
    run = functools.partial(attend, ny, rows, (expansion, root_offsets))
    steps = range(1, ny)

    def members(array, kind, dx=0, dy=0, flips=(0, 1), first=0):
        return tuple((array, first + i, (kind, dx, dy, flip)) for i, flip in enumerate(flips))

    def after(state, *values):
        *values, state[0] = lax.optimization_barrier((*values, state[0]))
        return values

    def hop(step, rows_held):
        pairs = [(i, (i - 1) % leaves) for i in range(leaves)]
        return lax.ppermute(rows_held, "leaf", pairs if step < leaves - 1 else pairs[1:])

    direct = leaves == 4
    ahead = [own]
    if direct:
        for pairs in (((1, 0), (2, 1), (3, 2)), ((0, 2), (3, 1))):
            ahead.append(lax.ppermute(own, "leaf", pairs))
    elif leaves > 1:
        ahead.append(hop(1, own))
    own, q_got = lax.optimization_barrier((own, to_core(q_other)))
    q_pair = (q_mine, q_got)
    own_x, own_y = to_x(own), [to_y(own, step) for step in steps]
    state = run([own, root], (members(0, "own") + members(1, "root"),), q_pair, None, False)

    root, sent_up = after(state, root, own)
    if direct:
        before = lax.ppermute(sent_up, "leaf", ((0, 1), (1, 2)))
    root_x, root_y = to_x(root), [to_y(root, step) for step in steps]

    def near(kind):
        groups = [members(0, kind, 1) + members(1, kind, 0, 1)]
        return groups + [members(step, kind, 0, step) for step in steps if step > 1]

    if leaves > 2 and not direct:
        (held,) = fence(state, ahead[-1])
        ahead[-1] = held
        ahead.append(hop(2, held))
    own_x, *own_y = after(state, own_x, *own_y)
    state = run([own_x, *own_y], tuple(near("own")), None, state, False)
    if direct:
        ahead = after(state, *ahead)
        relay = pick(state, expansion, lambda table, g: jnp.where(table[0, 0] == 3, 1, 0), ahead[1:])
        ahead += [before, lax.ppermute(relay, "leaf", [(1, 0)])]
    else:
        for step in range(3, leaves):
            (held,) = fence(state, ahead[-1])
            ahead[-1] = held
            ahead.append(hop(step, held))
    own_x, root_x, *root_y = after(state, own_x, root_x, *root_y)
    own_far = [to_y(own_x, step) for step in steps]
    root_far = [to_x(array) for array in root_y]
    state = run([root_x, *root_y], tuple(near("root")), None, state, False)

    def choose(table, g):
        offset = table[0, g] - g
        if not direct:
            return lax.rem(offset + leaves, leaves)
        far_one = jnp.where(g == 0, 4, 2)
        return jnp.where(offset == 0, 0, jnp.where(offset == 1, 1, jnp.where(offset == -1, 3, far_one)))

    parent_rows = pick(state, expansion, choose, after(state, *ahead))
    (parent_rows,) = after(state, parent_rows)
    kin_x, kin_y = to_x(parent_rows), [to_y(parent_rows, step) for step in steps]
    groups = [members(i, "own", 1, i + 1) + members(ny - 1 + i, "root", 1, i + 1) for i in range(ny - 1)]
    groups[0] += members(2 * ny - 2, "kin")
    state = run([*own_far, *root_far, parent_rows], tuple(groups), None, state, False)

    (kin_x,) = after(state, kin_x)
    tops = [to_y(kin_x[:rows], step) for step in steps]
    lows = [to_x(array[rows:]) for array in kin_y]
    groups = [members(0, "kin") + members(1, "kin")] + [members(step, "kin") for step in steps if step > 1]
    state = run([kin_x, *kin_y], tuple(groups), None, state, False)
    groups = [members(i, "kin", flips=(0,)) + members(len(tops) + i, "kin", flips=(1,)) for i in range(len(tops))]
    out_mine, out_other = run([*tops, *lows], tuple(groups), None, state, True)
    return assemble(out_mine, to_core(out_other))


def solution(mesh):
    return jax.shard_map(
        on_device,
        mesh=mesh,
        in_specs=(
            P(("leaf", "ctx"), None),
            P(("leaf", "ctx"), None),
            P(("leaf", "ctx"), None),
            P("ctx", None),
            P("ctx", None),
            P(),
            P(),
        ),
        out_specs=P(("leaf", "ctx"), None),
        check_vma=False,
    )
```

```python
import functools
import math

import jax
import jax.numpy as jnp
from jax import lax
from jax.experimental import pallas as pl
from jax.experimental.pallas import tpu as pltpu
from jax.sharding import PartitionSpec as P

HQ = 64
KVH = 8
HD = 128
GW = HQ // KVH
HALF_KV = KVH // 2
NEG = -1e30
EXP_SCALE = math.log2(math.e) / math.sqrt(HD)
ROW_BLOCK = 256
KEY_CHUNK = 256


def attend_kernel(ny, rows, arrays, groups, first, last, *refs):
    refs = list(refs)
    take = lambda count: [refs.pop(0) for _ in range(count)]
    exp_ref, off_ref = take(2)
    raw = take(2) if first else None
    key_refs = take(arrays)
    value_refs = take(arrays)
    head = pl.program_id(0)
    if not first:
        take(3)
    if last:
        outs = take(2)
    else:
        take(1)[0][...] = jnp.zeros((8, HD), jnp.float32)
    held, qs = take(2)
    stacked = GW * rows

    group = lax.axis_index("leaf")
    spot = lax.axis_index("ctx")
    core, chip = lax.rem(spot, 2), spot // 2
    chip_x, chip_y = lax.rem(chip, 2), chip // 2
    visible = off_ref[group]
    depth = exp_ref[1, group]

    def block_start(dx, dy, flip):
        x = lax.rem(chip_x + dx, 2)
        y = lax.rem(chip_y - dy + ny, ny)
        k = lax.rem(core + flip, 2)
        return ((y * 2 + x) * 2 + k) * rows

    if first:
        for s, q_ref in enumerate(raw):
            for g in range(GW):
                qs[head, s, g * rows : (g + 1) * rows, :] = q_ref[:, g * HD : (g + 1) * HD]

    def step(members, limits, masked, fresh):
        width = len(members) * rows
        cut = lambda refs: [refs[a][b * rows : (b + 1) * rows, :] for a, b, _ in members]
        keys = jnp.concatenate(cut(key_refs), axis=0)
        values = jnp.concatenate(cut(value_refs), axis=0)
        values = jnp.concatenate([values, jnp.ones_like(values)], axis=1)
        size = min(ROW_BLOCK, stacked)
        todo = [(s, slice(base, base + size)) for s in range(2) for base in range(0, stacked, size)]

        chunks = [slice(c, min(c + KEY_CHUNK, width)) for c in range(0, width, KEY_CHUNK)]
        biases = {}

        def bias_of(s):
            if s not in biases:
                column = lax.broadcasted_iota(jnp.int32, (rows, rows), 1)
                line = lax.broadcasted_iota(jnp.int32, (rows, rows), 0)
                allowed = []
                for (_, _, block), limit in zip(members, limits[s]):
                    ahead = column - line if block[0] == "own" else column
                    allowed.append(jnp.where(ahead < limit, 0.0, NEG))
                biases[s] = jnp.concatenate(allowed, axis=1)
            return biases[s]

        def score(item, chunk):
            s, here = item
            found = lax.dot_general(
                qs[head, s, here, :], keys[chunk], (((1,), (1,)), ((), ())), preferred_element_type=jnp.float32
            )
            if masked:
                found = found + jnp.concatenate([bias_of(s)[:, chunk]] * (size // rows), axis=0)
            return found

        def peak_of(scores):
            parts = [part[:, c : c + HD] for part in scores for c in range(0, part.shape[1], HD)]
            return jnp.max(functools.reduce(jnp.maximum, parts), axis=1, keepdims=True)

        scores = [score(todo[0], chunk) for chunk in chunks]
        peak = peak_of(scores)
        for at, (s, here) in enumerate(todo):
            if fresh:
                new = jnp.broadcast_to(peak, (size, HD))
            else:
                old = held[head, s, here, 2 * HD :]
                new = jnp.maximum(old, peak)
            following, weights = [], []
            for i, chunk in enumerate(chunks):
                if at + 1 < len(todo):
                    following.append(score(todo[at + 1], chunk))
                shifted = scores[i] - jnp.concatenate([new] * (scores[i].shape[1] // HD), axis=1)
                weights.append(jnp.exp2(shifted * EXP_SCALE).astype(jnp.bfloat16))
            update = jnp.dot(jnp.concatenate(weights, axis=1), values, preferred_element_type=jnp.float32)
            if following:
                scores, peak = following, peak_of(following)
            if fresh:
                held[head, s, here, : 2 * HD] = update
            else:
                shrink = jnp.exp2((old - new) * EXP_SCALE)
                before = held[head, s, here, : 2 * HD] * jnp.concatenate([shrink, shrink], axis=1)
                held[head, s, here, : 2 * HD] = before + update
            held[head, s, here, 2 * HD :] = new

    for number, members in enumerate(groups):
        limits = []
        full, some = jnp.bool_(True), jnp.bool_(False)
        for s in range(2):
            first_row = block_start(0, 0, s)
            limits.append([])
            for _, _, (kind, dx, dy, flip) in members:
                if kind == "root":
                    limit = visible - block_start(dx, dy, flip)
                    some_here = limit > 0
                elif kind == "own":
                    limit = first_row - block_start(dx, dy, flip) + 1
                    some_here = limit + rows - 1 > 0
                else:
                    limit = jnp.where(depth > 0, rows, 0)
                    some_here = limit > 0
                limits[s].append(limit)
                full = full & (limit >= rows)
                some = some | some_here
        kinds = {block[0] for _, _, block in members}
        if first and number == 0:
            step(members, limits, True, True)
            continue
        pl.when(full)(functools.partial(step, members, limits, False, False))
        if kinds != {"kin"}:
            pl.when(jnp.logical_not(full) & some)(functools.partial(step, members, limits, True, False))

    if last:
        for s in range(2):
            for g in range(GW):
                here = slice(g * rows, (g + 1) * rows)
                done = held[head, s, here, :HD] / held[head, s, here, HD : 2 * HD]
                outs[s][:, g * HD : (g + 1) * HD] = done.astype(jnp.bfloat16)


WHOLE = pl.BlockSpec(memory_space=pltpu.VMEM)


def in_vmem(array):
    return pltpu.with_memory_space_constraint(array, pltpu.VMEM)


def fence(state, *values):
    mark, held, prepared = state
    *values, mark = lax.optimization_barrier((*values, mark))

    def kernel(mark_ref, *refs):
        refs[2][...] = mark_ref[...]

    state[:] = pl.pallas_call(
        kernel,
        in_specs=[WHOLE] * 3,
        out_specs=[WHOLE] * 3,
        out_shape=[
            jax.ShapeDtypeStruct(mark.shape, mark.dtype),
            pltpu.VMEM(held.shape, held.dtype),
            pltpu.VMEM(prepared.shape, prepared.dtype),
        ],
        input_output_aliases={1: 1, 2: 2},
        compiler_params=pltpu.CompilerParams(vmem_limit_bytes=4 * 2**20),
    )(mark, in_vmem(held), in_vmem(prepared))
    return values


def pick(state, table, choose, arrays):
    mark, held, prepared = state
    count = len(arrays)

    def kernel(table_ref, mark_ref, *refs):
        out_ref, mark_out_ref, _, _, sem = refs[count + 2 :]
        mark_out_ref[...] = mark_ref[...]
        chosen = choose(table_ref, lax.axis_index("leaf"))
        for i, ref in enumerate(refs[:count]):

            @pl.when(chosen == i)
            def _():
                copy = pltpu.make_async_copy(ref, out_ref, sem)
                copy.start()
                copy.wait()

    anywhere = pl.BlockSpec(memory_space=pl.ANY)
    picked, *state[:] = pl.pallas_call(
        kernel,
        in_specs=[pl.BlockSpec(memory_space=pltpu.SMEM), WHOLE] + [anywhere] * count + [WHOLE] * 2,
        out_specs=[anywhere, WHOLE, WHOLE, WHOLE],
        out_shape=[
            jax.ShapeDtypeStruct(arrays[0].shape, arrays[0].dtype),
            jax.ShapeDtypeStruct(mark.shape, mark.dtype),
            pltpu.VMEM(held.shape, held.dtype),
            pltpu.VMEM(prepared.shape, prepared.dtype),
        ],
        scratch_shapes=[pltpu.SemaphoreType.DMA(())],
        input_output_aliases={count + 2: 2, count + 3: 3},
        compiler_params=pltpu.CompilerParams(vmem_limit_bytes=4 * 2**20),
    )(table, mark, *arrays, in_vmem(held), in_vmem(prepared))
    return picked


def pack(beside, *arrays):
    rows, width = arrays[0].shape
    half = width // 2

    def kernel(*refs):
        *in_refs, mine_ref, other_ref, sems = refs
        core = lax.rem(lax.axis_index("ctx"), 2)
        copies = []
        for out_ref, place in ((other_ref, 1 - core), (mine_ref, core)):
            columns = pl.ds(pl.multiple_of(place * half, half), half)
            for i, ref in enumerate(in_refs):
                target = out_ref.at[pl.ds(i // beside * rows, rows), pl.ds(i % beside * half, half)]
                copies.append(pltpu.make_async_copy(ref.at[:, columns], target, sems.at[len(copies)]))
        for copy in copies:
            copy.start()
        for copy in copies:
            copy.wait()

    anywhere = pl.BlockSpec(memory_space=pl.ANY)
    packed = jax.ShapeDtypeStruct((len(arrays) // beside * rows, beside * half), arrays[0].dtype)
    return pl.pallas_call(
        kernel,
        in_specs=[anywhere] * len(arrays),
        out_specs=[anywhere] * 2,
        out_shape=[packed] * 2,
        scratch_shapes=[pltpu.SemaphoreType.DMA((2 * len(arrays),))],
        compiler_params=pltpu.CompilerParams(vmem_limit_bytes=4 * 2**20),
    )(*(pltpu.with_memory_space_constraint(array, pltpu.HBM) for array in arrays))


def assemble(mine, got):
    rows, half = mine.shape

    def kernel(mine_ref, got_ref, out_ref, sems):
        core = lax.rem(lax.axis_index("ctx"), 2)
        copies = []
        for i, (ref, place) in enumerate(((mine_ref, core), (got_ref, 1 - core))):
            columns = pl.ds(pl.multiple_of(place * half, half), half)
            copies.append(pltpu.make_async_copy(ref, out_ref.at[:, columns], sems.at[i]))
            copies[i].start()
        for copy in copies:
            copy.wait()

    anywhere = pl.BlockSpec(memory_space=pl.ANY)
    return pl.pallas_call(
        kernel,
        in_specs=[anywhere] * 2,
        out_specs=anywhere,
        out_shape=jax.ShapeDtypeStruct((rows, 2 * half), mine.dtype),
        scratch_shapes=[pltpu.SemaphoreType.DMA((2,))],
        compiler_params=pltpu.CompilerParams(vmem_limit_bytes=4 * 2**20),
    )(mine, got)


def attend(ny, rows, tables, arrays, groups, queries, state, last):
    stacked = GW * rows
    first = state is None
    smem = pl.BlockSpec(memory_space=pltpu.SMEM)
    row_spec = pl.BlockSpec((rows, GW * HD), lambda h: (0, h))
    operands = [*tables]
    specs = [smem, smem]
    if first:
        operands += queries
        specs += [row_spec, row_spec]
    else:
        mark, state, prepared = state
    for shift in (0, HALF_KV):
        for array in arrays:
            operands.append(array)
            specs.append(pl.BlockSpec((array.shape[0], HD), functools.partial(lambda s, h: (0, s + h), shift)))
    aliases = {}
    if last:
        out_shape = [jax.ShapeDtypeStruct((rows, HALF_KV * GW * HD), jnp.bfloat16)] * 2
        out_specs = [row_spec, row_spec]
    else:
        out_shape = [jax.ShapeDtypeStruct((8, HD), jnp.float32)]
        out_specs = [pl.BlockSpec((8, HD), lambda h: (0, 0))]
    if not first:
        aliases = {len(operands) + 1 + i: len(out_shape) + i for i in range(2)}
        operands += [mark, in_vmem(state), in_vmem(prepared)]
        specs += [pl.BlockSpec(memory_space=pl.ANY), WHOLE, WHOLE]
    out_shape.append(pltpu.VMEM((HALF_KV, 2, stacked, 3 * HD), jnp.float32))
    out_shape.append(pltpu.VMEM((HALF_KV, 2, stacked, HD), jnp.bfloat16))
    out_specs += [WHOLE, WHOLE]
    scores = HALF_KV * 2 * stacked * rows * sum(len(members) for members in groups)
    out = pl.pallas_call(
        functools.partial(attend_kernel, ny, rows, len(arrays), groups, first, last),
        grid=(HALF_KV,),
        in_specs=specs,
        out_specs=out_specs,
        out_shape=out_shape,
        input_output_aliases=aliases,
        compiler_params=pltpu.CompilerParams(vmem_limit_bytes=24 * 2**20),
        cost_estimate=pl.CostEstimate(flops=8 * scores * HD, bytes_accessed=4 * 2**20, transcendentals=scores),
    )(*operands)
    return out[:2] if last else list(out)


def on_device(queries, seg_keys, seg_values, root_keys, root_values, expansion, root_offsets):
    leaves, spots = lax.axis_size("leaf"), lax.axis_size("ctx")
    ny = spots // 4
    rows = queries.shape[0]
    group = lax.axis_index("leaf")
    def index(x, y, k):
        return ((y % ny) * 2 + x % 2) * 2 + k % 2

    places = [(x, y, k) for y in range(ny) for x in range(2) for k in range(2)]

    def to_core(array):
        return lax.ppermute(array, "ctx", [(index(x, y, k), index(x, y, k + 1)) for x, y, k in places])

    def to_x(array):
        return lax.ppermute(array, "ctx", [(index(x, y, k), index(x + 1, y, k)) for x, y, k in places])

    def to_y(array, step):
        return lax.ppermute(array, "ctx", [(index(x, y, k), index(x, y + step, k)) for x, y, k in places])

    mine, sent = pack(2, seg_keys, seg_values, root_keys, root_values)
    queries, sent = lax.optimization_barrier((queries, sent))
    q_mine, q_other = pack(1, queries)
    q_other, got = lax.optimization_barrier((q_other, to_core(sent)))
    own = jnp.concatenate([mine[:rows], got[:rows]], axis=0)
    root = jnp.concatenate([mine[rows:], got[rows:]], axis=0)
    run = functools.partial(attend, ny, rows, (expansion, root_offsets))
    steps = range(1, ny)

    def members(array, kind, dx=0, dy=0, flips=(0, 1), first=0):
        return tuple((array, first + i, (kind, dx, dy, flip)) for i, flip in enumerate(flips))

    def after(state, *values):
        *values, state[0] = lax.optimization_barrier((*values, state[0]))
        return values

    def hop(step, rows_held):
        pairs = [(i, (i - 1) % leaves) for i in range(leaves)]
        return lax.ppermute(rows_held, "leaf", pairs if step < leaves - 1 else pairs[1:])

    own_x, own_y = to_x(own), [to_y(own, step) for step in steps]
    own, q_got = lax.optimization_barrier((own, to_core(q_other)))
    q_pair = (q_mine, q_got)
    direct = leaves == 4
    ahead = [own]
    if direct:
        for pairs in (((1, 0), (2, 1), (3, 2)), ((0, 2), (3, 1))):
            ahead.append(lax.ppermute(own, "leaf", pairs))
    elif leaves > 1:
        ahead.append(hop(1, own))
    state = run([own, root], (members(0, "own") + members(1, "root"),), q_pair, None, False)

    root, sent_up = after(state, root, own)
    if direct:
        before = lax.ppermute(sent_up, "leaf", ((0, 1), (1, 2)))
    root_x, root_y = to_x(root), [to_y(root, step) for step in steps]

    def near(kind):
        groups = [members(0, kind, 1) + members(1, kind, 0, 1)]
        return groups + [members(step, kind, 0, step) for step in steps if step > 1]

    if leaves > 2 and not direct:
        (held,) = fence(state, ahead[-1])
        ahead[-1] = held
        ahead.append(hop(2, held))
    own_x, *own_y = after(state, own_x, *own_y)
    state = run([own_x, *own_y], tuple(near("own")), None, state, False)
    if direct:
        ahead = after(state, *ahead)
        relay = pick(state, expansion, lambda table, g: jnp.where(table[0, 0] == 3, 1, 0), ahead[1:])
        ahead += [before, lax.ppermute(relay, "leaf", [(1, 0)])]
    else:
        for step in range(3, leaves):
            (held,) = fence(state, ahead[-1])
            ahead[-1] = held
            ahead.append(hop(step, held))
    own_x, root_x, *root_y = after(state, own_x, root_x, *root_y)
    own_far = [to_y(own_x, step) for step in steps]
    root_far = [to_x(array) for array in root_y]
    state = run([root_x, *root_y], tuple(near("root")), None, state, False)

    def choose(table, g):
        offset = table[0, g] - g
        if not direct:
            return lax.rem(offset + leaves, leaves)
        far_one = jnp.where(g == 0, 4, 2)
        return jnp.where(offset == 0, 0, jnp.where(offset == 1, 1, jnp.where(offset == -1, 3, far_one)))

    parent_rows = pick(state, expansion, choose, after(state, *ahead))
    (parent_rows,) = after(state, parent_rows)
    kin_x, kin_y = to_x(parent_rows), [to_y(parent_rows, step) for step in steps]
    groups = [members(i, "own", 1, i + 1) + members(ny - 1 + i, "root", 1, i + 1) for i in range(ny - 1)]
    groups[0] += members(2 * ny - 2, "kin")
    state = run([*own_far, *root_far, parent_rows], tuple(groups), None, state, False)

    (kin_x,) = after(state, kin_x)
    tops = [to_y(kin_x[:rows], step) for step in steps]
    lows = [to_x(array[rows:]) for array in kin_y]
    groups = [members(0, "kin") + members(1, "kin")] + [members(step, "kin") for step in steps if step > 1]
    state = run([kin_x, *kin_y], tuple(groups), None, state, False)
    groups = [members(i, "kin", flips=(0,)) + members(len(tops) + i, "kin", flips=(1,)) for i in range(len(tops))]
    out_mine, out_other = run([*tops, *lows], tuple(groups), None, state, True)
    return assemble(out_mine, to_core(out_other))


def solution(mesh):
    return jax.shard_map(
        on_device,
        mesh=mesh,
        in_specs=(
            P(("leaf", "ctx"), None),
            P(("leaf", "ctx"), None),
            P(("leaf", "ctx"), None),
            P("ctx", None),
            P("ctx", None),
            P(),
            P(),
        ),
        out_specs=P(("leaf", "ctx"), None),
        check_vma=False,
    )
```

```python
import functools
import math

import jax
import jax.numpy as jnp
from jax import lax
from jax.experimental import pallas as pl
from jax.experimental.pallas import tpu as pltpu
from jax.sharding import PartitionSpec as P

HQ = 64
KVH = 8
HD = 128
GW = HQ // KVH
HALF_KV = KVH // 2
NEG = -1e30
EXP_SCALE = math.log2(math.e) / math.sqrt(HD)
ROW_BLOCK = 256
KEY_CHUNK = 256


def attend_kernel(ny, rows, arrays, groups, sides, first, last, *refs):
    refs = list(refs)
    take = lambda count: [refs.pop(0) for _ in range(count)]
    exp_ref, off_ref = take(2)
    raw = take(2) if first else None
    key_refs = take(arrays)
    value_refs = take(arrays)
    head = pl.program_id(0)
    if not first:
        take(3)
    if last:
        outs = take(len(sides))
    else:
        take(1)[0][...] = jnp.zeros((8, HD), jnp.float32)
    held, qs = take(2)
    stacked = GW * rows

    group = lax.axis_index("leaf")
    spot = lax.axis_index("ctx")
    core, chip = lax.rem(spot, 2), spot // 2
    chip_x, chip_y = lax.rem(chip, 2), chip // 2
    visible = off_ref[group]
    depth = exp_ref[1, group]

    def block_start(dx, dy, flip):
        x = lax.rem(chip_x + dx, 2)
        y = lax.rem(chip_y - dy + ny, ny)
        k = lax.rem(core + flip, 2)
        return ((y * 2 + x) * 2 + k) * rows

    if first:
        for s, q_ref in enumerate(raw):
            for g in range(GW):
                qs[head, s, g * rows : (g + 1) * rows, :] = q_ref[:, g * HD : (g + 1) * HD]

    def step(members, limits, masked, fresh):
        width = len(members) * rows
        cut = lambda refs: [refs[a][b * rows : (b + 1) * rows, :] for a, b, _ in members]
        keys = jnp.concatenate(cut(key_refs), axis=0)
        values = jnp.concatenate(cut(value_refs), axis=0)
        values = jnp.concatenate([values, jnp.ones_like(values)], axis=1)
        size = min(ROW_BLOCK, stacked)
        todo = [(s, slice(base, base + size)) for s in sides for base in range(0, stacked, size)]

        chunks = [slice(c, min(c + KEY_CHUNK, width)) for c in range(0, width, KEY_CHUNK)]
        biases = {}

        def bias_of(s):
            if s not in biases:
                column = lax.broadcasted_iota(jnp.int32, (rows, rows), 1)
                line = lax.broadcasted_iota(jnp.int32, (rows, rows), 0)
                allowed = []
                for (_, _, block), limit in zip(members, limits[s]):
                    ahead = column - line if block[0] == "own" else column
                    allowed.append(jnp.where(ahead < limit, 0.0, NEG))
                biases[s] = jnp.concatenate(allowed, axis=1)
            return biases[s]

        def score(item, chunk):
            s, here = item
            found = lax.dot_general(
                qs[head, s, here, :], keys[chunk], (((1,), (1,)), ((), ())), preferred_element_type=jnp.float32
            )
            if masked:
                found = found + jnp.concatenate([bias_of(s)[:, chunk]] * (size // rows), axis=0)
            return found

        def peak_of(scores):
            parts = [part[:, c : c + HD] for part in scores for c in range(0, part.shape[1], HD)]
            return jnp.max(functools.reduce(jnp.maximum, parts), axis=1, keepdims=True)

        scores = [score(todo[0], chunk) for chunk in chunks]
        peak = peak_of(scores)
        for at, (s, here) in enumerate(todo):
            if fresh:
                new = jnp.broadcast_to(peak, (size, HD))
            else:
                old = held[head, s, here, 2 * HD :]
                new = jnp.maximum(old, peak)
            following, weights = [], []
            for i, chunk in enumerate(chunks):
                if at + 1 < len(todo):
                    following.append(score(todo[at + 1], chunk))
                shifted = scores[i] - jnp.concatenate([new] * (scores[i].shape[1] // HD), axis=1)
                weights.append(jnp.exp2(shifted * EXP_SCALE).astype(jnp.bfloat16))
            update = jnp.dot(jnp.concatenate(weights, axis=1), values, preferred_element_type=jnp.float32)
            if following:
                scores, peak = following, peak_of(following)
            if fresh:
                held[head, s, here, : 2 * HD] = update
            else:
                shrink = jnp.exp2((old - new) * EXP_SCALE)
                before = held[head, s, here, : 2 * HD] * jnp.concatenate([shrink, shrink], axis=1)
                held[head, s, here, : 2 * HD] = before + update
            held[head, s, here, 2 * HD :] = new

    for number, members in enumerate(groups):
        limits = []
        full, some = jnp.bool_(True), jnp.bool_(False)
        for s in range(2):
            first_row = block_start(0, 0, s)
            limits.append([])
            for _, _, (kind, dx, dy, flip) in members:
                if kind == "root":
                    limit = visible - block_start(dx, dy, flip)
                    some_here = limit > 0
                elif kind == "own":
                    limit = first_row - block_start(dx, dy, flip) + 1
                    some_here = limit + rows - 1 > 0
                else:
                    limit = jnp.where(depth > 0, rows, 0)
                    some_here = limit > 0
                limits[s].append(limit)
                full = full & (limit >= rows)
                some = some | some_here
        kinds = {block[0] for _, _, block in members}
        if first and number == 0:
            step(members, limits, True, True)
            continue
        pl.when(full)(functools.partial(step, members, limits, False, False))
        if kinds != {"kin"}:
            pl.when(jnp.logical_not(full) & some)(functools.partial(step, members, limits, True, False))

    if last:
        for out_ref, s in zip(outs, sides):
            for g in range(GW):
                here = slice(g * rows, (g + 1) * rows)
                done = held[head, s, here, :HD] / held[head, s, here, HD : 2 * HD]
                out_ref[:, g * HD : (g + 1) * HD] = done.astype(jnp.bfloat16)


WHOLE = pl.BlockSpec(memory_space=pltpu.VMEM)


def in_vmem(array):
    return pltpu.with_memory_space_constraint(array, pltpu.VMEM)


def fence(state, *values):
    mark, held, prepared = state
    *values, mark = lax.optimization_barrier((*values, mark))

    def kernel(mark_ref, *refs):
        refs[2][...] = mark_ref[...]

    state[:] = pl.pallas_call(
        kernel,
        in_specs=[WHOLE] * 3,
        out_specs=[WHOLE] * 3,
        out_shape=[
            jax.ShapeDtypeStruct(mark.shape, mark.dtype),
            pltpu.VMEM(held.shape, held.dtype),
            pltpu.VMEM(prepared.shape, prepared.dtype),
        ],
        input_output_aliases={1: 1, 2: 2},
        compiler_params=pltpu.CompilerParams(vmem_limit_bytes=4 * 2**20),
    )(mark, in_vmem(held), in_vmem(prepared))
    return values


def pick(state, table, choose, arrays):
    mark, held, prepared = state
    count = len(arrays)

    def kernel(table_ref, mark_ref, *refs):
        out_ref, mark_out_ref, _, _, sem = refs[count + 2 :]
        mark_out_ref[...] = mark_ref[...]
        chosen = choose(table_ref, lax.axis_index("leaf"))
        for i, ref in enumerate(refs[:count]):

            @pl.when(chosen == i)
            def _():
                copy = pltpu.make_async_copy(ref, out_ref, sem)
                copy.start()
                copy.wait()

    anywhere = pl.BlockSpec(memory_space=pl.ANY)
    picked, *state[:] = pl.pallas_call(
        kernel,
        in_specs=[pl.BlockSpec(memory_space=pltpu.SMEM), WHOLE] + [anywhere] * count + [WHOLE] * 2,
        out_specs=[anywhere, WHOLE, WHOLE, WHOLE],
        out_shape=[
            jax.ShapeDtypeStruct(arrays[0].shape, arrays[0].dtype),
            jax.ShapeDtypeStruct(mark.shape, mark.dtype),
            pltpu.VMEM(held.shape, held.dtype),
            pltpu.VMEM(prepared.shape, prepared.dtype),
        ],
        scratch_shapes=[pltpu.SemaphoreType.DMA(())],
        input_output_aliases={count + 2: 2, count + 3: 3},
        compiler_params=pltpu.CompilerParams(vmem_limit_bytes=4 * 2**20),
    )(table, mark, *arrays, in_vmem(held), in_vmem(prepared))
    return picked


def pack(beside, *arrays):
    rows, width = arrays[0].shape
    half = width // 2

    def kernel(*refs):
        *in_refs, mine_ref, other_ref, sems = refs
        core = lax.rem(lax.axis_index("ctx"), 2)
        copies = []
        for out_ref, place in ((other_ref, 1 - core), (mine_ref, core)):
            columns = pl.ds(pl.multiple_of(place * half, half), half)
            for i, ref in enumerate(in_refs):
                target = out_ref.at[pl.ds(i // beside * rows, rows), pl.ds(i % beside * half, half)]
                copies.append(pltpu.make_async_copy(ref.at[:, columns], target, sems.at[len(copies)]))
        for copy in copies:
            copy.start()
        for copy in copies:
            copy.wait()

    anywhere = pl.BlockSpec(memory_space=pl.ANY)
    packed = jax.ShapeDtypeStruct((len(arrays) // beside * rows, beside * half), arrays[0].dtype)
    return pl.pallas_call(
        kernel,
        in_specs=[anywhere] * len(arrays),
        out_specs=[anywhere] * 2,
        out_shape=[packed] * 2,
        scratch_shapes=[pltpu.SemaphoreType.DMA((2 * len(arrays),))],
        compiler_params=pltpu.CompilerParams(vmem_limit_bytes=4 * 2**20),
    )(*(pltpu.with_memory_space_constraint(array, pltpu.HBM) for array in arrays))


def assemble(mine, got):
    rows, half = mine.shape

    def kernel(mine_ref, got_ref, out_ref, sems):
        core = lax.rem(lax.axis_index("ctx"), 2)
        copies = []
        for i, (ref, place) in enumerate(((mine_ref, core), (got_ref, 1 - core))):
            columns = pl.ds(pl.multiple_of(place * half, half), half)
            copies.append(pltpu.make_async_copy(ref, out_ref.at[:, columns], sems.at[i]))
            copies[i].start()
        for copy in copies:
            copy.wait()

    anywhere = pl.BlockSpec(memory_space=pl.ANY)
    return pl.pallas_call(
        kernel,
        in_specs=[anywhere] * 2,
        out_specs=anywhere,
        out_shape=jax.ShapeDtypeStruct((rows, 2 * half), mine.dtype),
        scratch_shapes=[pltpu.SemaphoreType.DMA((2,))],
        compiler_params=pltpu.CompilerParams(vmem_limit_bytes=4 * 2**20),
    )(mine, got)


def attend(ny, rows, tables, arrays, groups, queries, state, last, sides=(0, 1)):
    stacked = GW * rows
    first = state is None
    smem = pl.BlockSpec(memory_space=pltpu.SMEM)
    row_spec = pl.BlockSpec((rows, GW * HD), lambda h: (0, h))
    operands = [*tables]
    specs = [smem, smem]
    if first:
        operands += queries
        specs += [row_spec, row_spec]
    else:
        mark, state, prepared = state
    for shift in (0, HALF_KV):
        for array in arrays:
            operands.append(array)
            specs.append(pl.BlockSpec((array.shape[0], HD), functools.partial(lambda s, h: (0, s + h), shift)))
    aliases = {}
    if last:
        out_shape = [jax.ShapeDtypeStruct((rows, HALF_KV * GW * HD), jnp.bfloat16)] * len(sides)
        out_specs = [row_spec] * len(sides)
    else:
        out_shape = [jax.ShapeDtypeStruct((8, HD), jnp.float32)]
        out_specs = [pl.BlockSpec((8, HD), lambda h: (0, 0))]
    if not first:
        aliases = {len(operands) + 1 + i: len(out_shape) + i for i in range(2)}
        operands += [mark, in_vmem(state), in_vmem(prepared)]
        specs += [pl.BlockSpec(memory_space=pl.ANY), WHOLE, WHOLE]
    out_shape.append(pltpu.VMEM((HALF_KV, 2, stacked, 3 * HD), jnp.float32))
    out_shape.append(pltpu.VMEM((HALF_KV, 2, stacked, HD), jnp.bfloat16))
    out_specs += [WHOLE, WHOLE]
    scores = HALF_KV * len(sides) * stacked * rows * sum(len(members) for members in groups)
    out = pl.pallas_call(
        functools.partial(attend_kernel, ny, rows, len(arrays), groups, sides, first, last),
        grid=(HALF_KV,),
        in_specs=specs,
        out_specs=out_specs,
        out_shape=out_shape,
        input_output_aliases=aliases,
        compiler_params=pltpu.CompilerParams(vmem_limit_bytes=24 * 2**20),
        cost_estimate=pl.CostEstimate(flops=8 * scores * HD, bytes_accessed=4 * 2**20, transcendentals=scores),
    )(*operands)
    return list(out)


def on_device(queries, seg_keys, seg_values, root_keys, root_values, expansion, root_offsets):
    leaves, spots = lax.axis_size("leaf"), lax.axis_size("ctx")
    ny = spots // 4
    rows = queries.shape[0]
    group = lax.axis_index("leaf")
    def index(x, y, k):
        return ((y % ny) * 2 + x % 2) * 2 + k % 2

    places = [(x, y, k) for y in range(ny) for x in range(2) for k in range(2)]

    def to_core(array):
        return lax.ppermute(array, "ctx", [(index(x, y, k), index(x, y, k + 1)) for x, y, k in places])

    def to_x(array):
        return lax.ppermute(array, "ctx", [(index(x, y, k), index(x + 1, y, k)) for x, y, k in places])

    def to_y(array, step):
        return lax.ppermute(array, "ctx", [(index(x, y, k), index(x, y + step, k)) for x, y, k in places])

    mine, sent = pack(2, seg_keys, seg_values, root_keys, root_values)
    queries, sent = lax.optimization_barrier((queries, sent))
    q_mine, q_other = pack(1, queries)
    q_other, got = lax.optimization_barrier((q_other, to_core(sent)))
    own = jnp.concatenate([mine[:rows], got[:rows]], axis=0)
    root = jnp.concatenate([mine[rows:], got[rows:]], axis=0)
    run = functools.partial(attend, ny, rows, (expansion, root_offsets))
    steps = range(1, ny)

    def members(array, kind, dx=0, dy=0, flips=(0, 1), first=0):
        return tuple((array, first + i, (kind, dx, dy, flip)) for i, flip in enumerate(flips))

    def after(state, *values):
        *values, state[0] = lax.optimization_barrier((*values, state[0]))
        return values

    def hop(step, rows_held):
        pairs = [(i, (i - 1) % leaves) for i in range(leaves)]
        return lax.ppermute(rows_held, "leaf", pairs if step < leaves - 1 else pairs[1:])

    own_x, own_y = to_x(own), [to_y(own, step) for step in steps]
    own, q_got = lax.optimization_barrier((own, to_core(q_other)))
    q_pair = (q_mine, q_got)
    direct = leaves == 4
    ahead = [own]
    if direct:
        for pairs in (((1, 0), (2, 1), (3, 2)), ((0, 2), (3, 1))):
            ahead.append(lax.ppermute(own, "leaf", pairs))
    elif leaves > 1:
        ahead.append(hop(1, own))
    state = run([own, root], (members(0, "own") + members(1, "root"),), q_pair, None, False)

    root, sent_up = after(state, root, own)
    if direct:
        before = lax.ppermute(sent_up, "leaf", ((0, 1), (1, 2)))
    root_x, root_y = to_x(root), [to_y(root, step) for step in steps]

    def near(kind):
        groups = [members(0, kind, 1) + members(1, kind, 0, 1)]
        return groups + [members(step, kind, 0, step) for step in steps if step > 1]

    if leaves > 2 and not direct:
        (held,) = fence(state, ahead[-1])
        ahead[-1] = held
        ahead.append(hop(2, held))
    own_x, *own_y = after(state, own_x, *own_y)
    state = run([own_x, *own_y], tuple(near("own")), None, state, False)
    if direct:
        ahead = after(state, *ahead)
        relay = pick(state, expansion, lambda table, g: jnp.where(table[0, 0] == 3, 1, 0), ahead[1:])
        ahead += [before, lax.ppermute(relay, "leaf", [(1, 0)])]
    else:
        for step in range(3, leaves):
            (held,) = fence(state, ahead[-1])
            ahead[-1] = held
            ahead.append(hop(step, held))
    own_x, root_x, *root_y = after(state, own_x, root_x, *root_y)
    own_far = [to_y(own_x, step) for step in steps]
    root_far = [to_x(array) for array in root_y]
    state = run([root_x, *root_y], tuple(near("root")), None, state, False)

    def choose(table, g):
        offset = table[0, g] - g
        if not direct:
            return lax.rem(offset + leaves, leaves)
        far_one = jnp.where(g == 0, 4, 2)
        return jnp.where(offset == 0, 0, jnp.where(offset == 1, 1, jnp.where(offset == -1, 3, far_one)))

    parent_rows = pick(state, expansion, choose, after(state, *ahead))
    (parent_rows,) = after(state, parent_rows)
    kin_x, kin_y = to_x(parent_rows), [to_y(parent_rows, step) for step in steps]
    groups = [members(i, "own", 1, i + 1) + members(ny - 1 + i, "root", 1, i + 1) for i in range(ny - 1)]
    groups[0] += members(2 * ny - 2, "kin")
    state = run([*own_far, *root_far, parent_rows], tuple(groups), None, state, False)

    (kin_x,) = after(state, kin_x)
    tops = [to_y(kin_x[:rows], step) for step in steps]
    lows = [to_x(array[rows:]) for array in kin_y]
    groups = [members(0, "kin") + members(1, "kin")] + [members(step, "kin") for step in steps if step > 1]
    state = run([kin_x, *kin_y], tuple(groups), None, state, False)
    groups = [members(i, "kin", flips=(0,)) + members(len(tops) + i, "kin", flips=(1,)) for i in range(len(tops))]
    out_other, *kept = run([*tops, *lows], tuple(groups), None, state, True, (1,))
    out_got = to_core(out_other)
    out_mine, *_ = run([*tops, *lows], tuple(groups), None, [state[0], *kept], True, (0,))
    return assemble(out_mine, out_got)


def solution(mesh):
    return jax.shard_map(
        on_device,
        mesh=mesh,
        in_specs=(
            P(("leaf", "ctx"), None),
            P(("leaf", "ctx"), None),
            P(("leaf", "ctx"), None),
            P("ctx", None),
            P("ctx", None),
            P(),
            P(),
        ),
        out_specs=P(("leaf", "ctx"), None),
        check_vma=False,
    )
```

```python
import functools
import math

import jax
import jax.numpy as jnp
from jax import lax
from jax.experimental import pallas as pl
from jax.experimental.pallas import tpu as pltpu
from jax.sharding import PartitionSpec as P

HQ = 64
KVH = 8
HD = 128
GW = HQ // KVH
HALF_KV = KVH // 2
NEG = -1e30
EXP_SCALE = math.log2(math.e) / math.sqrt(HD)
ROW_BLOCK = 256
KEY_CHUNK = 256


def attend_kernel(ny, rows, arrays, groups, sides, first, last, *refs):
    refs = list(refs)
    take = lambda count: [refs.pop(0) for _ in range(count)]
    exp_ref, off_ref = take(2)
    raw = take(2) if first else None
    key_refs = take(arrays)
    value_refs = take(arrays)
    head = pl.program_id(0)
    if not first:
        take(3)
    if last:
        outs = take(len(sides))
    else:
        take(1)[0][...] = jnp.zeros((8, HD), jnp.float32)
    held, qs = take(2)
    stacked = GW * rows

    group = lax.axis_index("leaf")
    spot = lax.axis_index("ctx")
    core, chip = lax.rem(spot, 2), spot // 2
    chip_x, chip_y = lax.rem(chip, 2), chip // 2
    visible = off_ref[group]
    depth = exp_ref[1, group]

    def block_start(dx, dy, flip):
        x = lax.rem(chip_x + dx, 2)
        y = lax.rem(chip_y - dy + ny, ny)
        k = lax.rem(core + flip, 2)
        return ((y * 2 + x) * 2 + k) * rows

    if first:
        for s, q_ref in enumerate(raw):
            for g in range(GW):
                qs[head, s, g * rows : (g + 1) * rows, :] = q_ref[:, g * HD : (g + 1) * HD]

    def step(members, limits, masked, fresh):
        width = len(members) * rows
        cut = lambda refs: [refs[a][b * rows : (b + 1) * rows, :] for a, b, _ in members]
        keys = jnp.concatenate(cut(key_refs), axis=0)
        values = jnp.concatenate(cut(value_refs), axis=0)
        values = jnp.concatenate([values, jnp.ones_like(values)], axis=1)
        size = min(ROW_BLOCK, stacked)
        todo = [(s, slice(base, base + size)) for s in sides for base in range(0, stacked, size)]

        chunks = [slice(c, min(c + KEY_CHUNK, width)) for c in range(0, width, KEY_CHUNK)]
        biases = {}

        def bias_of(s):
            if s not in biases:
                column = lax.broadcasted_iota(jnp.int32, (rows, rows), 1)
                line = lax.broadcasted_iota(jnp.int32, (rows, rows), 0)
                allowed = []
                for (_, _, block), limit in zip(members, limits[s]):
                    ahead = column - line if block[0] == "own" else column
                    allowed.append(jnp.where(ahead < limit, 0.0, NEG))
                biases[s] = jnp.concatenate(allowed, axis=1)
            return biases[s]

        def score(item, chunk):
            s, here = item
            found = lax.dot_general(
                qs[head, s, here, :], keys[chunk], (((1,), (1,)), ((), ())), preferred_element_type=jnp.float32
            )
            if masked:
                found = found + jnp.concatenate([bias_of(s)[:, chunk]] * (size // rows), axis=0)
            return found

        def peak_of(scores):
            parts = [part[:, c : c + HD] for part in scores for c in range(0, part.shape[1], HD)]
            return jnp.max(functools.reduce(jnp.maximum, parts), axis=1, keepdims=True)

        scores = [score(todo[0], chunk) for chunk in chunks]
        peak = peak_of(scores)
        for at, (s, here) in enumerate(todo):
            if fresh:
                new = jnp.broadcast_to(peak, (size, HD))
            else:
                old = held[head, s, here, 2 * HD :]
                new = jnp.maximum(old, peak)
            following, weights = [], []
            for i, chunk in enumerate(chunks):
                if at + 1 < len(todo):
                    following.append(score(todo[at + 1], chunk))
                shifted = scores[i] - jnp.concatenate([new] * (scores[i].shape[1] // HD), axis=1)
                weights.append(jnp.exp2(shifted * EXP_SCALE).astype(jnp.bfloat16))
            update = jnp.dot(jnp.concatenate(weights, axis=1), values, preferred_element_type=jnp.float32)
            if following:
                scores, peak = following, peak_of(following)
            if fresh:
                held[head, s, here, : 2 * HD] = update
            else:
                shrink = jnp.exp2((old - new) * EXP_SCALE)
                before = held[head, s, here, : 2 * HD] * jnp.concatenate([shrink, shrink], axis=1)
                held[head, s, here, : 2 * HD] = before + update
            held[head, s, here, 2 * HD :] = new

    for number, members in enumerate(groups):
        limits = []
        full, some = jnp.bool_(True), jnp.bool_(False)
        for s in range(2):
            first_row = block_start(0, 0, s)
            limits.append([])
            for _, _, (kind, dx, dy, flip) in members:
                if kind == "root":
                    limit = visible - block_start(dx, dy, flip)
                    some_here = limit > 0
                elif kind == "own":
                    limit = first_row - block_start(dx, dy, flip) + 1
                    some_here = limit + rows - 1 > 0
                else:
                    limit = jnp.where(depth > 0, rows, 0)
                    some_here = limit > 0
                limits[s].append(limit)
                full = full & (limit >= rows)
                some = some | some_here
        kinds = {block[0] for _, _, block in members}
        if first and number == 0:
            step(members, limits, True, True)
            continue
        pl.when(full)(functools.partial(step, members, limits, False, False))
        if kinds != {"kin"}:
            pl.when(jnp.logical_not(full) & some)(functools.partial(step, members, limits, True, False))

    if last:
        for out_ref, s in zip(outs, sides):
            for g in range(GW):
                here = slice(g * rows, (g + 1) * rows)
                done = held[head, s, here, :HD] / held[head, s, here, HD : 2 * HD]
                out_ref[:, g * HD : (g + 1) * HD] = done.astype(jnp.bfloat16)


WHOLE = pl.BlockSpec(memory_space=pltpu.VMEM)


def in_vmem(array):
    return pltpu.with_memory_space_constraint(array, pltpu.VMEM)


def fence(state, *values):
    mark, held, prepared = state
    *values, mark = lax.optimization_barrier((*values, mark))

    def kernel(mark_ref, *refs):
        refs[2][...] = mark_ref[...]

    state[:] = pl.pallas_call(
        kernel,
        in_specs=[WHOLE] * 3,
        out_specs=[WHOLE] * 3,
        out_shape=[
            jax.ShapeDtypeStruct(mark.shape, mark.dtype),
            pltpu.VMEM(held.shape, held.dtype),
            pltpu.VMEM(prepared.shape, prepared.dtype),
        ],
        input_output_aliases={1: 1, 2: 2},
        compiler_params=pltpu.CompilerParams(vmem_limit_bytes=4 * 2**20),
    )(mark, in_vmem(held), in_vmem(prepared))
    return values


def pick(state, table, choose, arrays):
    mark, held, prepared = state
    count = len(arrays)

    def kernel(table_ref, mark_ref, *refs):
        out_ref, mark_out_ref, _, _, sem = refs[count + 2 :]
        mark_out_ref[...] = mark_ref[...]
        chosen = choose(table_ref, lax.axis_index("leaf"))
        for i, ref in enumerate(refs[:count]):

            @pl.when(chosen == i)
            def _():
                copy = pltpu.make_async_copy(ref, out_ref, sem)
                copy.start()
                copy.wait()

    anywhere = pl.BlockSpec(memory_space=pl.ANY)
    picked, *state[:] = pl.pallas_call(
        kernel,
        in_specs=[pl.BlockSpec(memory_space=pltpu.SMEM), WHOLE] + [anywhere] * count + [WHOLE] * 2,
        out_specs=[anywhere, WHOLE, WHOLE, WHOLE],
        out_shape=[
            jax.ShapeDtypeStruct(arrays[0].shape, arrays[0].dtype),
            jax.ShapeDtypeStruct(mark.shape, mark.dtype),
            pltpu.VMEM(held.shape, held.dtype),
            pltpu.VMEM(prepared.shape, prepared.dtype),
        ],
        scratch_shapes=[pltpu.SemaphoreType.DMA(())],
        input_output_aliases={count + 2: 2, count + 3: 3},
        compiler_params=pltpu.CompilerParams(vmem_limit_bytes=4 * 2**20),
    )(table, mark, *arrays, in_vmem(held), in_vmem(prepared))
    return picked


def pack(beside, *arrays):
    rows, width = arrays[0].shape
    half = width // 2

    def kernel(*refs):
        *in_refs, mine_ref, other_ref, sems = refs
        core = lax.rem(lax.axis_index("ctx"), 2)
        copies = []
        for out_ref, place in ((other_ref, 1 - core), (mine_ref, core)):
            columns = pl.ds(pl.multiple_of(place * half, half), half)
            for i, ref in enumerate(in_refs):
                target = out_ref.at[pl.ds(i // beside * rows, rows), pl.ds(i % beside * half, half)]
                copies.append(pltpu.make_async_copy(ref.at[:, columns], target, sems.at[len(copies)]))
        for copy in copies:
            copy.start()
        for copy in copies:
            copy.wait()

    anywhere = pl.BlockSpec(memory_space=pl.ANY)
    packed = jax.ShapeDtypeStruct((len(arrays) // beside * rows, beside * half), arrays[0].dtype)
    return pl.pallas_call(
        kernel,
        in_specs=[anywhere] * len(arrays),
        out_specs=[anywhere] * 2,
        out_shape=[packed] * 2,
        scratch_shapes=[pltpu.SemaphoreType.DMA((2 * len(arrays),))],
        compiler_params=pltpu.CompilerParams(vmem_limit_bytes=4 * 2**20),
    )(*(pltpu.with_memory_space_constraint(array, pltpu.HBM) for array in arrays))


def assemble(mine, got):
    rows, half = mine.shape

    def kernel(mine_ref, got_ref, out_ref, sems):
        core = lax.rem(lax.axis_index("ctx"), 2)
        copies = []
        for i, (ref, place) in enumerate(((mine_ref, core), (got_ref, 1 - core))):
            columns = pl.ds(pl.multiple_of(place * half, half), half)
            copies.append(pltpu.make_async_copy(ref, out_ref.at[:, columns], sems.at[i]))
            copies[i].start()
        for copy in copies:
            copy.wait()

    anywhere = pl.BlockSpec(memory_space=pl.ANY)
    return pl.pallas_call(
        kernel,
        in_specs=[anywhere] * 2,
        out_specs=anywhere,
        out_shape=jax.ShapeDtypeStruct((rows, 2 * half), mine.dtype),
        scratch_shapes=[pltpu.SemaphoreType.DMA((2,))],
        compiler_params=pltpu.CompilerParams(vmem_limit_bytes=4 * 2**20),
    )(mine, got)


def attend(ny, rows, tables, arrays, groups, queries, state, last, sides=(0, 1)):
    stacked = GW * rows
    first = state is None
    smem = pl.BlockSpec(memory_space=pltpu.SMEM)
    row_spec = pl.BlockSpec((rows, GW * HD), lambda h: (0, h))
    operands = [*tables]
    specs = [smem, smem]
    if first:
        operands += queries
        specs += [row_spec, row_spec]
    else:
        mark, state, prepared = state
    for shift in (0, HALF_KV):
        for array in arrays:
            operands.append(array)
            specs.append(pl.BlockSpec((array.shape[0], HD), functools.partial(lambda s, h: (0, s + h), shift)))
    aliases = {}
    if last:
        out_shape = [jax.ShapeDtypeStruct((rows, HALF_KV * GW * HD), jnp.bfloat16)] * len(sides)
        out_specs = [row_spec] * len(sides)
    else:
        out_shape = [jax.ShapeDtypeStruct((8, HD), jnp.float32)]
        out_specs = [pl.BlockSpec((8, HD), lambda h: (0, 0))]
    if not first:
        aliases = {len(operands) + 1 + i: len(out_shape) + i for i in range(2)}
        operands += [mark, in_vmem(state), in_vmem(prepared)]
        specs += [pl.BlockSpec(memory_space=pl.ANY), WHOLE, WHOLE]
    out_shape.append(pltpu.VMEM((HALF_KV, 2, stacked, 3 * HD), jnp.float32))
    out_shape.append(pltpu.VMEM((HALF_KV, 2, stacked, HD), jnp.bfloat16))
    out_specs += [WHOLE, WHOLE]
    scores = HALF_KV * len(sides) * stacked * rows * sum(len(members) for members in groups)
    out = pl.pallas_call(
        functools.partial(attend_kernel, ny, rows, len(arrays), groups, sides, first, last),
        grid=(HALF_KV,),
        in_specs=specs,
        out_specs=out_specs,
        out_shape=out_shape,
        input_output_aliases=aliases,
        compiler_params=pltpu.CompilerParams(vmem_limit_bytes=24 * 2**20),
        cost_estimate=pl.CostEstimate(flops=8 * scores * HD, bytes_accessed=4 * 2**20, transcendentals=scores),
    )(*operands)
    return list(out)


def on_device(queries, seg_keys, seg_values, root_keys, root_values, expansion, root_offsets):
    leaves, spots = lax.axis_size("leaf"), lax.axis_size("ctx")
    ny = spots // 4
    rows = queries.shape[0]
    group = lax.axis_index("leaf")
    def index(x, y, k):
        return ((y % ny) * 2 + x % 2) * 2 + k % 2

    places = [(x, y, k) for y in range(ny) for x in range(2) for k in range(2)]

    def to_core(array):
        return lax.ppermute(array, "ctx", [(index(x, y, k), index(x, y, k + 1)) for x, y, k in places])

    def to_x(array):
        return lax.ppermute(array, "ctx", [(index(x, y, k), index(x + 1, y, k)) for x, y, k in places])

    def to_y(array, step):
        return lax.ppermute(array, "ctx", [(index(x, y, k), index(x, y + step, k)) for x, y, k in places])

    mine, sent = pack(2, seg_keys, seg_values, root_keys, root_values)
    queries, sent = lax.optimization_barrier((queries, sent))
    q_mine, q_other = pack(1, queries)
    q_other, got = lax.optimization_barrier((q_other, to_core(sent)))
    own = jnp.concatenate([mine[:rows], got[:rows]], axis=0)
    root = jnp.concatenate([mine[rows:], got[rows:]], axis=0)
    run = functools.partial(attend, ny, rows, (expansion, root_offsets))
    steps = range(1, ny)

    def members(array, kind, dx=0, dy=0, flips=(0, 1), first=0):
        return tuple((array, first + i, (kind, dx, dy, flip)) for i, flip in enumerate(flips))

    def after(state, *values):
        *values, state[0] = lax.optimization_barrier((*values, state[0]))
        return values

    def hop(step, rows_held):
        pairs = [(i, (i - 1) % leaves) for i in range(leaves)]
        return lax.ppermute(rows_held, "leaf", pairs if step < leaves - 1 else pairs[1:])

    own_x, own_y = to_x(own), [to_y(own, step) for step in steps]
    own, q_got = lax.optimization_barrier((own, to_core(q_other)))
    q_pair = (q_mine, q_got)
    direct = leaves == 4
    ahead = [own]
    if direct:
        for pairs in (((1, 0), (2, 1), (3, 2)), ((0, 2), (3, 1))):
            ahead.append(lax.ppermute(own, "leaf", pairs))
    elif leaves > 1:
        ahead.append(hop(1, own))
    state = run([own, root], (members(0, "own") + members(1, "root"),), q_pair, None, False)

    (root,) = after(state, root)
    root_x, root_y = to_x(root), [to_y(root, step) for step in steps]

    def near(kind):
        groups = [members(0, kind, 1) + members(1, kind, 0, 1)]
        return groups + [members(step, kind, 0, step) for step in steps if step > 1]

    if leaves > 2 and not direct:
        (held,) = fence(state, ahead[-1])
        ahead[-1] = held
        ahead.append(hop(2, held))
    own_x, *own_y = after(state, own_x, *own_y)
    state = run([own_x, *own_y], tuple(near("own")), None, state, False)
    if direct:
        (sent_up,) = after(state, own)
        before = lax.ppermute(sent_up, "leaf", ((0, 1), (1, 2)))
        ahead = after(state, *ahead)
        relay = pick(state, expansion, lambda table, g: jnp.where(table[0, 0] == 3, 1, 0), ahead[1:])
        ahead += [before, lax.ppermute(relay, "leaf", [(1, 0)])]
    else:
        for step in range(3, leaves):
            (held,) = fence(state, ahead[-1])
            ahead[-1] = held
            ahead.append(hop(step, held))
    own_x, root_x, *root_y = after(state, own_x, root_x, *root_y)
    own_far = [to_y(own_x, step) for step in steps]
    root_far = [to_x(array) for array in root_y]
    state = run([root_x, *root_y], tuple(near("root")), None, state, False)

    def choose(table, g):
        offset = table[0, g] - g
        if not direct:
            return lax.rem(offset + leaves, leaves)
        far_one = jnp.where(g == 0, 4, 2)
        return jnp.where(offset == 0, 0, jnp.where(offset == 1, 1, jnp.where(offset == -1, 3, far_one)))

    parent_rows = pick(state, expansion, choose, after(state, *ahead))
    (parent_rows,) = after(state, parent_rows)
    kin_x, kin_y = to_x(parent_rows), [to_y(parent_rows, step) for step in steps]
    groups = [members(i, "own", 1, i + 1) + members(ny - 1 + i, "root", 1, i + 1) for i in range(ny - 1)]
    groups[0] += members(2 * ny - 2, "kin")
    state = run([*own_far, *root_far, parent_rows], tuple(groups), None, state, False)

    (kin_x,) = after(state, kin_x)
    tops = [to_y(kin_x[:rows], step) for step in steps]
    lows = [to_x(array[rows:]) for array in kin_y]
    groups = [members(0, "kin") + members(1, "kin")] + [members(step, "kin") for step in steps if step > 1]
    state = run([kin_x, *kin_y], tuple(groups), None, state, False)
    groups = [members(i, "kin", flips=(0,)) + members(len(tops) + i, "kin", flips=(1,)) for i in range(len(tops))]
    out_other, *kept = run([*tops, *lows], tuple(groups), None, state, True, (1,))
    out_got = to_core(out_other)
    out_mine, *_ = run([*tops, *lows], tuple(groups), None, [state[0], *kept], True, (0,))
    return assemble(out_mine, out_got)


def solution(mesh):
    return jax.shard_map(
        on_device,
        mesh=mesh,
        in_specs=(
            P(("leaf", "ctx"), None),
            P(("leaf", "ctx"), None),
            P(("leaf", "ctx"), None),
            P("ctx", None),
            P("ctx", None),
            P(),
            P(),
        ),
        out_specs=P(("leaf", "ctx"), None),
        check_vma=False,
    )
```
